32 devices in a mesh: struct: 2 (over y), sample: 16 (over z, x, core).
Axes of the slice: x: 2, y: 2, z: 4, core: 2. Of those that a mesh axis runs over, the one named last changes fastest.
Arguments:
- acts: bfloat16 [2, 32, 768, 768], P('struct', 'sample'), may hold values from -6 to 6
- cond: bfloat16 [2, 768, 384], P('struct'), may hold values from -6 to 6
- pair: bfloat16 [2, 768, 768, 128], P('struct', 'sample'), may hold values from -6 to 6
- lengths: int32 [2], P('struct'), may hold values from 384 to 768, as said below
- token_mask: int32 [2, 768], P('struct'), may hold values 0 or 1
- cond_gains: bfloat16 [768], replicated, may hold values from 0.099609375 to 1.8984375
- cond_w: bfloat16 [384, 3072], replicated, may hold values from -0.3125 to 0.3125
- cond_bias: bfloat16 [1536], replicated, may hold values from -4 to 4
- output_gate_weights: bfloat16 [384, 1536], replicated, may hold values from -0.3125 to 0.3125
- zero_bias: bfloat16 [1536], replicated, may hold values from -4 to 4
- qkvg_w: bfloat16 [768, 3072], replicated, may hold values from -0.21875 to 0.21875
- q_bias: bfloat16 [768], replicated, may hold values from -3 to 3
- out_w: bfloat16 [768, 768], replicated, may hold values from -3 to 3
- swiglu_w: bfloat16 [768, 3072], replicated, may hold values from -0.21875 to 0.21875
- down_w: bfloat16 [1536, 768], replicated, may hold values from -0.4375 to 0.4375
- pair_gain: bfloat16 [128], replicated, may hold values from 0.099609375 to 1.8984375
- pair_w: bfloat16 [128, 16], replicated, may hold values from -0.5 to 0.5
- cotangent: bfloat16 [2, 32, 768, 768], P('struct', 'sample'), may hold values from -6 to 6
Outputs:
- block_out: bfloat16 [2, 32, 768, 768], P('struct', 'sample')
- acts_grad: bfloat16 [2, 32, 768, 768], P('struct', 'sample')
- cond_grad: float32 [2, 768, 384], P('struct', 'sample')
- pair_grad: float32 [2, 768, 768, 128], P('struct', 'sample')
- cond_gains_grad: float32 [768], P('sample')
- cond_w_grad: float32 [384, 3072], P('sample')
- cond_bias_grad: float32 [1536], P('sample')
- zero_w_grad: float32 [384, 1536], P('sample')
- zero_bias_grad: float32 [1536], P('sample')
- qkvg_w_grad: float32 [768, 3072], P('sample')
- q_bias_grad: float32 [768], P('sample')
- out_w_grad: float32 [768, 768], P('sample')
- swiglu_w_grad: float32 [768, 3072], P('sample')
- down_w_grad: float32 [1536, 768], P('sample')
- pair_gain_grad: float32 [128], P('sample')
- pair_w_grad: float32 [128, 16], P('sample')
The draws below stay inside these ranges and needn't reach their ends.
Inputs may be any that keep to these rules, and one draw needn't show every extreme that they name: `lengths`: each structure has 384 to 768 tokens; in every draw some structure has 768.
All inputs are finite; a program needn't handle non-finite values. No bound on the sum of `token_mask` on one device may be relied on, other than what follows from the above.
Results may differ from the reference program's by a relative error of at most 0.013.
The reference program's roundings to bfloat16 on the way count: a program that leaves them out, or rounds other values in their place, can miss the bound.
Values may be sent and summed in bfloat16 or wider, within the bound.
No kernel may reach another device: no remote copies, remote signals or barrier semaphores. Data moves between devices by JAX's collectives and lax.ppermute only.
A program may use at most 384 MiB of HBM per device.

```python
import jax
import jax.numpy as jnp
from jax import lax

D = 768
H = 16
HD = 48
P_SIZE = 128
C = 384
F = 1536
LMAX = 768
STRUCTS = 2
SAMPLES = 32


def draw_lengths(key, part):
    key = jax.random.fold_in(key, 7)
    pick_key, force_key = jax.random.split(key)
    spread_lengths = jax.random.randint(pick_key, (STRUCTS,), LMAX // 2, LMAX + 1)
    longest = jax.random.randint(force_key, (), 0, STRUCTS)
    struct_index = jnp.arange(STRUCTS, dtype=jnp.int32)
    return jnp.where(struct_index == longest, LMAX, spread_lengths).astype(jnp.int32)


def place_ends(drawn, own_key, least, high):
    longest = drawn.shape.index(max(drawn.shape))
    spots = []
    for shift in (0, 1):
        where = [jax.random.randint(jax.random.fold_in(own_key, axis), (), 0, length) for axis, length in enumerate(drawn.shape)]
        where[longest] = (where[longest] + shift) % drawn.shape[longest]
        spots.append(tuple(where))
    return drawn.at[spots[0]].set(least).at[spots[1]].set(high)


def shard_levels(rng, shape, pieces, low, top_value):
    loudness = 1.0
    for dim, shards_of in pieces:
        heights = jax.random.uniform(jax.random.fold_in(jax.random.fold_in(rng, 6), dim), (shards_of,), jnp.float32, low / len(pieces), top_value / len(pieces))
        loudness = loudness * jnp.repeat(jnp.exp(heights), shape[dim] // shards_of).reshape((-1,) + (1,) * (len(shape) - 1 - dim))
    return loudness


def gaussian(key, extent, scale, reach, cuts=(), kind=jnp.bfloat16):
    entries = jax.random.normal(key, extent, jnp.float32) * scale
    if len(cuts) > 0:
        entries = shard_levels(key, extent, cuts, -0.22, 0.18) * entries
    return jnp.clip(entries, min=-reach, max=reach).astype(kind)


def setup_inputs(seed: int = 0) -> dict:
    streams_of = jax.random.split(jax.random.key(seed), 19)
    acts = gaussian(streams_of[0], (STRUCTS, SAMPLES, LMAX, D), 1.0, 6.0, ((0, 2), (1, 16)))
    cond = gaussian(streams_of[1], (STRUCTS, LMAX, C), 1.0, 6.0, ((0, 2),))
    pair = gaussian(streams_of[2], (STRUCTS, LMAX, LMAX, P_SIZE), 1.0, 6.0, ((0, 2), (1, 16)))
    lengths = draw_lengths(jax.random.fold_in(streams_of[18], 71), 0)
    token_mask = place_ends((jax.random.randint(streams_of[4], (STRUCTS, LMAX), 0, 8) < 7).astype(jnp.int32), jax.random.fold_in(streams_of[4], 1), 0, 1)
    cond_gains = jnp.clip(1.0 + 0.18 * jax.random.normal(streams_of[5], (2 * C,), jnp.float32), 0.099609375, 1.8984375).astype(jnp.bfloat16)
    cond_w = gaussian(streams_of[6], (C, 4 * D), C ** -0.5, 0.3125)
    cond_bias = gaussian(streams_of[7], (2 * D,), 1.0, 4.0)
    output_gate_weights = gaussian(streams_of[8], (C, 2 * D), C ** -0.5, 0.3125)
    zero_bias = gaussian(streams_of[9], (2 * D,), 1.0, 4.0)
    qkvg_w = gaussian(streams_of[10], (D, 4 * D), D ** -0.5, 0.21875)
    q_bias = gaussian(streams_of[11], (D,), 0.5, 3.0)
    out_w = gaussian(streams_of[12], (D, D), 4 ** -0.5, 3.0)
    swiglu_w = gaussian(streams_of[13], (D, 2 * F), D ** -0.5, 0.21875)
    down_w = gaussian(streams_of[14], (F, D), (F // 8) ** -0.5, 0.4375)
    pair_gain = jnp.clip(1.0 + 0.18 * jax.random.normal(streams_of[15], (P_SIZE,), jnp.float32), 0.099609375, 1.8984375).astype(jnp.bfloat16)
    pair_w = gaussian(streams_of[16], (P_SIZE, H), P_SIZE ** -0.5, 0.5)
    cotangent = gaussian(streams_of[17], (STRUCTS, SAMPLES, LMAX, D), 1.0, 6.0, ((0, 2), (1, 16)))
    return dict(acts=acts, cond=cond, pair=pair, lengths=lengths, token_mask=token_mask, cond_gains=cond_gains, cond_w=cond_w, cond_bias=cond_bias, output_gate_weights=output_gate_weights, zero_bias=zero_bias, qkvg_w=qkvg_w, q_bias=q_bias, out_w=out_w, swiglu_w=swiglu_w, down_w=down_w, pair_gain=pair_gain, pair_w=pair_w, cotangent=cotangent)


@jax.custom_vjp
def low(v):
    return lax.optimization_barrier(v.astype(jnp.bfloat16)).astype(jnp.float32)

@jax.custom_vjp
def low_back(v):
    return v

def low_keep(v):
    return (low(v), None)

def low_pass(kept, grad):
    return (grad,)

def back_keep(v):
    return (v, None)

def back_low(kept, grad):
    return (low(grad),)
low.defvjp(low_keep, low_pass)
low_back.defvjp(back_keep, back_low)
EPS = 1e-05
HIGHEST = lax.Precision.HIGHEST
MASKED = -1000000000.0

def matmul(left_side, right_side):
    return jnp.dot(left_side, right_side, precision=HIGHEST, preferred_element_type=jnp.float32)

def layer_norm(values):
    center = values - lax.optimization_barrier(jnp.mean(values, axis=-1, keepdims=True))
    return center * lax.rsqrt(lax.optimization_barrier(jnp.mean(center * center, axis=-1, keepdims=True)) + EPS)

def pair_bias(pair_one, pair_gain, pair_w):
    normed = low(layer_norm(pair_one) * pair_gain)
    pair_term = jnp.einsum('ijc,ch->ihj', normed, pair_w, precision=HIGHEST)
    return low_back(low(pair_term))

def one_sample(acts_one, single_conditioning, pair_term, key_valid, params):
    cond_gains, cond_w, cond_bias, output_gate_weights, zero_bias, qkvg_w, q_bias, out_w, swiglu_w, down_w = params
    acts_normed = layer_norm(acts_one)
    zero_gates = jax.nn.sigmoid(low_back(matmul(single_conditioning, output_gate_weights)) + zero_bias)
    cond_normed = layer_norm(single_conditioning)

    def adaptive(branch):
        scaled_rows = low(cond_normed * cond_gains[branch * C:(branch + 1) * C])
        projected = low_back(matmul(scaled_rows, cond_w[:, 2 * branch * D:2 * (branch + 1) * D]))
        factor = jax.nn.sigmoid(projected[:, :D] + cond_bias[branch * D:(branch + 1) * D])
        return low(factor * acts_normed + projected[:, D:])
    joined = low_back(matmul(adaptive(0), qkvg_w))
    queries = low(joined[:, :D] + q_bias).reshape(LMAX, H, HD)
    key_rows = low(joined[:, D:2 * D]).reshape(LMAX, H, HD)
    value_rows = low(joined[:, 2 * D:3 * D]).reshape(LMAX, H, HD)
    gate_heads = jax.nn.sigmoid(joined[:, 3 * D:])
    raw_scores = low_back(jnp.einsum('qhd,khd->qhk', queries, key_rows, precision=HIGHEST))
    scores = jnp.where(key_valid[None, None, :], raw_scores * HD ** (-0.5) + pair_term, MASKED)
    probs_low = low(jax.nn.softmax(scores, axis=-1))
    mixed_heads = low_back(jnp.einsum('qhk,khd->qhd', probs_low, value_rows, precision=HIGHEST)).reshape(LMAX, D)
    attended = low_back(matmul(low(gate_heads * mixed_heads), out_w))
    hidden = low_back(matmul(adaptive(1), swiglu_w))
    product = low(jax.nn.silu(hidden[:, :F]) * hidden[:, F:])
    transition = low_back(matmul(product, down_w))
    return acts_one + zero_gates[:, :D] * attended + zero_gates[:, D:] * transition

def widen(tensor):
    return tensor.astype(jnp.float32)

def reference(acts, cond, pair, lengths, token_mask, cond_gains, cond_w, cond_bias, output_gate_weights, zero_bias, qkvg_w, q_bias, out_w, swiglu_w, down_w, pair_gain, pair_w, cotangent):
    position = jnp.arange(LMAX, dtype=jnp.int32)
    key_valid = (position[None, :] < lengths[:, None]) & ((token_mask == 1) | (position[None, :] == 0))
    params = tuple((widen(tensor) for tensor in (cond_gains, cond_w, cond_bias, output_gate_weights, zero_bias, qkvg_w, q_bias, out_w, swiglu_w, down_w)))
    pair_params = (widen(pair_gain), widen(pair_w))
    sample_step = jax.checkpoint(one_sample)

    def forward(acts_all, cond_all, pair_all, weights, pair_weights):

        def per_struct(item):
            acts_struct, cond_struct, pair_struct, valid_struct = item
            pair_term = pair_bias(pair_struct, pair_weights[0], pair_weights[1])

            def per_sample(acts_one):
                return sample_step(acts_one, cond_struct, pair_term, valid_struct, weights)
            return lax.map(per_sample, acts_struct)
        return lax.map(per_struct, (acts_all, cond_all, pair_all, key_valid))
    output, pullback = jax.vjp(forward, widen(acts), widen(cond), widen(pair), params, pair_params)
    grad_acts, conditioning_gradient, grad_pair, grad_params, grad_pair_params = pullback(widen(cotangent))
    return (output.astype(jnp.bfloat16), grad_acts.astype(jnp.bfloat16), conditioning_gradient, grad_pair, grad_params[0], grad_params[1], grad_params[2], grad_params[3], grad_params[4], grad_params[5], grad_params[6], grad_params[7], grad_params[8], grad_params[9], grad_pair_params[0], grad_pair_params[1])
```

```python
import functools

import jax
import jax.numpy as jnp
from jax import lax
from jax.experimental import pallas as pl
from jax.experimental.pallas import tpu as pltpu
from jax.sharding import PartitionSpec as P

EPS = 1e-05
MASKED = -1000000000.0
F32 = jnp.float32
BF16 = jnp.bfloat16
CHUNK_HEADS = 4
WINDOW = 256
LANES = 128
TOKENS = 128
PAIR_ROWS = 8
VMEM_LIMIT = 60 * 2**20


def dot(left, right, left_dim=1, right_dim=0):
    return lax.dot_general(
        left, right, (((left_dim,), (right_dim,)), ((), ())), preferred_element_type=F32
    )


def layer_norm(values):
    center = values - jnp.mean(values, axis=-1, keepdims=True)
    inverse = lax.rsqrt(jnp.mean(center * center, axis=-1, keepdims=True) + EPS)
    return (center * inverse, inverse)


def norm_back(grad_in, normed, inverse):
    mean_grad = jnp.mean(grad_in, axis=-1, keepdims=True)
    mean_proj = jnp.mean(grad_in * normed, axis=-1, keepdims=True)
    return inverse * (grad_in - mean_grad - normed * mean_proj)


def slope(gate):
    return gate * (1.0 - gate)


def column_sum(values):
    return jnp.sum(values.reshape(-1, values.shape[-1]), axis=0, keepdims=True)


def params(flops_limit=VMEM_LIMIT):
    return pltpu.CompilerParams(
        vmem_limit_bytes=flops_limit, dimension_semantics=("arbitrary",)
    )


def cost(flops, nbytes, exps=0):
    return pl.CostEstimate(flops=int(flops), bytes_accessed=int(nbytes), transcendentals=int(exps))


def whole(array):
    rank = len(array.shape)
    return pl.BlockSpec(array.shape, lambda t: (0,) * rank, pipeline_mode=pl.Buffered(1))


def fixed_out(shape):
    rank = len(shape)
    return pl.BlockSpec(shape, lambda t: (0,) * rank, pipeline_mode=pl.Buffered(1))


def rows_of(block, axis, rank, squeeze=None):
    return pl.BlockSpec(block, lambda t: tuple(t if a == axis else 0 for a in range(rank)))


def pair_forward_kernel(pair_ref, gain_ref, weight_ref, valid_ref, out_ref):
    gain = gain_ref[...].astype(F32)
    valid = valid_ref[...] > 0

    def row(i, carry):
        normed, _ = layer_norm(pair_ref[i].astype(F32))
        affine = (normed * gain).astype(BF16)
        term = dot(weight_ref[...], affine, 1, 1)
        out_ref[i] = jnp.where(valid, term, MASKED).astype(BF16)
        return carry

    lax.fori_loop(0, pair_ref.shape[0], row, 0, unroll=2)


def pair_forward(pair, gain, weight_t, valid):
    rows, length, channels = pair.shape
    heads = weight_t.shape[0]
    return pl.pallas_call(
        pair_forward_kernel,
        grid=(rows // PAIR_ROWS,),
        in_specs=[
            rows_of((PAIR_ROWS, length, channels), 0, 3),
            whole(gain),
            whole(weight_t),
            whole(valid),
        ],
        out_specs=rows_of((PAIR_ROWS, heads, length), 0, 3),
        out_shape=jax.ShapeDtypeStruct((rows, heads, length), BF16),
        compiler_params=params(),
        cost_estimate=cost(2 * pair.size * heads, pair.size * 2.3),
        name="pair_forward",
    )(pair, gain, weight_t, valid)


def pair_backward_kernel(pair_ref, grad_ref, gain_ref, weight_ref, out_ref, weight_grad_ref, gain_grad_ref):
    gain = gain_ref[...].astype(F32)

    @pl.when(pl.program_id(0) == 0)
    def _():
        weight_grad_ref[...] = jnp.zeros_like(weight_grad_ref)
        gain_grad_ref[...] = jnp.zeros_like(gain_grad_ref)

    def row(i, carry):
        normed, inverse = layer_norm(pair_ref[i].astype(F32))
        affine = (normed * gain).astype(BF16)
        grad = grad_ref[i]
        weight_grad_ref[...] += dot(grad, affine)
        grad_affine = dot(grad, weight_ref[...], 0, 0)
        gain_grad_ref[...] += column_sum(grad_affine * normed)
        out_ref[i] = norm_back(grad_affine * gain, normed, inverse)
        return carry

    lax.fori_loop(0, pair_ref.shape[0], row, 0, unroll=2)


def pair_backward(pair, grad, gain, weight_t):
    rows, length, channels = pair.shape
    heads = weight_t.shape[0]
    return pl.pallas_call(
        pair_backward_kernel,
        grid=(rows // PAIR_ROWS,),
        in_specs=[
            rows_of((PAIR_ROWS, length, channels), 0, 3),
            rows_of((PAIR_ROWS, heads, length), 0, 3),
            whole(gain),
            whole(weight_t),
        ],
        out_specs=[
            rows_of((PAIR_ROWS, length, channels), 0, 3),
            fixed_out((heads, channels)),
            fixed_out((1, channels)),
        ],
        out_shape=[
            jax.ShapeDtypeStruct((rows, length, channels), F32),
            jax.ShapeDtypeStruct((heads, channels), F32),
            jax.ShapeDtypeStruct((1, channels), F32),
        ],
        compiler_params=params(),
        cost_estimate=cost(4 * pair.size * heads, pair.size * 6.3),
        name="pair_backward",
    )(pair, grad, gain, weight_t)


def conditioned(cond_normed, gain, weight, bias):
    width = bias.shape[-1]
    scaled = (cond_normed * gain.astype(F32)).astype(BF16)
    projected = dot(scaled, weight)
    factor = jax.nn.sigmoid(projected[:, :width] + bias.astype(F32))
    return scaled, factor, projected[:, width:]


def window_start(chunk, head_dim):
    return chunk * CHUNK_HEADS * head_dim // LANES * LANES


def inputs_kernel(
    head_dim, acts_ref, cot_ref, cond_ref, gain_ref, cond_w_ref, cond_b_ref, zero_w_ref, zero_b_ref,
    qkvg_ref, q_bias_ref, out_wt_ref,
    input_ref, gate_ref, gated_grad_ref, q_ref, k_ref, v_ref, g_ref, qt_ref, kt_ref, vt_ref, gt_ref,
):
    samples, tokens, width = acts_ref.shape
    cond = cond_ref[...]
    cond_normed, _ = layer_norm(cond.astype(F32))
    zero_gate = jax.nn.sigmoid(dot(cond, zero_w_ref[...]) + zero_b_ref[...].astype(F32))
    _, factor, shift = conditioned(cond_normed, gain_ref[...], cond_w_ref[...], cond_b_ref[...])
    normed, _ = layer_norm(acts_ref[...].astype(F32))
    first = (factor[None] * normed + shift[None]).astype(BF16)
    input_ref[...] = first
    first = first.reshape(samples * tokens, width)
    grad_att = (cot_ref[...].astype(F32) * zero_gate[None]).astype(BF16)
    grad_gated = dot(grad_att.reshape(samples * tokens, width), out_wt_ref[...])
    gated_grad_ref[...] = grad_gated.reshape(samples, tokens, width)
    gate = jax.nn.sigmoid(dot(first, qkvg_ref[:, 3 * width :]))
    gate_ref[...] = gate.reshape(samples, tokens, width)

    def put(values, nat_ref, t_ref):
        low = values.astype(BF16).reshape(samples, tokens, width)
        for chunk in range(nat_ref.shape[0]):
            start = window_start(chunk, head_dim)
            nat_ref[chunk] = low[:, :, start : start + WINDOW]
        for s in range(samples):
            t_ref[s] = low[s].T

    put(grad_gated * gate, g_ref, gt_ref)
    put(dot(first, qkvg_ref[:, :width]) + q_bias_ref[...].astype(F32), q_ref, qt_ref)
    put(dot(first, qkvg_ref[:, width : 2 * width]), k_ref, kt_ref)
    put(dot(first, qkvg_ref[:, 2 * width : 3 * width]), v_ref, vt_ref)


def inputs_call(acts, cot, cond, gain, cond_w, cond_b, zero_w, zero_b, qkvg_w, q_bias, out_wt, heads):
    samples, length, width = acts.shape
    chunks = heads // CHUNK_HEADS
    block = rows_of((samples, TOKENS, width), 1, 3)
    nat = rows_of((chunks, samples, TOKENS, WINDOW), 2, 4)
    turned = rows_of((samples, width, TOKENS), 2, 3)
    rows = samples * length
    fixed = (gain, cond_w, cond_b, zero_w, zero_b, qkvg_w, q_bias, out_wt)
    return pl.pallas_call(
        functools.partial(inputs_kernel, width // heads),
        grid=(length // TOKENS,),
        in_specs=[block, block, rows_of((TOKENS, cond.shape[1]), 0, 2)] + [whole(a) for a in fixed],
        out_specs=[block] * 3 + [nat] * 4 + [turned] * 4,
        out_shape=[
            jax.ShapeDtypeStruct(acts.shape, BF16),
            jax.ShapeDtypeStruct(acts.shape, F32),
            jax.ShapeDtypeStruct(acts.shape, F32),
        ]
        + [jax.ShapeDtypeStruct((chunks, samples, length, WINDOW), BF16)] * 4
        + [jax.ShapeDtypeStruct((samples, width, length), BF16)] * 4,
        compiler_params=params(),
        cost_estimate=cost(2 * rows * width * width * 6, rows * width * 40),
        name="inputs",
    )(acts, cot, cond, *fixed)


def add_to(step, ref, value):
    @pl.when(step == 0)
    def _():
        ref[...] = value

    @pl.when(step > 0)
    def _():
        ref[...] += value


def zero_back(grad_zero, cond, zero_w_ref):
    total = jnp.sum(grad_zero, axis=0)
    low = total.astype(BF16)
    return dot(cond, low, 0, 0), column_sum(total), dot(low, zero_w_ref[...], 1, 1)


def adaptive_back(grad_input, normed, factor, scaled, gain, cond_normed, cond_w_ref):
    grad_factor = jnp.sum(grad_input * normed * slope(factor)[None], axis=0)
    projected = jnp.concatenate([grad_factor, jnp.sum(grad_input, axis=0)], axis=-1).astype(BF16)
    weight_grad = dot(scaled, projected, 0, 0)
    grad_scaled = dot(projected, cond_w_ref[...], 1, 1)
    return (
        weight_grad,
        column_sum(grad_factor),
        column_sum(grad_scaled * cond_normed),
        grad_scaled * gain.astype(F32),
        grad_input * factor[None],
    )


def transition_kernel(
    acts_ref, cot_ref, cond_ref, gain_ref, cond_w_ref, cond_b_ref, zero_w_ref, zero_b_ref,
    swiglu_ref, down_ref,
    partial_ref, acts_grad_ref, cond_gate_ref, cond_norm_ref,
    swiglu_out, down_out, cond_w_out, zero_w_out, cond_b_out, zero_b_out, gain_out,
    swiglu_acc, down_acc, cond_w_acc, zero_w_acc,
):
    step = pl.program_id(0)
    samples, tokens, width = acts_ref.shape
    rows = samples * tokens
    hidden_width = down_ref.shape[0]
    cond = cond_ref[...]
    cond_normed, _ = layer_norm(cond.astype(F32))
    zero_gate = jax.nn.sigmoid(dot(cond, zero_w_ref[...]) + zero_b_ref[...].astype(F32))
    scaled, factor, shift = conditioned(cond_normed, gain_ref[...], cond_w_ref[...], cond_b_ref[...])
    acts = acts_ref[...].astype(F32)
    normed, _ = layer_norm(acts)
    second = (factor[None] * normed + shift[None]).astype(BF16).reshape(rows, width)
    grad_out = cot_ref[...].astype(F32)
    grad_tr = (grad_out * zero_gate[None]).astype(BF16).reshape(rows, width)
    hidden = dot(second, swiglu_ref[...])
    gate_part = hidden[:, :hidden_width]
    up_part = hidden[:, hidden_width:]
    gate_sig = jax.nn.sigmoid(gate_part)
    silu = gate_part * gate_sig
    product = (silu * up_part).astype(BF16)
    transition = dot(product, down_ref[...]).reshape(samples, tokens, width)
    partial_ref[...] = acts + zero_gate[None] * transition
    grad_product = dot(grad_tr, down_ref[...], 1, 1)
    add_to(step, down_acc, dot(product, grad_tr, 0, 0))
    grad_up = grad_product * silu
    grad_gate = grad_product * up_part * gate_sig * (1.0 + gate_part * (1.0 - gate_sig))
    grad_hidden = jnp.concatenate([grad_gate, grad_up], axis=-1).astype(BF16)
    add_to(step, swiglu_acc, dot(second, grad_hidden, 0, 0))
    grad_input = dot(grad_hidden, swiglu_ref[...], 1, 1).reshape(samples, tokens, width)
    zero_grad, zero_sum, cond_gate = zero_back(
        grad_out * transition * slope(zero_gate)[None], cond, zero_w_ref
    )
    cond_gate_ref[...] = cond_gate
    add_to(step, zero_w_acc, zero_grad)
    add_to(step, zero_b_out, zero_sum)
    weight_grad, bias_sum, gain_sum, cond_norm, acts_grad = adaptive_back(
        grad_input, normed, factor, scaled, gain_ref[...], cond_normed, cond_w_ref
    )
    add_to(step, cond_w_acc, weight_grad)
    add_to(step, cond_b_out, bias_sum)
    add_to(step, gain_out, gain_sum)
    cond_norm_ref[...] = cond_norm
    acts_grad_ref[...] = acts_grad

    @pl.when(step == pl.num_programs(0) - 1)
    def _():
        swiglu_out[...] = swiglu_acc[...].astype(BF16)
        down_out[...] = down_acc[...].astype(BF16)
        cond_w_out[...] = cond_w_acc[...].astype(BF16)
        zero_w_out[...] = zero_w_acc[...].astype(BF16)


def transition_call(acts, cot, cond, gain, cond_w, cond_b, zero_w, zero_b, swiglu, down):
    samples, length, width = acts.shape
    cond_width = cond.shape[1]
    hidden = down.shape[0]
    rows = samples * length
    block = rows_of((samples, TOKENS, width), 1, 3)
    cond_block = rows_of((TOKENS, cond_width), 0, 2)
    fixed = (gain, cond_w, cond_b, zero_w, zero_b, swiglu, down)
    weights = [(width, 2 * hidden), (hidden, width), (cond_width, 2 * width), (cond_width, width)]
    vectors = [(1, width), (1, width), (1, cond_width)]
    return pl.pallas_call(
        transition_kernel,
        grid=(length // TOKENS,),
        in_specs=[block, block, cond_block] + [whole(a) for a in fixed],
        out_specs=[block, block, cond_block, cond_block] + [fixed_out(s) for s in weights + vectors],
        out_shape=[jax.ShapeDtypeStruct(acts.shape, F32)] * 2
        + [jax.ShapeDtypeStruct(cond.shape, F32)] * 2
        + [jax.ShapeDtypeStruct(s, BF16) for s in weights]
        + [jax.ShapeDtypeStruct(s, F32) for s in vectors],
        scratch_shapes=[pltpu.VMEM(s, F32) for s in weights],
        compiler_params=params(),
        cost_estimate=cost(2 * rows * width * hidden * 9, rows * width * 40),
        name="transition",
    )(acts, cot, cond, *fixed)


def attention_kernel(
    head_dim, first_lane, q_ref, k_ref, v_ref, g_ref, qt_ref, kt_ref, vt_ref, gt_ref, bias_ref,
    mixed_ref, dq_ref, dkt_ref, dvt_ref, db_ref, kz, vz, plow, dslow, dsum,
):
    h = pl.program_id(0)
    samples, length, wide = q_ref.shape
    scale = head_dim ** (-0.5)
    off = pl.multiple_of(first_lane + h * head_dim, 16)
    lane = lax.broadcasted_iota(jnp.int32, (1, wide), 1)
    mask = ((lane >= off) & (lane < off + head_dim)).astype(BF16)

    @pl.when(h == 0)
    def _():
        mixed_ref[...] = jnp.zeros_like(mixed_ref)
        dq_ref[...] = jnp.zeros_like(dq_ref)

    kz[...] = jnp.zeros_like(kz)
    vz[...] = jnp.zeros_like(vz)
    for s in range(samples):
        kz[s, pl.ds(off, head_dim), :] = kt_ref[s]
        vz[s, pl.ds(off, head_dim), :] = vt_ref[s]
    bias = bias_ref[:, 0].reshape(length, length).astype(F32)
    for s in range(samples):
        x = dot(q_ref[s], kz[s]) * scale + bias
        x = jnp.exp(x - jnp.max(x, axis=-1, keepdims=True))
        probs = x * (1.0 / jnp.sum(x, axis=-1, keepdims=True))
        low = probs.astype(BF16)
        plow[...] = low
        mixed = dot(low, v_ref[s] * mask)
        mixed_ref[s] += mixed
        grad = g_ref[s]
        delta = jnp.sum(grad.astype(F32) * mixed, axis=-1, keepdims=True)
        grad_scores = probs * (dot(grad, vz[s]) - delta)
        grad_low = (grad_scores * scale).astype(BF16)
        dslow[...] = grad_low
        total = grad_scores if s == 0 else dsum[...] + grad_scores
        if s < samples - 1:
            dsum[...] = total
        else:
            db_ref[:, 0] = total.astype(BF16).reshape(db_ref.shape[0], db_ref.shape[2], length)
        dq_ref[s] += dot(grad_low, k_ref[s] * mask)
        dvt_ref[s] = dot(gt_ref[s], plow[...]).astype(BF16)
        dkt_ref[s] = dot(qt_ref[s], dslow[...]).astype(BF16)


def attention_call(chunk, nats, turned, bias, head_dim):
    _, samples, length, wide = nats[0].shape
    parts, _, part_rows, _ = bias.shape
    nat = pl.BlockSpec((None, samples, length, wide), lambda h: (chunk, 0, 0, 0))
    turn = pl.BlockSpec((samples, head_dim, length), lambda h: (0, chunk * CHUNK_HEADS + h, 0))
    turn_out = pl.BlockSpec((samples, head_dim, length), lambda h: (0, h, 0))
    bias_in = pl.BlockSpec((parts, 1, part_rows, length), lambda h: (0, chunk * CHUNK_HEADS + h, 0, 0))
    bias_out = pl.BlockSpec((parts, 1, part_rows, length), lambda h: (0, h, 0, 0))
    held = pl.BlockSpec((samples, length, wide), lambda h: (0, 0, 0))
    pairs = samples * CHUNK_HEADS
    return pl.pallas_call(
        functools.partial(
            attention_kernel, head_dim, chunk * CHUNK_HEADS * head_dim - window_start(chunk, head_dim)
        ),
        grid=(CHUNK_HEADS,),
        in_specs=[nat] * 4 + [turn] * 4 + [bias_in],
        out_specs=[held, held, turn_out, turn_out, bias_out],
        out_shape=[
            jax.ShapeDtypeStruct((samples, length, wide), F32),
            jax.ShapeDtypeStruct((samples, length, wide), F32),
            jax.ShapeDtypeStruct((samples, CHUNK_HEADS * head_dim, length), BF16),
            jax.ShapeDtypeStruct((samples, CHUNK_HEADS * head_dim, length), BF16),
            jax.ShapeDtypeStruct((parts, CHUNK_HEADS, part_rows, length), BF16),
        ],
        scratch_shapes=[
            pltpu.VMEM((samples, wide, length), BF16),
            pltpu.VMEM((samples, wide, length), BF16),
            pltpu.VMEM((length, length), BF16),
            pltpu.VMEM((length, length), BF16),
            pltpu.VMEM((length, length), F32),
        ],
        compiler_params=params(),
        cost_estimate=cost(
            12 * pairs * length * length * wide, 8 * CHUNK_HEADS * length * length, pairs * length * length
        ),
        name="attention",
    )(*nats, *turned, bias)


def outputs_kernel(
    head_dim, chunks, *refs
):
    (acts_ref, cot_ref, cond_ref, input_ref, gate_ref, gated_grad_ref, partial_ref, acts_part_ref,
     cond_gate_in, cond_norm_in), refs = refs[:10], refs[10:]
    mixed_refs, refs = refs[:chunks], refs[chunks:]
    dq_refs, refs = refs[:chunks], refs[chunks:]
    dkt_refs, refs = refs[:chunks], refs[chunks:]
    dvt_refs, refs = refs[:chunks], refs[chunks:]
    (gain_ref, cond_w_ref, cond_b_ref, zero_w_ref, zero_b_ref, qkvg_t_ref, out_w_ref), refs = refs[:7], refs[7:]
    (block_ref, acts_grad_ref, cond_grad_ref, qkvg_out, out_out, cond_w_out, zero_w_out,
     cond_b_out, zero_b_out, gain_out, q_bias_out), refs = refs[:11], refs[11:]
    qkvg_acc, out_acc, cond_w_acc, zero_w_acc = refs
    step = pl.program_id(0)
    samples, tokens, width = acts_ref.shape
    rows = samples * tokens
    cond = cond_ref[...]
    cond_normed, cond_inverse = layer_norm(cond.astype(F32))
    zero_gate = jax.nn.sigmoid(dot(cond, zero_w_ref[...]) + zero_b_ref[...].astype(F32))
    scaled, factor, _ = conditioned(cond_normed, gain_ref[...], cond_w_ref[...], cond_b_ref[...])
    normed, inverse = layer_norm(acts_ref[...].astype(F32))
    first = input_ref[...].reshape(rows, width)
    grad_out = cot_ref[...].astype(F32)
    grad_att = (grad_out * zero_gate[None]).astype(BF16).reshape(rows, width)

    def join(window_refs):
        pieces = []
        for tile in range(width // LANES):
            held = [
                ref[:, :, tile * LANES - start : (tile + 1) * LANES - start]
                for chunk, ref in enumerate(window_refs)
                for start in [window_start(chunk, head_dim)]
                if start <= tile * LANES < start + WINDOW
            ]
            pieces.append(functools.reduce(jnp.add, held))
        return jnp.concatenate(pieces, axis=-1).reshape(rows, width)

    def turn(turned_refs):
        joined = jnp.concatenate([ref[...] for ref in turned_refs], axis=1)
        return jnp.concatenate([joined[s].T for s in range(samples)], axis=0)

    mixed = join(mixed_refs)
    gate = gate_ref[...].reshape(rows, width)
    gated = (gate * mixed).astype(BF16)
    attended = dot(gated, out_w_ref[...]).reshape(samples, tokens, width)
    block_ref[...] = (partial_ref[...] + zero_gate[None] * attended).astype(BF16)
    add_to(step, out_acc, dot(gated, grad_att, 0, 0))
    zero_grad, zero_sum, cond_gate = zero_back(
        grad_out * attended * slope(zero_gate)[None], cond, zero_w_ref
    )
    add_to(step, zero_w_acc, zero_grad)
    add_to(step, zero_b_out, zero_sum)
    grad_queries = join(dq_refs)
    add_to(step, q_bias_out, column_sum(grad_queries))
    grad_gate = gated_grad_ref[...].reshape(rows, width) * mixed * slope(gate)
    grad_joined = jnp.concatenate(
        [grad_queries.astype(BF16), turn(dkt_refs), turn(dvt_refs), grad_gate.astype(BF16)], axis=-1
    )
    add_to(step, qkvg_acc, dot(first, grad_joined, 0, 0))
    grad_input = dot(grad_joined, qkvg_t_ref[...]).reshape(samples, tokens, width)
    weight_grad, bias_sum, gain_sum, cond_norm, acts_part = adaptive_back(
        grad_input, normed, factor, scaled, gain_ref[...], cond_normed, cond_w_ref
    )
    add_to(step, cond_w_acc, weight_grad)
    add_to(step, cond_b_out, bias_sum)
    add_to(step, gain_out, gain_sum)
    acts_grad_ref[...] = (
        grad_out + norm_back(acts_part + acts_part_ref[...], normed, inverse)
    ).astype(BF16)
    cond_grad_ref[...] = (
        cond_gate
        + cond_gate_in[...]
        + norm_back(cond_norm + cond_norm_in[...], cond_normed, cond_inverse)
    )

    @pl.when(step == pl.num_programs(0) - 1)
    def _():
        qkvg_out[...] = qkvg_acc[...].astype(BF16)
        out_out[...] = out_acc[...].astype(BF16)
        cond_w_out[...] = cond_w_acc[...].astype(BF16)
        zero_w_out[...] = zero_w_acc[...].astype(BF16)


def outputs_call(acts, cot, cond, first, gate, gated_grad, partial, acts_part, cond_gate, cond_norm,
                 mixeds, dqs, dkts, dvts, fixed, heads):
    samples, length, width = acts.shape
    cond_width = cond.shape[1]
    rows = samples * length
    chunks = len(mixeds)
    block = rows_of((samples, TOKENS, width), 1, 3)
    cond_block = rows_of((TOKENS, cond_width), 0, 2)
    window = rows_of((samples, TOKENS, WINDOW), 1, 3)
    turned = rows_of((samples, width // chunks, TOKENS), 2, 3)
    weights = [(width, 4 * width), (width, width), (cond_width, 2 * width), (cond_width, width)]
    vectors = [(1, width), (1, width), (1, cond_width), (1, width)]
    return pl.pallas_call(
        functools.partial(outputs_kernel, width // heads, chunks),
        grid=(length // TOKENS,),
        in_specs=[block, block, cond_block] + [block] * 5 + [cond_block] * 2
        + [window] * (2 * chunks) + [turned] * (2 * chunks) + [whole(a) for a in fixed],
        out_specs=[block, block, cond_block] + [fixed_out(s) for s in weights + vectors],
        out_shape=[jax.ShapeDtypeStruct(acts.shape, BF16)] * 2
        + [jax.ShapeDtypeStruct(cond.shape, F32)]
        + [jax.ShapeDtypeStruct(s, BF16) for s in weights]
        + [jax.ShapeDtypeStruct(s, F32) for s in vectors],
        scratch_shapes=[pltpu.VMEM(s, F32) for s in weights],
        compiler_params=params(),
        cost_estimate=cost(2 * rows * width * width * 12, rows * width * 50),
        name="outputs",
    )(acts, cot, cond, first, gate, gated_grad, partial, acts_part, cond_gate, cond_norm,
      *mixeds, *dqs, *dkts, *dvts, *fixed)


def scatter_sum(parts, axis, count, order):
    bits = count.bit_length() - 1
    index = lax.axis_index(axis)
    held = [part.reshape((2,) * bits + part.shape[1:]) for part in parts]
    left = list(range(bits - 1, -1, -1))
    for bit in order:
        place = left.index(bit)
        left.remove(bit)
        mine = (index >> bit) & 1
        pairs = [(i, i ^ (1 << bit)) for i in range(count)]
        sent = [
            lax.ppermute(lax.dynamic_index_in_dim(part, 1 - mine, place, keepdims=False), axis, pairs)
            for part in held
        ]
        kept = [lax.dynamic_index_in_dim(part, mine, place, keepdims=False) for part in held]
        held = [(k.astype(F32) + s.astype(F32)).astype(k.dtype) for k, s in zip(kept, sent)]
    return held


def all_sum(parts, axis, count):
    for bit in range(count.bit_length() - 1):
        pairs = [(i, i ^ (1 << bit)) for i in range(count)]
        sent = [lax.ppermute(part, axis, pairs) for part in parts]
        parts = [(p.astype(F32) + s.astype(F32)).astype(p.dtype) for p, s in zip(parts, sent)]
    return parts


def body(
    struct_count, sample_devices,
    acts, cond, pair, lengths, token_mask, cond_gains, cond_w, cond_bias, output_gate_weights, zero_bias,
    qkvg_w, q_bias, out_w, swiglu_w, down_w, pair_gain, pair_w, cotangent,
):
    acts, cond, pair, cotangent = acts[0], cond[0], pair[0], cotangent[0]
    samples, length, width = acts.shape
    cond_width = cond.shape[1]
    heads = pair_w.shape[1]
    head_dim = width // heads
    chunks = heads // CHUNK_HEADS
    count = sample_devices
    share = length // count
    low_first = range(count.bit_length() - 1)
    position = lax.iota(jnp.int32, length)
    key_valid = (position < lengths[0]) & ((token_mask[0] == 1) | (position == 0))
    valid = key_valid.astype(F32)[None]
    gain_row = pair_gain[None]
    pair_wt = pair_w.T

    bias_rows = pair_forward(pair, gain_row, pair_wt, valid)
    bias = lax.all_gather(jnp.swapaxes(bias_rows, 0, 1), "sample", axis=0, tiled=False)
    split = share % 16 != 0
    if split:
        bias = jnp.swapaxes(bias, 0, 1).reshape(1, heads, length, length)

    gains = [cond_gains[None, b * cond_width : (b + 1) * cond_width] for b in range(2)]
    cond_ws = [cond_w[:, 2 * b * width : 2 * (b + 1) * width] for b in range(2)]
    cond_bs = [cond_bias[None, b * width : (b + 1) * width] for b in range(2)]
    zero_ws = [output_gate_weights[:, b * width : (b + 1) * width] for b in range(2)]
    zero_bs = [zero_bias[None, b * width : (b + 1) * width] for b in range(2)]

    first, gate, gated_grad, *rest = inputs_call(
        acts, cotangent, cond, gains[0], cond_ws[0], cond_bs[0], zero_ws[0], zero_bs[0],
        qkvg_w, q_bias[None], out_w.T, heads,
    )
    nats, turned = rest[:4], rest[4:]
    (partial, acts_part, cond_gate, cond_norm, swiglu_grad, down_grad, cond_w_one, zero_w_one,
     cond_b_one, zero_b_one, gain_one) = transition_call(
        acts, cotangent, cond, gains[1], cond_ws[1], cond_bs[1], zero_ws[1], zero_bs[1],
        swiglu_w, down_w,
    )

    def slabs(array):
        return array.reshape((count, array.shape[0] // count) + array.shape[1:])

    early = scatter_sum(
        [slabs(a) for a in (swiglu_grad, down_grad, cond_w_one, zero_w_one)], "sample", count, low_first
    )
    early = all_sum(early, "struct", struct_count)

    mixeds, dqs, dkts, dvts, bias_grads = [], [], [], [], []
    for chunk in range(chunks):
        mixed, dq, dkt, dvt, db = attention_call(chunk, nats, turned, bias, head_dim)
        mixeds.append(mixed)
        dqs.append(dq)
        dkts.append(dkt)
        dvts.append(dvt)
        if split:
            db = jnp.swapaxes(db.reshape(CHUNK_HEADS, count, share, length), 0, 1)
        bias_grads += scatter_sum([db], "sample", count, low_first)

    (block_out, acts_grad, cond_grad, qkvg_grad, out_grad, cond_w_zero, zero_w_zero,
     cond_b_zero, zero_b_zero, gain_zero, q_bias_grad) = outputs_call(
        acts, cotangent, cond, first, gate, gated_grad, partial, acts_part, cond_gate, cond_norm,
        mixeds, dqs, dkts, dvts,
        (gains[0], cond_ws[0], cond_bs[0], zero_ws[0], zero_bs[0], qkvg_w.T, out_w), heads,
    )
    late = scatter_sum(
        [slabs(a) for a in (qkvg_grad, out_grad, cond_w_zero, zero_w_zero)], "sample", count, low_first
    )
    late = all_sum(late, "struct", struct_count)
    (cond_grad,) = scatter_sum([slabs(cond_grad)], "sample", count, low_first)

    bias_grad = jnp.swapaxes(jnp.concatenate(bias_grads, axis=0), 0, 1)
    grad_pair, pair_w_grad, pair_gain_grad = pair_backward(pair, bias_grad, gain_row, pair_wt)
    vectors = [
        jnp.concatenate([gain_zero[0], gain_one[0]]),
        jnp.concatenate([cond_b_zero[0], cond_b_one[0]]),
        jnp.concatenate([zero_b_zero[0], zero_b_one[0]]),
        q_bias_grad[0],
        pair_gain_grad[0],
        pair_w_grad.T.reshape(-1),
    ]
    sizes = [v.shape[0] // count for v in vectors]
    packed = jnp.concatenate([v.reshape(count, -1) for v in vectors], axis=1)
    (packed,) = scatter_sum([packed], "sample", count, low_first)
    (packed,) = all_sum([packed], "struct", struct_count)
    small = []
    at = 0
    for size in sizes:
        small.append(packed[at : at + size])
        at += size
    wide = lambda array: array.astype(F32)
    return (
        block_out[None],
        acts_grad[None],
        cond_grad[None],
        grad_pair[None],
        small[0],
        wide(jnp.concatenate([late[2], early[2]], axis=1)),
        small[1],
        wide(jnp.concatenate([late[3], early[3]], axis=1)),
        small[2],
        wide(late[0]),
        small[3],
        wide(late[1]),
        wide(early[0]),
        wide(early[1]),
        small[4],
        small[5].reshape(-1, heads),
    )


def solution(mesh):
    per_struct = P("struct", "sample", None, None)
    in_specs = (
        (per_struct, P("struct", None, None), per_struct, P("struct"), P("struct", None))
        + (P(),) * 12
        + (per_struct,)
    )
    one, two = P("sample"), P("sample", None)
    out_specs = (
        per_struct, per_struct, P("struct", "sample", None), per_struct,
        one, two, one, two, one, two, one, two, two, two, one, two,
    )
    local = functools.partial(body, mesh.shape["struct"], mesh.shape["sample"])
    return jax.shard_map(local, mesh=mesh, in_specs=in_specs, out_specs=out_specs, check_vma=False)
```

```python
import functools

import jax
import jax.numpy as jnp
from jax import lax
from jax.experimental import pallas as pl
from jax.experimental.pallas import tpu as pltpu
from jax.sharding import PartitionSpec as P

EPS = 1e-05
MASKED = -1000000000.0
F32 = jnp.float32
BF16 = jnp.bfloat16
CHUNK_HEADS = 4
WINDOW = 256
LANES = 128
PIECE = 384
TOKENS = 128
HIDDEN = 768
VMEM_LIMIT = 60 * 2**20


def dot(left, right, left_dim=1, right_dim=0):
    return lax.dot_general(
        left, right, (((left_dim,), (right_dim,)), ((), ())), preferred_element_type=F32
    )


def layer_norm(values):
    center = values - jnp.mean(values, axis=-1, keepdims=True)
    inverse = lax.rsqrt(jnp.mean(center * center, axis=-1, keepdims=True) + EPS)
    return (center * inverse, inverse)


def norm_back(grad_in, normed, inverse):
    mean_grad = jnp.mean(grad_in, axis=-1, keepdims=True)
    mean_proj = jnp.mean(grad_in * normed, axis=-1, keepdims=True)
    return inverse * (grad_in - mean_grad - normed * mean_proj)


def slope(gate):
    return gate * (1.0 - gate)


def column_sum(values):
    return jnp.sum(values.reshape(-1, values.shape[-1]), axis=0, keepdims=True)


def clear(step, *refs):
    @pl.when(step == 0)
    def _():
        for ref in refs:
            ref[...] = jnp.zeros_like(ref)


def spec(block, along=None, at=None):
    rank = len(block)
    if along is not None:
        return pl.BlockSpec(block, lambda t: tuple(t if a == along else 0 for a in range(rank)))
    index = (0,) * rank if at is None else at
    return pl.BlockSpec(block, lambda t: index, pipeline_mode=pl.Buffered(1))


class Order:
    def __init__(self):
        self.zero = 0


def call(name, kernel, grid, ins, outs, scratch, deps, order):
    inputs = len(ins)
    results = len(outs)

    def run(*refs):
        given, rest = refs[:inputs], refs[inputs + len(deps) :]
        rest[results][0] = 0
        kernel(*given, *rest[:results], *rest[results + 1 :])

    *found, zero = pl.pallas_call(
        run,
        grid=(grid,),
        in_specs=[s for _, s in ins] + [pl.BlockSpec(memory_space=pl.ANY)] * len(deps),
        out_specs=[s for _, _, s in outs] + [pl.BlockSpec(memory_space=pltpu.SMEM)],
        out_shape=[jax.ShapeDtypeStruct(shape, dtype) for shape, dtype, _ in outs]
        + [jax.ShapeDtypeStruct((1,), jnp.int32)],
        scratch_shapes=scratch,
        compiler_params=pltpu.CompilerParams(
            vmem_limit_bytes=VMEM_LIMIT, dimension_semantics=("arbitrary",)
        ),
        cost_estimate=pl.CostEstimate(flops=10**11, bytes_accessed=10**6, transcendentals=0),
        name=name,
    )(*[a for a, _ in ins], *deps)
    order.zero = zero[0]
    return found


def tick(deps, order):
    def kernel(out_ref):
        out_ref[0] = 1

    call("tick", kernel, 1, [], [((1,), jnp.int32, pl.BlockSpec(memory_space=pltpu.SMEM))], [], deps, order)


class Halving:
    def __init__(self, order, counts):
        self.order = order
        self.counts = counts

    def places(self):
        found = []
        for p in range(2 ** len(self.order)):
            dest, half = 0, 0
            for i, (axis, bit) in enumerate(self.order):
                value = (p >> (len(self.order) - 1 - i)) & 1
                if axis == "sample":
                    dest |= value << bit
                else:
                    half = value
            found.append((dest, half))
        return found

    def halves(self):
        return 2 if any(axis == "struct" for axis, _ in self.order) else 1

    def pieces(self, shape):
        rows, columns = shape
        return rows // self.counts["sample"], columns // self.halves() // PIECE

    def slabs(self, shapes):
        return (2 ** len(self.order), sum(r * c for r, c in map(self.pieces, shapes)), PIECE)

    def pack(self, out_ref, arrays):
        for p, (dest, half) in enumerate(self.places()):
            held = []
            for array in arrays:
                rows, count = self.pieces(array.shape)
                for c in range(count):
                    at = (half * count + c) * PIECE
                    held.append(array[dest * rows : (dest + 1) * rows, at : at + PIECE])
            out_ref[p] = jnp.concatenate(held, axis=0).astype(out_ref.dtype)

    def unpack(self, slab, shapes):
        found, at = [], 0
        for shape in shapes:
            rows, count = self.pieces(shape)
            part = slab[at : at + rows * count].reshape(count, rows, PIECE)
            found.append(jnp.swapaxes(part, 0, 1).reshape(rows, count * PIECE))
            at += rows * count
        return found

    def arrange(self, array):
        bits = len(self.order)
        split = array.reshape((2,) * bits + array.shape[1:])
        turn = [bits - 1 - bit for _, bit in self.order] + list(range(bits, split.ndim))
        return jnp.transpose(split, turn).reshape(array.shape)

    def run(self, array, order, over_struct=True):
        def exchange(array, axis, bit):
            return lax.ppermute(array, axis, [(i, i ^ (1 << bit)) for i in range(self.counts[axis])])

        def take(pair, start, size):
            left, right = [lax.dynamic_slice_in_dim(a, start, size, 0) for a in pair]
            zero = order.zero.astype(F32) if size == 1 else 0.0
            return (left.astype(F32) + right.astype(F32) + zero).astype(left.dtype)

        pair, start, size = None, 0, array.shape[0]
        for axis, bit in self.order:
            mine = (lax.axis_index(axis) >> bit) & 1
            size = size // 2
            if pair is None:
                sent = kept = array
                after = mine * size
            else:
                start = start + order.zero
                sent = take(pair, start + (1 - mine) * size, size)
                kept = take(pair, start + mine * size, size)
                after = 0
            received = exchange(sent, axis, bit)
            yield [sent]
            pair, start = (kept, received), after
        held = take(pair, start + order.zero, 1)[0]
        if not over_struct:
            return held
        if self.halves() == 2:
            received = exchange(held, "struct", 0)
            yield [held]
            first = lax.axis_index("struct") == 0
            return jnp.where(first, held, received), jnp.where(first, received, held)
        for bit in range(self.counts["struct"].bit_length() - 1):
            received = exchange(held, "struct", bit)
            yield [held]
            held = (held.astype(F32) + received.astype(F32)).astype(held.dtype)
        return held

    def unpack_sum(self, result, shapes):
        if self.halves() == 1:
            return self.unpack(result, shapes)
        parts = [self.unpack(half, shapes) for half in result]
        return [jnp.concatenate(pair, axis=1) for pair in zip(*parts)]


def doubling(array, exchanges, counts, order):
    for axis, bit in exchanges:
        received = lax.ppermute(array, axis, [(i, i ^ (1 << bit)) for i in range(counts[axis])])
        yield [array]
        array = array + received + order.zero.astype(F32)
    return array


class Running:
    def __init__(self, steps):
        self.steps = steps
        self.result = None

    def step(self):
        if self.result is None:
            try:
                return list(next(self.steps))
            except StopIteration as stop:
                self.result = stop.value
                return list(self.result) if isinstance(self.result, tuple) else [self.result]
        return []

    def finish(self):
        while self.result is None:
            self.step()
        return self.result


def advance(*running):
    return [array for r in running for array in r.step()]


def finish(*running):
    while any(r.result is None for r in running):
        advance(*running)
    return [r.result for r in running]


def pair_forward_kernel(pair_ref, gain_ref, weight_ref, mask_ref, lengths_ref, out_ref, terms):
    gain = gain_ref[...].astype(F32)
    rows, length, channels = pair_ref.shape
    average = jnp.full((channels, channels), 1.0 / channels, BF16)
    position = lax.broadcasted_iota(jnp.int32, (1, length), 1)
    valid = (position < lengths_ref[0]) & ((mask_ref[...] == 1) | (position == 0))
    for i in range(rows):
        values = pair_ref[i]
        center = values.astype(F32) - dot(values, average)
        inverse = lax.rsqrt(jnp.mean(center * center, axis=-1, keepdims=True) + EPS)
        affine = (center * inverse * gain).astype(BF16)
        terms[i] = jnp.where(valid, dot(weight_ref[...], affine, 0, 1), MASKED)
    for h in range(terms.shape[1]):
        out_ref[h] = terms[:, h, :].astype(BF16)


def pair_forward(pair, gain, weight, mask, lengths, order):
    rows, length, channels = pair.shape
    heads = weight.shape[1]
    block = 16 if rows % 16 == 0 else rows
    return call(
        "pair_forward",
        pair_forward_kernel,
        rows // block,
        [
            (pair, spec((block, length, channels), 0)),
            (gain, spec(gain.shape)),
            (weight, spec(weight.shape)),
            (mask, spec(mask.shape)),
            (lengths, pl.BlockSpec(memory_space=pltpu.SMEM)),
        ],
        [((heads, rows, length), BF16, spec((heads, block, length), 1))],
        [pltpu.VMEM((block, heads, length), F32)],
        [],
        order,
    )[0]


def pair_backward_kernel(chunks, pair_ref, gain_ref, weight_ref, *refs):
    grad_refs, (out_ref, weight_grad_ref, grads) = refs[:chunks], refs[chunks:]
    gain = gain_ref[...]
    channels = pair_ref.shape[2]
    average = jnp.full((channels, channels), 1.0 / channels, BF16)
    clear(pl.program_id(0), weight_grad_ref)
    for chunk, ref in enumerate(grad_refs):
        for h in range(ref.shape[0]):
            grads[:, chunk * ref.shape[0] + h, :] = ref[h].astype(F32)
    scaled = weight_ref[...].astype(F32) * gain
    means = jnp.broadcast_to(jnp.mean(scaled, axis=-1, keepdims=True), scaled.shape)
    full = jnp.concatenate([scaled, means], axis=1)
    high = full.astype(BF16)
    parts = jnp.concatenate([high, (full - high.astype(F32)).astype(BF16)], axis=0)

    def row(i, carry):
        values = pair_ref[i]
        center = values.astype(F32) - dot(values, average)
        inverse = lax.rsqrt(jnp.mean(center * center, axis=-1, keepdims=True) + EPS)
        normed = center * inverse
        grad = grads[i].astype(BF16)
        weight_grad_ref[...] += dot(grad, (normed * gain).astype(BF16))
        both = dot(jnp.concatenate([grad, grad], axis=0), parts, 0, 0)
        grad_normed = both[:, :channels]
        mean_proj = jnp.mean(grad_normed * normed, axis=-1, keepdims=True)
        out_ref[i] = inverse * (grad_normed - both[:, channels:] - normed * mean_proj)
        return carry

    lax.fori_loop(0, pair_ref.shape[0], row, 0, unroll=8)


def pair_backward(block, pair, grads, gain, weight_t, deps, order):
    rows, length, channels = pair.shape
    heads = weight_t.shape[0]
    return call(
        "pair_backward",
        functools.partial(pair_backward_kernel, len(grads)),
        rows // block,
        [
            (pair, spec((block, length, channels), 0)),
            (gain, spec(gain.shape)),
            (weight_t, spec(weight_t.shape)),
        ]
        + [(g, spec((g.shape[0], block, length), 1)) for g in grads],
        [
            (pair.shape, F32, spec((block, length, channels), 0)),
            ((heads, channels), F32, spec((heads, channels))),
        ],
        [pltpu.VMEM((block, heads, length), F32)],
        deps,
        order,
    )


def conditions(cond_ref, gain_ref, cond_w_ref, cond_b_ref, zero_w_ref, zero_b_ref, zero_gate_ref, factor_ref, shift_ref):
    cond = cond_ref[...]
    width = zero_gate_ref.shape[1]
    zero_gate_ref[...] = jax.nn.sigmoid(dot(cond, zero_w_ref[...]) + zero_b_ref[...])
    cond_normed, _ = layer_norm(cond.astype(F32))
    projected = dot((cond_normed * gain_ref[...]).astype(BF16), cond_w_ref[...])
    factor_ref[...] = jax.nn.sigmoid(projected[:, :width] + cond_b_ref[...])
    shift_ref[...] = projected[:, width:]


def conditions_back(cond_ref, gain_ref, cond_w_ref, zero_w_ref, zero_grad, projected):
    cond = cond_ref[...]
    cond_normed, cond_inverse = layer_norm(cond.astype(F32))
    scaled = (cond_normed * gain_ref[...]).astype(BF16)
    grad_scaled = dot(projected, cond_w_ref[...], 1, 1)
    return (
        dot(scaled, projected, 0, 0),
        dot(cond, zero_grad, 0, 0),
        column_sum(grad_scaled * cond_normed),
        dot(zero_grad, zero_w_ref[...], 1, 1),
        grad_scaled * gain_ref[...],
        cond_normed,
        cond_inverse,
    )


def step_rows(step, tokens):
    return pl.ds(pl.multiple_of(step * tokens, tokens), tokens)


def window_start(chunk, head_dim):
    return chunk * CHUNK_HEADS * head_dim // LANES * LANES


def inputs_kernel(
    head_dim, acts_ref, cot_ref, cond_ref, gain_ref, cond_w_ref, cond_b_ref, zero_w_ref, zero_b_ref,
    qkvg_ref, q_bias_ref, out_w_ref,
    input_ref, gate_ref, gated_grad_ref, q_ref, k_ref, v_ref, g_ref, qt_ref, kt_ref, vt_ref, gt_ref,
    zero_gate_ref, factor_ref, shift_ref,
):
    step = pl.program_id(0)
    samples, tokens, width = acts_ref.shape

    @pl.when(step == 0)
    def _():
        conditions(
            cond_ref, gain_ref, cond_w_ref, cond_b_ref, zero_w_ref, zero_b_ref, zero_gate_ref, factor_ref, shift_ref
        )

    here = step_rows(step, tokens)
    normed, _ = layer_norm(acts_ref[...].astype(F32))
    first = (factor_ref[here, :][None] * normed + shift_ref[here, :][None]).astype(BF16)
    input_ref[...] = first
    first = first.reshape(samples * tokens, width)
    grad_att = (cot_ref[...].astype(F32) * zero_gate_ref[here, :][None]).astype(BF16)
    grad_gated = dot(grad_att.reshape(samples * tokens, width), out_w_ref[...], 1, 1)
    gated_grad_ref[...] = grad_gated.reshape(samples, tokens, width)
    gate = jax.nn.sigmoid(dot(first, qkvg_ref[:, 3 * width :]))
    gate_ref[...] = gate.reshape(samples, tokens, width)

    def put(values, nat_ref, t_ref):
        low = values.astype(BF16).reshape(samples, tokens, width)
        for chunk in range(nat_ref.shape[0]):
            start = window_start(chunk, head_dim)
            nat_ref[chunk] = low[:, :, start : start + WINDOW]
        for s in range(samples):
            t_ref[s] = low[s].T

    put(grad_gated * gate, g_ref, gt_ref)
    put(dot(first, qkvg_ref[:, :width]) + q_bias_ref[...], q_ref, qt_ref)
    put(dot(first, qkvg_ref[:, width : 2 * width]), k_ref, kt_ref)
    put(dot(first, qkvg_ref[:, 2 * width : 3 * width]), v_ref, vt_ref)


def inputs_call(acts, cot, cond, branch, qkvg_w, q_bias, out_w, heads, deps, order):
    samples, length, width = acts.shape
    chunks = heads // CHUNK_HEADS
    block = spec((samples, TOKENS, width), 1)
    nat = spec((chunks, samples, TOKENS, WINDOW), 2)
    turned = spec((samples, width, TOKENS), 2)
    rows = samples * length
    return call(
        "inputs",
        functools.partial(inputs_kernel, width // heads),
        length // TOKENS,
        [(acts, block), (cot, block), (cond, spec(cond.shape))]
        + branch
        + [(a, spec(a.shape)) for a in (qkvg_w, q_bias, out_w)],
        [(acts.shape, BF16, block), (acts.shape, F32, block), (acts.shape, F32, block)]
        + [((chunks, samples, length, WINDOW), BF16, nat)] * 4
        + [((samples, width, length), BF16, turned)] * 4
        + [((length, width), F32, spec((length, width)))] * 2,
        [pltpu.VMEM((length, width), F32)],
        deps,
        order,
    )


def transition_kernel(
    halving, acts_ref, cot_ref, cond_ref, gain_ref, cond_w_ref, cond_b_ref, zero_w_ref, zero_b_ref,
    swiglu_ref, down_ref,
    partial_ref, acts_grad_ref, cond_gate_ref, cond_norm_ref, packed_out, cond_b_out, zero_b_out, gain_out,
    swiglu_acc, down_acc, zero_gate_ref, factor_ref, shift_ref, zero_low, projected,
):
    step = pl.program_id(0)
    clear(step, swiglu_acc, down_acc, cond_b_out, zero_b_out)
    samples, tokens, width = acts_ref.shape
    rows = samples * tokens
    hidden_width = down_ref.shape[0]

    @pl.when(step == 0)
    def _():
        conditions(
            cond_ref, gain_ref, cond_w_ref, cond_b_ref, zero_w_ref, zero_b_ref, zero_gate_ref, factor_ref, shift_ref
        )

    here = step_rows(step, tokens)
    zero_gate = zero_gate_ref[here, :]
    factor = factor_ref[here, :]
    acts = acts_ref[...].astype(F32)
    normed, _ = layer_norm(acts)
    second = (factor[None] * normed + shift_ref[here, :][None]).astype(BF16).reshape(rows, width)
    grad_out = cot_ref[...].astype(F32)
    grad_tr = (grad_out * zero_gate[None]).astype(BF16).reshape(rows, width)
    transition = grad_input = 0.0
    second_t = second.T
    for at in range(0, hidden_width, HIDDEN):
        gate_at, up_at = slice(at, at + HIDDEN), slice(hidden_width + at, hidden_width + at + HIDDEN)
        gate_part = dot(second, swiglu_ref[:, gate_at])
        up_part = dot(second, swiglu_ref[:, up_at])
        gate_sig = jax.nn.sigmoid(gate_part)
        silu = gate_part * gate_sig
        product = (silu * up_part).astype(BF16)
        transition += dot(product, down_ref[gate_at, :])
        grad_product = dot(grad_tr, down_ref[gate_at, :], 1, 1)
        down_acc[gate_at, :] += dot(product, grad_tr, 0, 0)
        grad_up = (grad_product * silu).astype(BF16)
        grad_gate = (grad_product * up_part * gate_sig * (1.0 + gate_part * (1.0 - gate_sig))).astype(BF16)
        swiglu_acc[:, gate_at] += dot(second_t, grad_gate)
        swiglu_acc[:, up_at] += dot(second_t, grad_up)
        grad_input += dot(grad_gate, swiglu_ref[:, gate_at], 1, 1)
        grad_input += dot(grad_up, swiglu_ref[:, up_at], 1, 1)
    transition = transition.reshape(samples, tokens, width)
    grad_input = grad_input.reshape(samples, tokens, width)
    partial_ref[...] = acts + zero_gate[None] * transition
    grad_zero = jnp.sum(grad_out * transition, axis=0) * slope(zero_gate)
    zero_b_out[...] += column_sum(grad_zero)
    zero_low[here, :] = grad_zero.astype(BF16)
    grad_factor = jnp.sum(grad_input * normed, axis=0) * slope(factor)
    cond_b_out[...] += column_sum(grad_factor)
    projected[here, :width] = grad_factor.astype(BF16)
    projected[here, width:] = jnp.sum(grad_input, axis=0).astype(BF16)
    acts_grad_ref[...] = grad_input * factor[None]

    @pl.when(step == pl.num_programs(0) - 1)
    def _():
        cond_w_grad, zero_w_grad, gain_grad, cond_gate, cond_norm, _, _ = conditions_back(
            cond_ref, gain_ref, cond_w_ref, zero_w_ref, zero_low[...], projected[...]
        )
        gain_out[...] = gain_grad
        cond_gate_ref[...] = cond_gate
        cond_norm_ref[...] = cond_norm
        halving.pack(packed_out, [swiglu_acc, down_acc, cond_w_grad, zero_w_grad])


def transition_call(acts, cot, cond, branch, swiglu, down, halving, deps, order):
    samples, length, width = acts.shape
    cond_width = cond.shape[1]
    hidden = down.shape[0]
    rows = samples * length
    block = spec((samples, TOKENS, width), 1)
    weights = [(width, 2 * hidden), (hidden, width), (cond_width, 2 * width), (cond_width, width)]
    vectors = [(1, width), (1, width), (1, cond_width)]
    results = call(
        "transition",
        functools.partial(transition_kernel, halving),
        length // TOKENS,
        [(acts, block), (cot, block), (cond, spec(cond.shape))]
        + branch
        + [(swiglu, spec(swiglu.shape)), (down, spec(down.shape))],
        [(acts.shape, F32, block)] * 2
        + [(cond.shape, F32, spec(cond.shape))] * 2
        + [(halving.slabs(weights), BF16, spec(halving.slabs(weights)))]
        + [(s, F32, spec(s)) for s in vectors],
        [pltpu.VMEM(s, F32) for s in weights[:2]]
        + [pltpu.VMEM((length, width), F32)] * 3
        + [pltpu.VMEM((length, width), BF16), pltpu.VMEM((length, 2 * width), BF16)],
        deps,
        order,
    )
    return results, weights


def attention_kernel(
    halving, head_dim, first_lane, q_ref, k_ref, v_ref, g_ref, qt_ref, kt_ref, vt_ref, gt_ref, bias_ref,
    mixed_ref, dq_ref, dkt_ref, dvt_ref, db_ref, kz, vz, plow, dslow, dsum,
):
    h = pl.program_id(0)
    samples, length, wide = q_ref.shape
    scale = head_dim ** (-0.5)
    off = pl.multiple_of(first_lane + h * head_dim, 16)
    lane = lax.broadcasted_iota(jnp.int32, (1, wide), 1)
    mask = ((lane >= off) & (lane < off + head_dim)).astype(BF16)

    @pl.when(h == 0)
    def _():
        mixed_ref[...] = jnp.zeros_like(mixed_ref)
        dq_ref[...] = jnp.zeros_like(dq_ref)

    kz[...] = jnp.zeros_like(kz)
    vz[...] = jnp.zeros_like(vz)
    for s in range(samples):
        kz[s, pl.ds(off, head_dim), :] = kt_ref[s]
        vz[s, pl.ds(off, head_dim), :] = vt_ref[s]
    parts, _, share, _ = bias_ref.shape
    if share % 16 == 0:
        bias = bias_ref[:, 0].reshape(length, length).astype(F32)
    else:
        bias = jnp.concatenate([bias_ref[p, 0].astype(F32) for p in range(parts)], axis=0)
    for s in range(samples):
        x = dot(q_ref[s], kz[s]) * scale + bias
        x = jnp.exp(x - jnp.max(x, axis=-1, keepdims=True))
        probs = x * (1.0 / jnp.sum(x, axis=-1, keepdims=True))
        low = probs.astype(BF16)
        plow[...] = low
        mixed = dot(low, v_ref[s] * mask)
        mixed_ref[s] += mixed
        grad = g_ref[s]
        delta = jnp.sum(grad.astype(F32) * mixed, axis=-1, keepdims=True)
        grad_scores = probs * (dot(grad, vz[s]) - delta)
        grad_low = (grad_scores * scale).astype(BF16)
        dslow[...] = grad_low
        total = grad_scores if s == 0 else dsum[...] + grad_scores
        if s < samples - 1:
            dsum[...] = total
        else:
            for p, (dest, _) in enumerate(halving.places()):
                db_ref[p, 0] = total[dest * share : (dest + 1) * share].astype(BF16)
        dq_ref[s] += dot(grad_low, k_ref[s] * mask)
        dvt_ref[s] = dot(gt_ref[s], plow[...]).astype(BF16)
        dkt_ref[s] = dot(qt_ref[s], dslow[...]).astype(BF16)


def attention_call(chunk, nats, turned, bias, first_head, head_dim, halving, deps, order):
    _, samples, length, wide = nats[0].shape
    parts, _, share, _ = bias.shape
    local = chunk * CHUNK_HEADS - first_head
    nat = pl.BlockSpec((None, samples, length, wide), lambda h: (chunk, 0, 0, 0))
    turn = pl.BlockSpec((samples, head_dim, length), lambda h: (0, chunk * CHUNK_HEADS + h, 0))
    turn_out = pl.BlockSpec((samples, head_dim, length), lambda h: (0, h, 0))
    bias_in = pl.BlockSpec((parts, 1, share, length), lambda h: (0, local + h, 0, 0))
    bias_out = pl.BlockSpec((parts, 1, share, length), lambda h: (0, h, 0, 0))
    held = pl.BlockSpec((samples, length, wide), lambda h: (0, 0, 0))
    return call(
        "attention",
        functools.partial(
            attention_kernel,
            halving,
            head_dim,
            chunk * CHUNK_HEADS * head_dim - window_start(chunk, head_dim),
        ),
        CHUNK_HEADS,
        [(a, nat) for a in nats] + [(a, turn) for a in turned] + [(bias, bias_in)],
        [((samples, length, wide), F32, held)] * 2
        + [((samples, CHUNK_HEADS * head_dim, length), BF16, turn_out)] * 2
        + [((parts, CHUNK_HEADS, share, length), BF16, bias_out)],
        [
            pltpu.VMEM((samples, wide, length), BF16),
            pltpu.VMEM((samples, wide, length), BF16),
            pltpu.VMEM((length, length), BF16),
            pltpu.VMEM((length, length), BF16),
            pltpu.VMEM((length, length), F32),
        ],
        deps,
        order,
    )


def mixed_kernel(head_dim, chunks, *refs):
    (cot_ref, gate_ref, gated_grad_ref, partial_ref, zero_gate_ref, out_w_ref), refs = refs[:6], refs[6:]
    mixed_refs, refs = refs[:chunks], refs[chunks:]
    dq_refs, refs = refs[:chunks], refs[chunks:]
    dkt_refs, refs = refs[:chunks], refs[chunks:]
    dvt_refs, refs = refs[:chunks], refs[chunks:]
    block_ref, joined_ref, zero_low_ref, out_out, zero_b_out, q_bias_out = refs
    clear(pl.program_id(0), out_out, zero_b_out, q_bias_out)
    samples, tokens, width = cot_ref.shape
    rows = samples * tokens
    zero_gate = zero_gate_ref[...]
    grad_out = cot_ref[...].astype(F32)
    grad_att = (grad_out * zero_gate[None]).astype(BF16).reshape(rows, width)

    def join(window_refs):
        pieces = []
        for tile in range(width // LANES):
            held = [
                ref[:, :, tile * LANES - start : (tile + 1) * LANES - start]
                for chunk, ref in enumerate(window_refs)
                for start in [window_start(chunk, head_dim)]
                if start <= tile * LANES < start + WINDOW
            ]
            pieces.append(functools.reduce(jnp.add, held))
        return jnp.concatenate(pieces, axis=-1).reshape(rows, width)

    def turn(turned_refs):
        joined = jnp.concatenate([ref[...] for ref in turned_refs], axis=1)
        return jnp.concatenate([joined[s].T for s in range(samples)], axis=0)

    mixed = join(mixed_refs)
    gate = gate_ref[...].reshape(rows, width)
    gated = (gate * mixed).astype(BF16)
    attended = dot(gated, out_w_ref[...]).reshape(samples, tokens, width)
    block_ref[...] = (partial_ref[...] + zero_gate[None] * attended).astype(BF16)
    out_out[...] += dot(gated, grad_att, 0, 0)
    grad_zero = jnp.sum(grad_out * attended, axis=0) * slope(zero_gate)
    zero_b_out[...] += column_sum(grad_zero)
    zero_low_ref[...] = grad_zero.astype(BF16)
    grad_queries = join(dq_refs)
    q_bias_out[...] += column_sum(grad_queries)
    grad_gate = gated_grad_ref[...].reshape(rows, width) * mixed * slope(gate)
    parts = [grad_queries.astype(BF16), turn(dkt_refs), turn(dvt_refs), grad_gate.astype(BF16)]
    for i, part in enumerate(parts):
        joined_ref[:, :, i * width : (i + 1) * width] = part.reshape(samples, tokens, width)


def mixed_call(cot, gate, gated_grad, partial, zero_gate, out_w, mixeds, dqs, dkts, dvts, heads, deps, order):
    samples, length, width = cot.shape
    chunks = len(mixeds)
    block = spec((samples, TOKENS, width), 1)
    window = spec((samples, TOKENS, WINDOW), 1)
    turned = spec((samples, width // chunks, TOKENS), 2)
    tokens = spec((TOKENS, width), 0)
    return call(
        "mixed",
        functools.partial(mixed_kernel, width // heads, chunks),
        length // TOKENS,
        [(a, block) for a in (cot, gate, gated_grad, partial)]
        + [(zero_gate, tokens), (out_w, spec(out_w.shape))]
        + [(a, window) for a in mixeds + dqs]
        + [(a, turned) for a in dkts + dvts],
        [
            (cot.shape, BF16, block),
            ((samples, length, 4 * width), BF16, spec((samples, TOKENS, 4 * width), 1)),
            ((length, width), BF16, tokens),
        ]
        + [(s, F32, spec(s)) for s in ((width, width), (1, width), (1, width))],
        [],
        deps,
        order,
    )


def qkvg_kernel(halving, first_ref, joined_ref, packed_out):
    step = pl.program_id(0)
    samples, length, width = first_ref.shape
    rows = samples * length
    grad = dot(first_ref[...].reshape(rows, width), joined_ref[...].reshape(rows, width), 0, 0)
    blocks = 4
    share, count = halving.pieces((width, blocks * width))
    wide = width // PIECE

    for block in range(blocks):

        @pl.when(step == block)
        def _():
            for p, (dest, half) in enumerate(halving.places()):
                for c in range(wide):
                    piece = block * wide + c - half * count
                    if 0 <= piece < count:
                        packed_out[p, piece * share : (piece + 1) * share] = grad[
                            dest * share : (dest + 1) * share, c * PIECE : (c + 1) * PIECE
                        ].astype(BF16)


def qkvg_call(first, grad_joined, halving, deps, order):
    samples, length, width = first.shape
    slabs = halving.slabs([(width, 4 * width)])
    (packed,) = call(
        "qkvg_grad",
        functools.partial(qkvg_kernel, halving),
        4,
        [(first, spec(first.shape)), (grad_joined, spec((samples, length, width), 2))],
        [(slabs, BF16, spec(slabs))],
        [],
        deps,
        order,
    )
    return packed


def outputs_kernel(
    acts_ref, cot_ref, joined_ref, acts_part_ref, factor_ref, qkvg_ref, acts_grad_ref, projected_ref, cond_b_out
):
    clear(pl.program_id(0), cond_b_out)
    samples, tokens, width = acts_ref.shape
    rows = samples * tokens
    factor = factor_ref[...]
    normed, inverse = layer_norm(acts_ref[...].astype(F32))
    grad_input = dot(joined_ref[...].reshape(rows, 4 * width), qkvg_ref[...], 1, 1).reshape(
        samples, tokens, width
    )
    grad_factor = jnp.sum(grad_input * normed, axis=0) * slope(factor)
    cond_b_out[...] += column_sum(grad_factor)
    projected_ref[:, :width] = grad_factor.astype(BF16)
    projected_ref[:, width:] = jnp.sum(grad_input, axis=0).astype(BF16)
    acts_grad_ref[...] = (
        cot_ref[...].astype(F32) + norm_back(grad_input * factor[None] + acts_part_ref[...], normed, inverse)
    ).astype(BF16)


def outputs_call(acts, cot, joined, acts_part, factor, qkvg_w, deps, order):
    samples, length, width = acts.shape
    block = spec((samples, TOKENS, width), 1)
    return call(
        "outputs",
        outputs_kernel,
        length // TOKENS,
        [(acts, block), (cot, block), (joined, spec((samples, TOKENS, 4 * width), 1)), (acts_part, block)]
        + [(factor, spec((TOKENS, width), 0)), (qkvg_w, spec(qkvg_w.shape))],
        [
            (acts.shape, BF16, block),
            ((length, 2 * width), BF16, spec((TOKENS, 2 * width), 0)),
            ((1, width), F32, spec((1, width))),
        ],
        [],
        deps,
        order,
    )


def conditions_kernel(
    rest, small, vector_parts, cond_ref, gain_ref, cond_w_ref, zero_w_ref, zero_low_ref, projected_ref,
    cond_gate_in, cond_norm_in, out_w_grad_ref, *refs
):
    vector_refs, (packed_out, small_out) = refs[:vector_parts], refs[vector_parts:]
    cond_w_grad, zero_w_grad, gain_grad, cond_gate, cond_norm, cond_normed, cond_inverse = conditions_back(
        cond_ref, gain_ref, cond_w_ref, zero_w_ref, zero_low_ref[...], projected_ref[...]
    )
    cond_grad = (
        cond_gate + cond_gate_in[...] + norm_back(cond_norm + cond_norm_in[...], cond_normed, cond_inverse)
    )
    rest.pack(packed_out, [out_w_grad_ref, cond_w_grad, zero_w_grad])
    vectors = [gain_grad] + [ref[...] for ref in vector_refs]
    pieces = [v[:, at : at + PIECE] for v in vectors for at in range(0, v.shape[1], PIECE)]
    share = cond_grad.shape[0] // rest.counts["sample"]
    for p, (dest, _) in enumerate(small.places()):
        small_out[p] = jnp.concatenate([cond_grad[dest * share : (dest + 1) * share]] + pieces, axis=0)


def conditions_call(cond, branch, zero_w, zero_low, projected, cond_gate, cond_norm, out_w_grad, vectors, rest, small, deps, order):
    length, cond_width = cond.shape
    width = zero_low.shape[1]
    weights = [out_w_grad.shape, (cond_width, 2 * width), (cond_width, width)]
    slabs = rest.slabs(weights)
    sent = length // rest.counts["sample"] + (sum(v.shape[1] for v in vectors) + cond_width) // PIECE
    small_slabs = (rest.counts["sample"], sent, PIECE)
    fixed = (zero_low, projected, cond_gate, cond_norm, out_w_grad, *vectors)
    results = call(
        "conditions",
        functools.partial(conditions_kernel, rest, small, len(vectors)),
        1,
        [(cond, spec(cond.shape))] + branch[:2] + [zero_w] + [(a, spec(a.shape)) for a in fixed],
        [(slabs, BF16, spec(slabs)), (small_slabs, F32, spec(small_slabs))],
        [],
        deps,
        order,
    )
    return results, weights


def body(
    struct_count, sample_devices,
    acts, cond, pair, lengths, token_mask, cond_gains, cond_w, cond_bias, output_gate_weights, zero_bias,
    qkvg_w, q_bias, out_w, swiglu_w, down_w, pair_gain, pair_w, cotangent,
):
    acts, cond, pair, cotangent = acts[0], cond[0], pair[0], cotangent[0]
    samples, length, width = acts.shape
    cond_width = cond.shape[1]
    heads = pair_w.shape[1]
    head_dim = width // heads
    chunks = heads // CHUNK_HEADS
    counts = {"struct": struct_count, "sample": sample_devices}
    bits = sample_devices.bit_length() - 1
    pair_wt = pair_w.T
    order = Order()

    bias_rows = pair_forward(pair, pair_gain[None], pair_w, token_mask, lengths, order)
    bias = lax.all_gather(bias_rows, "sample", axis=0, tiled=False)

    rows = {}
    at = 0
    packed = [
        ("gain", cond_gains), ("cond_b", cond_bias), ("zero_b", zero_bias), ("q_bias", q_bias), ("pair", pair_gain)
    ]
    vector = jnp.concatenate([v for _, v in packed]).astype(F32)[None]
    for name, v in packed:
        rows[name] = vector[:, at : at + v.shape[0]]
        at += v.shape[0]

    def conditioning(b):
        return [
            (rows["gain"], spec((1, cond_width), at=(0, b))),
            (cond_w, spec((cond_width, 2 * width), at=(0, b))),
            (rows["cond_b"], spec((1, width), at=(0, b))),
        ]

    def zero(b):
        return [
            (output_gate_weights, spec((cond_width, width), at=(0, b))),
            (rows["zero_b"], spec((1, width), at=(0, b))),
        ]

    def path(*order):
        steps = [("struct", 0) if o == "y" else ("sample", o) for o in order]
        steps = [s for s in steps if s[0] == "sample" or struct_count == 2]
        return Halving(steps + [("sample", b) for b in range(4, bits)], counts)

    along_x = path(0, 1, 2, 3)
    along_y = path(0, "y", 2, 3, 1)
    results, early_shapes = transition_call(
        acts, cotangent, cond, conditioning(1) + zero(1), swiglu_w, down_w, along_y, [], order
    )
    partial, acts_part, cond_gate, cond_norm, early, cond_b_one, zero_b_one, gain_one = results
    early = Running(along_y.run(early, order))
    first, gate, gated_grad, *rest = inputs_call(
        acts, cotangent, cond, conditioning(0) + zero(0), qkvg_w, rows["q_bias"], out_w, heads, advance(early), order
    )
    nats, turned, (zero_gate, factor) = rest[:4], rest[4:8], rest[8:]

    mixeds, dqs, dkts, dvts, bias_sums = [], [], [], [], []
    deps = advance(early)
    for chunk in range(chunks):
        mixed, dq, dkt, dvt, db = attention_call(chunk, nats, turned, bias, 0, head_dim, along_x, deps, order)
        mixeds.append(mixed)
        dqs.append(dq)
        dkts.append(dkt)
        dvts.append(dvt)
        bias_sums.append(Running(along_x.run(db, order, over_struct=False)))
        deps = advance(*bias_sums)
        deps += advance(early)

    block_out, grad_joined, zero_low, out_grad, zero_b_zero, q_bias_grad = mixed_call(
        cotangent, gate, gated_grad, partial, zero_gate, out_w, mixeds, dqs, dkts, dvts, heads, deps, order
    )
    deps = advance(*bias_sums, early)
    qkvg_sum = Running(along_y.run(qkvg_call(first, grad_joined, along_y, deps, order), order))
    deps = advance(*bias_sums[:-1], qkvg_sum)
    acts_grad, projected, cond_b_zero = outputs_call(
        acts, cotangent, grad_joined, acts_part, factor, qkvg_w, deps, order
    )
    deps = advance(*bias_sums, qkvg_sum, early)
    (rest, small), rest_shapes = conditions_call(
        cond, conditioning(0), zero(0)[0], zero_low, projected, cond_gate, cond_norm, out_grad,
        [gain_one, cond_b_zero, cond_b_one, zero_b_zero, zero_b_one, q_bias_grad], along_y, along_x, deps, order,
    )
    rest = Running(along_y.run(rest, order))
    small = Running(along_x.run(small, order, over_struct=False))
    deps = advance(*bias_sums, rest, small)
    while any(b.result is None for b in bias_sums):
        tick(deps, order)
        deps = advance(*bias_sums)
    share = length // sample_devices
    block = 16 if share % 16 == 0 else share
    grads = [b.result.reshape(CHUNK_HEADS, -1, length) for b in bias_sums]
    deps += advance(qkvg_sum, rest, small)
    grad_pair, pair_w_grad = pair_backward(block, pair, grads, rows["pair"], pair_wt, deps, order)
    exchanges = [("sample", bit) for bit in range(bits)]
    over_struct = [("struct", bit) for bit in range(struct_count.bit_length() - 1)]
    pair_sum = Running(doubling(pair_w_grad, over_struct + exchanges, counts, order))
    while small.result is None:
        tick(advance(pair_sum, rest, small, qkvg_sum, early), order)
    cond_sum = small.result[:share]
    small = Running(doubling(small.result[share:], over_struct, counts, order))
    finish(pair_sum, rest, small, qkvg_sum, early)

    swiglu_sum, down_sum, cond_w_one, zero_w_one = along_y.unpack_sum(early.result, early_shapes)
    (qkvg_sum,) = along_y.unpack_sum(qkvg_sum.result, [qkvg_w.shape])
    out_sum, cond_w_zero, zero_w_zero = along_y.unpack_sum(rest.result, rest_shapes)

    device = lax.axis_index("sample")

    def mine(array, axis=0):
        size = array.shape[axis] // sample_devices
        return lax.dynamic_slice_in_dim(array, device * size, size, axis)

    vector = small.result.reshape(-1)
    at, found = 0, []
    for size in (2 * cond_width, 2 * width, 2 * width, width):
        found.append(mine(vector[at : at + size]))
        at += size
    gains, cond_b, zero_b, q_b = found
    pair_w_sum = mine(pair_sum.result, 1).T
    pair_g = jnp.sum(pair_w_sum * mine(pair_w).astype(F32), axis=-1) / mine(pair_gain).astype(F32)

    def wide(*parts):
        return jnp.concatenate([p.astype(F32) for p in parts], axis=-1)

    return (
        block_out[None],
        acts_grad[None],
        cond_sum[None],
        grad_pair[None],
        gains,
        wide(cond_w_zero, cond_w_one),
        cond_b,
        wide(zero_w_zero, zero_w_one),
        zero_b,
        wide(qkvg_sum),
        q_b,
        wide(out_sum),
        wide(swiglu_sum),
        wide(down_sum),
        pair_g,
        pair_w_sum,
    )


def solution(mesh):
    per_struct = P("struct", "sample", None, None)
    in_specs = (
        (per_struct, P("struct", None, None), per_struct, P("struct"), P("struct", None))
        + (P(),) * 12
        + (per_struct,)
    )
    one, two = P("sample"), P("sample", None)
    out_specs = (
        per_struct, per_struct, P("struct", "sample", None), per_struct,
        one, two, one, two, one, two, one, two, two, two, one, two,
    )
    local = functools.partial(body, mesh.shape["struct"], mesh.shape["sample"])
    return jax.shard_map(local, mesh=mesh, in_specs=in_specs, out_specs=out_specs, check_vma=False)
```

```python
import functools

import jax
import jax.numpy as jnp
from jax import lax
from jax.experimental import pallas as pl
from jax.experimental.pallas import tpu as pltpu
from jax.sharding import PartitionSpec as P

EPS = 1e-05
MASKED = -1000000000.0
F32 = jnp.float32
BF16 = jnp.bfloat16
CHUNK_HEADS = 2
WINDOW = 256
LANES = 128
PIECE = 384
LONG, SHORT = 10**11, 17 * 10**9
TOKENS = 128
HIDDEN = 768
VMEM_LIMIT = 60 * 2**20


def dot(left, right, left_dim=1, right_dim=0):
    return lax.dot_general(
        left, right, (((left_dim,), (right_dim,)), ((), ())), preferred_element_type=F32
    )


def layer_norm(values):
    center = values - jnp.mean(values, axis=-1, keepdims=True)
    inverse = lax.rsqrt(jnp.mean(center * center, axis=-1, keepdims=True) + EPS)
    return (center * inverse, inverse)


def norm_back(grad_in, normed, inverse):
    mean_grad = jnp.mean(grad_in, axis=-1, keepdims=True)
    mean_proj = jnp.mean(grad_in * normed, axis=-1, keepdims=True)
    return inverse * (grad_in - mean_grad - normed * mean_proj)


def slope(gate):
    return gate * (1.0 - gate)


def column_sum(values):
    return jnp.sum(values.reshape(-1, values.shape[-1]), axis=0, keepdims=True)


def clear(step, *refs):
    @pl.when(step == 0)
    def _():
        for ref in refs:
            ref[...] = jnp.zeros_like(ref)


def spec(block, along=None, at=None):
    rank = len(block)
    if along is not None:
        return pl.BlockSpec(block, lambda t, core: tuple(t if a == along else 0 for a in range(rank)))
    index = (0,) * rank if at is None else at
    return pl.BlockSpec(
        block,
        lambda t, core: tuple(i(core[0]) if callable(i) else i for i in index),
        pipeline_mode=pl.Buffered(1),
    )


class Order:
    def __init__(self, place):
        self.place = place
        self.last = []


def call(name, kernel, grid, ins, outs, scratch, deps, order, flops=LONG, aliases={}):
    inputs = len(ins)
    deps = list(deps) + order.last

    def run(place_ref, *refs):
        kernel(place_ref, *refs[:inputs], *refs[inputs + len(deps) :])

    found = pl.pallas_call(
        run,
        grid_spec=pltpu.PrefetchScalarGridSpec(
            num_scalar_prefetch=1,
            grid=(grid,),
            in_specs=[s for _, s in ins] + [pl.BlockSpec(memory_space=pl.ANY)] * len(deps),
            out_specs=[s for _, _, s in outs],
            scratch_shapes=scratch,
        ),
        out_shape=[jax.ShapeDtypeStruct(shape, dtype) for shape, dtype, _ in outs],
        compiler_params=pltpu.CompilerParams(
            vmem_limit_bytes=VMEM_LIMIT, dimension_semantics=("arbitrary",)
        ),
        cost_estimate=pl.CostEstimate(flops=flops, bytes_accessed=10**6, transcendentals=0),
        name=name,
        input_output_aliases=aliases,
    )(order.place, *[a for a, _ in ins], *deps)
    order.last = [max(found, key=lambda array: array.size)]
    return found


def combine(outputs, order):
    ins, outs, plan = [], [], []
    for terms in outputs:
        if isinstance(terms, tuple):
            bit, *arrays = terms
            terms = [(array, array.shape[0], lambda place: 0) for array in arrays]
        else:
            bit = None
        array, slabs, _ = terms[0]
        shape = (slabs,) + array.shape[1:]
        rest = (0,) * (len(shape) - 1)
        plan.append((bit, list(range(len(ins), len(ins) + len(terms)))))
        for term, _, index in terms:
            ins.append(
                (term, pl.BlockSpec(shape, lambda t, place, index=index, rest=rest: (index(place),) + rest))
            )
        outs.append((shape, array.dtype, pl.BlockSpec(shape, lambda t, place, rest=rest: (0,) + rest)))

    def kernel(place, *refs):
        for (bit, sources), out_ref in zip(plan, refs[len(ins) :]):
            values = [refs[i][...] for i in sources]
            if bit is not None:
                out_ref[...] = jnp.where(place[bit] == 0, values[0], values[1])
            elif len(values) == 1:
                out_ref[...] = values[0]
            else:
                total = sum((v.astype(F32) for v in values[1:]), values[0].astype(F32))
                out_ref[...] = total.astype(out_ref.dtype)

    return call("combine", kernel, 1, ins, outs, [], [], order)


class Halving:
    def __init__(self, order, counts):
        self.order = order
        self.counts = counts

    def places(self):
        found = []
        for p in range(2 ** len(self.order)):
            dest, half = 0, 0
            for i, (axis, bit) in enumerate(self.order):
                value = (p >> (len(self.order) - 1 - i)) & 1
                if axis == "sample":
                    dest |= value << bit
                else:
                    half = value
            found.append((dest, half))
        return found

    def halves(self):
        return 2 if any(axis == "struct" for axis, _ in self.order) else 1

    def pieces(self, shape):
        rows, columns = shape
        return rows // self.counts["sample"], columns // self.halves() // PIECE

    def slabs(self, shapes):
        return (2 ** len(self.order), sum(r * c for r, c in map(self.pieces, shapes)), PIECE)

    def pack(self, out_ref, arrays, everywhere=()):
        for p, (dest, half) in enumerate(self.places()):
            held = []
            for array in arrays:
                rows, count = self.pieces(array.shape)
                for c in range(count):
                    at = (half * count + c) * PIECE
                    held.append(array[dest * rows : (dest + 1) * rows, at : at + PIECE])
            slab = jnp.concatenate(held + list(everywhere), axis=0)
            out_ref[p, : slab.shape[0]] = slab.astype(out_ref.dtype)
            if slab.shape[0] < out_ref.shape[1]:
                out_ref[p, slab.shape[0] :] = jnp.zeros(
                    (out_ref.shape[1] - slab.shape[0], PIECE), out_ref.dtype
                )

    def unpack(self, slab, shapes):
        found, at = [], 0
        for shape in shapes:
            rows, count = self.pieces(shape)
            found.append([slab[at + c * rows : at + (c + 1) * rows] for c in range(count)])
            at += rows * count
        return found

    def run(self, array, after="sum"):
        last = self.counts["sample"].bit_length() - 1

        def exchange(array, axis, bit):
            return lax.ppermute(array, axis, [(i, i ^ (1 << bit)) for i in range(self.counts[axis])])

        def halves(at, size):
            return [
                [
                    (p, size, lambda place, base=base, at=at, flip=flip: 2 * base(place) + (place[at] ^ flip))
                    for p, base in parts
                ]
                for flip in (1, 0)
            ]

        zero = lambda place: 0
        parts, size = [(array, zero)], array.shape[0]
        for axis, bit in self.order:
            at = bit if axis == "sample" else last
            size = size // 2
            if len(parts) == 1 and (axis, bit) == ("sample", 0):
                parts = [(array, lambda place: place[0]), (exchange(array, axis, bit), lambda place: place[0])]
                continue
            if len(parts) == 1:
                (sent,) = yield halves(at, size)[:1]
                parts = [(array, lambda place, at=at: place[at]), (exchange(sent, axis, bit), zero)]
            else:
                sent, kept = yield halves(at, size)
                parts = [(kept, zero), (exchange(sent, axis, bit), zero)]
        if after in ("swap", "cores"):
            sent, kept = yield halves(0, size // 2)
            return kept[0], exchange(sent, "sample", 0)[0] if after == "swap" else sent[0]
        (held,) = yield [[(p, 1, base) for p, base in parts]]
        if not after:
            return held[0]
        if self.halves() == 2:
            received = exchange(held, "struct", 0)
            first, second = yield [(last, held, received), (last, received, held)]
            return first[0], second[0]
        for bit in range(self.counts["struct"].bit_length() - 1):
            received = exchange(held, "struct", bit)
            (held,) = yield [[(p, 1, zero) for p in (held, received)]]
        return held[0]

class Running:
    def __init__(self, steps):
        self.steps = steps
        self.result = None
        self.send(None)

    def send(self, found):
        try:
            self.asked = self.steps.send(found)
        except StopIteration as stop:
            self.asked = []
            self.result = stop.value


def advance(order, *running):
    running = [r for r in running if r.result is None]
    asked = [output for r in running for output in r.asked]
    if not asked:
        return []
    made = combine(asked, order)
    at = 0
    for r in running:
        count = len(r.asked)
        r.send(made[at : at + count])
        at += count
    return made


def pair_forward_kernel(place, pair_ref, gain_ref, weight_ref, mask_ref, lengths_ref, out_ref, terms):
    gain = gain_ref[...].astype(F32)
    rows, length, channels = pair_ref.shape
    average = jnp.full((channels, channels), 1.0 / channels, BF16)
    position = lax.broadcasted_iota(jnp.int32, (1, length), 1)
    valid = (position < lengths_ref[0]) & ((mask_ref[...] == 1) | (position == 0))
    for i in range(rows):
        values = pair_ref[i]
        center = values.astype(F32) - dot(values, average)
        inverse = lax.rsqrt(jnp.mean(center * center, axis=-1, keepdims=True) + EPS)
        affine = (center * inverse * gain).astype(BF16)
        terms[i] = jnp.where(valid, dot(weight_ref[...], affine, 1, 1), MASKED)
    for h in range(terms.shape[1]):
        out_ref[h] = terms[:, h, :].astype(BF16)


def pair_forward(pair, gain, weight_t, mask, lengths, order):
    rows, length, channels = pair.shape
    heads = weight_t.shape[0]
    block = 16 if rows % 16 == 0 else rows
    return call(
        "pair_forward",
        pair_forward_kernel,
        rows // block,
        [
            (pair, spec((block, length, channels), 0)),
            (gain, spec(gain.shape)),
            (weight_t, spec(weight_t.shape)),
            (mask, spec(mask.shape)),
            (lengths, pl.BlockSpec(memory_space=pltpu.SMEM)),
        ],
        [((heads, rows, length), BF16, spec((heads, block, length), 1))],
        [pltpu.VMEM((block, heads, length), F32)],
        [],
        order,
    )[0]


def pair_backward_kernel(chunks, place, pair_ref, gain_ref, weight_ref, *refs):
    grad_refs, (out_ref, weight_grad_ref, grads) = refs[:chunks], refs[-3:]
    gain = gain_ref[...]
    channels = pair_ref.shape[2]
    average = jnp.full((channels, channels), 1.0 / channels, BF16)
    clear(pl.program_id(0), weight_grad_ref)
    head = 0
    for ref in grad_refs:
        for h in range(ref.shape[0]):
            grads[:, head, :] = ref[h].astype(F32)
            head += 1
    scaled = weight_ref[...].astype(F32) * gain
    means = jnp.broadcast_to(jnp.mean(scaled, axis=-1, keepdims=True), scaled.shape)
    full = jnp.concatenate([scaled, means], axis=1)
    high = full.astype(BF16)
    parts = jnp.concatenate([high, (full - high.astype(F32)).astype(BF16)], axis=0)

    def row(i, carry):
        values = pair_ref[i]
        center = values.astype(F32) - dot(values, average)
        inverse = lax.rsqrt(jnp.mean(center * center, axis=-1, keepdims=True) + EPS)
        normed = center * inverse
        grad = grads[i].astype(BF16)
        weight_grad_ref[...] += dot(grad, (normed * gain).astype(BF16))
        both = dot(jnp.concatenate([grad, grad], axis=0), parts, 0, 0)
        grad_normed = both[:, :channels]
        mean_proj = jnp.mean(grad_normed * normed, axis=-1, keepdims=True)
        out_ref[i] = inverse * (grad_normed - both[:, channels:] - normed * mean_proj)
        return carry

    lax.fori_loop(0, pair_ref.shape[0], row, 0, unroll=8)


def pair_backward(first, count, block, out, pair, grads, gain, weight_t, deps, order):
    rows, length, channels = pair.shape
    heads = weight_t.shape[0]
    blocked = pl.BlockSpec((block, length, channels), lambda t, place: (first + t, 0, 0))
    ins = [(pair, blocked), (gain, spec(gain.shape)), (weight_t, spec(weight_t.shape))] + [
        (g, pl.BlockSpec((g.shape[0], block, length), lambda t, place: (0, first + t, 0))) for g in grads
    ]
    aliases = {}
    if out is not None:
        aliases = {1 + len(ins): 0}
        ins.append((out, pl.BlockSpec(memory_space=pl.ANY)))
    return call(
        "pair_backward",
        functools.partial(pair_backward_kernel, len(grads)),
        count,
        ins,
        [(pair.shape, F32, blocked), ((heads, channels), F32, spec((heads, channels)))],
        [pltpu.VMEM((block, heads, length), F32)],
        deps,
        order,
        LONG,
        aliases,
    )


def conditions(cond_ref, gain_ref, cond_w_ref, cond_b_ref, zero_w_ref, zero_b_ref, zero_gate_ref, factor_ref, shift_ref):
    cond = cond_ref[...]
    width = zero_gate_ref.shape[1]
    zero_gate_ref[...] = jax.nn.sigmoid(dot(cond, zero_w_ref[...]) + zero_b_ref[...])
    cond_normed, _ = layer_norm(cond.astype(F32))
    projected = dot((cond_normed * gain_ref[...]).astype(BF16), cond_w_ref[...])
    factor_ref[...] = jax.nn.sigmoid(projected[:, :width] + cond_b_ref[...])
    shift_ref[...] = projected[:, width:]


def conditions_back(cond_ref, gain_ref, cond_w_ref, zero_w_ref, zero_grad, projected):
    cond = cond_ref[...]
    cond_normed, cond_inverse = layer_norm(cond.astype(F32))
    scaled = (cond_normed * gain_ref[...]).astype(BF16)
    grad_scaled = dot(projected, cond_w_ref[...], 1, 1)
    return (
        dot(scaled, projected, 0, 0),
        dot(cond, zero_grad, 0, 0),
        column_sum(grad_scaled * cond_normed),
        dot(zero_grad, zero_w_ref[...], 1, 1),
        grad_scaled * gain_ref[...],
        cond_normed,
        cond_inverse,
    )


def step_rows(step, tokens):
    return pl.ds(pl.multiple_of(step * tokens, tokens), tokens)


def window_start(chunk, head_dim, width):
    return min(chunk * CHUNK_HEADS * head_dim // LANES * LANES, width - WINDOW)


def inputs_kernel(
    place, acts_ref, acts_other_ref, cot_ref, cot_other_ref,
    cond_ref, gain_ref, cond_w_ref, cond_b_ref, zero_w_ref, zero_b_ref,
    query_ref, key_ref, value_ref, gate_w_ref, q_bias_ref, out_w_ref,
    input_ref, gate_ref, gated_grad_ref, q_ref, k_ref, v_ref, g_ref, qt_ref, kt_ref, vt_ref, gt_ref,
    zero_gate_ref, factor_ref, shift_ref,
):
    step = pl.program_id(0)
    samples, tokens, half = gate_ref.shape
    width = acts_ref.shape[2]
    rows = samples * tokens

    @pl.when(step == 0)
    def _():
        conditions(
            cond_ref, gain_ref, cond_w_ref, cond_b_ref, zero_w_ref, zero_b_ref, zero_gate_ref, factor_ref, shift_ref
        )

    here = step_rows(step, tokens)
    acts = jnp.concatenate([acts_ref[...], acts_other_ref[...]], axis=0)
    normed, _ = layer_norm(acts.astype(F32))
    first = (factor_ref[here, :][None] * normed + shift_ref[here, :][None]).astype(BF16)
    input_ref[...] = first
    first = first.reshape(rows, width)
    cot = jnp.concatenate([cot_ref[...], cot_other_ref[...]], axis=0)
    grad_att = (cot.astype(F32) * zero_gate_ref[here, :][None]).astype(BF16)
    grad_gated = dot(grad_att.reshape(rows, width), out_w_ref[...], 1, 1)
    gated_grad_ref[...] = grad_gated.reshape(samples, tokens, half)
    gate = jax.nn.sigmoid(dot(first, gate_w_ref[...]))
    gate_ref[...] = gate.reshape(samples, tokens, half)

    def put(values, nat_ref, t_ref):
        low = values.astype(BF16).reshape(samples, tokens, half)
        for window in range(nat_ref.shape[0]):
            nat_ref[window] = low[:, :, window * LANES : window * LANES + WINDOW]
        for s in range(samples):
            t_ref[s] = low[s].T

    put(grad_gated * gate, g_ref, gt_ref)
    put(dot(first, query_ref[...]) + q_bias_ref[...], q_ref, qt_ref)
    put(dot(first, key_ref[...]), k_ref, kt_ref)
    put(dot(first, value_ref[...]), v_ref, vt_ref)


def own(core):
    return core


def other(core):
    return 1 - core


def quarters(weight, whose):
    rows, columns = weight.shape
    return [
        (weight, spec((rows, columns // 8), at=(0, functools.partial(lambda j, core: 2 * j + whose(core), j))))
        for j in range(4)
    ]


def inputs_call(acts, acts_other, cot, cot_other, cond, branch, qkvg_w, q_bias, out_w, deps, order):
    own_samples, length, width = acts.shape
    samples, half = 2 * own_samples, width // 2
    windows = (half - WINDOW) // LANES + 1
    block = spec((own_samples, TOKENS, width), 1)
    wide = spec((samples, TOKENS, width), 1)
    narrow = spec((samples, TOKENS, half), 1)
    nat = spec((windows, samples, TOKENS, WINDOW), 2)
    turned = spec((samples, half, TOKENS), 2)
    return call(
        "inputs",
        inputs_kernel,
        length // TOKENS,
        [(a, block) for a in (acts, acts_other, cot, cot_other)]
        + [(cond, spec(cond.shape))]
        + branch
        + quarters(qkvg_w, own)
        + [(q_bias, spec((1, half), at=(0, own))), (out_w, spec((half, width), at=(own, 0)))],
        [
            ((samples, length, width), BF16, wide),
            ((samples, length, half), F32, narrow),
            ((samples, length, half), F32, narrow),
        ]
        + [((windows, samples, length, WINDOW), BF16, nat)] * 4
        + [((samples, half, length), BF16, turned)] * 4
        + [((length, width), F32, spec((length, width)))] * 2,
        [pltpu.VMEM((length, width), F32)],
        deps,
        order,
    )


def transition_kernel(
    halving, place, acts_ref, cot_ref, cond_ref, gain_ref, cond_w_ref, cond_b_ref, zero_w_ref, zero_b_ref,
    swiglu_ref, down_ref,
    partial_ref, acts_grad_ref, cond_gate_ref, cond_norm_ref, packed_out, cond_b_out, zero_b_out, gain_out,
    swiglu_acc, down_acc, zero_gate_ref, factor_ref, shift_ref, zero_low, projected,
):
    step = pl.program_id(0)
    clear(step, swiglu_acc, down_acc, cond_b_out, zero_b_out)
    samples, tokens, width = acts_ref.shape
    rows = samples * tokens
    hidden_width = down_ref.shape[0]

    @pl.when(step == 0)
    def _():
        conditions(
            cond_ref, gain_ref, cond_w_ref, cond_b_ref, zero_w_ref, zero_b_ref, zero_gate_ref, factor_ref, shift_ref
        )

    here = step_rows(step, tokens)
    zero_gate = zero_gate_ref[here, :]
    factor = factor_ref[here, :]
    acts = acts_ref[...].astype(F32)
    normed, _ = layer_norm(acts)
    second = (factor[None] * normed + shift_ref[here, :][None]).astype(BF16).reshape(rows, width)
    grad_out = cot_ref[...].astype(F32)
    grad_tr = (grad_out * zero_gate[None]).astype(BF16).reshape(rows, width)
    transition = grad_input = 0.0
    second_t = second.T
    for at in range(0, hidden_width, HIDDEN):
        gate_at, up_at = slice(at, at + HIDDEN), slice(hidden_width + at, hidden_width + at + HIDDEN)
        gate_part = dot(second, swiglu_ref[:, gate_at])
        up_part = dot(second, swiglu_ref[:, up_at])
        gate_sig = jax.nn.sigmoid(gate_part)
        silu = gate_part * gate_sig
        product = (silu * up_part).astype(BF16)
        transition += dot(product, down_ref[gate_at, :])
        grad_product = dot(grad_tr, down_ref[gate_at, :], 1, 1)
        down_acc[gate_at, :] += dot(product, grad_tr, 0, 0)
        grad_up = (grad_product * silu).astype(BF16)
        grad_gate = (grad_product * up_part * gate_sig * (1.0 + gate_part * (1.0 - gate_sig))).astype(BF16)
        swiglu_acc[:, gate_at] += dot(second_t, grad_gate)
        swiglu_acc[:, up_at] += dot(second_t, grad_up)
        grad_input += dot(grad_gate, swiglu_ref[:, gate_at], 1, 1)
        grad_input += dot(grad_up, swiglu_ref[:, up_at], 1, 1)
    transition = transition.reshape(samples, tokens, width)
    grad_input = grad_input.reshape(samples, tokens, width)
    partial_ref[...] = acts + zero_gate[None] * transition
    grad_zero = jnp.sum(grad_out * transition, axis=0) * slope(zero_gate)
    zero_b_out[...] += column_sum(grad_zero)
    zero_low[here, :] = grad_zero.astype(BF16)
    grad_factor = jnp.sum(grad_input * normed, axis=0) * slope(factor)
    cond_b_out[...] += column_sum(grad_factor)
    projected[here, :width] = grad_factor.astype(BF16)
    projected[here, width:] = jnp.sum(grad_input, axis=0).astype(BF16)
    acts_grad_ref[...] = grad_input * factor[None]

    @pl.when(step == pl.num_programs(0) - 1)
    def _():
        cond_w_grad, zero_w_grad, gain_grad, cond_gate, cond_norm, _, _ = conditions_back(
            cond_ref, gain_ref, cond_w_ref, zero_w_ref, zero_low[...], projected[...]
        )
        gain_out[...] = gain_grad
        cond_gate_ref[...] = cond_gate
        cond_norm_ref[...] = cond_norm
        halving.pack(packed_out, [swiglu_acc, down_acc, cond_w_grad, zero_w_grad])


def transition_call(acts, cot, cond, branch, swiglu, down, halving, deps, order):
    samples, length, width = acts.shape
    cond_width = cond.shape[1]
    hidden = down.shape[0]
    rows = samples * length
    block = spec((samples, TOKENS, width), 1)
    weights = [(width, 2 * hidden), (hidden, width), (cond_width, 2 * width), (cond_width, width)]
    vectors = [(1, width), (1, width), (1, cond_width)]
    results = call(
        "transition",
        functools.partial(transition_kernel, halving),
        length // TOKENS,
        [(acts, block), (cot, block), (cond, spec(cond.shape))]
        + branch
        + [(swiglu, spec(swiglu.shape)), (down, spec(down.shape))],
        [(acts.shape, F32, block)] * 2
        + [(cond.shape, F32, spec(cond.shape))] * 2
        + [(halving.slabs(weights), BF16, spec(halving.slabs(weights)))]
        + [(s, F32, spec(s)) for s in vectors],
        [pltpu.VMEM(s, F32) for s in weights[:2]]
        + [pltpu.VMEM((length, width), F32)] * 3
        + [pltpu.VMEM((length, width), BF16), pltpu.VMEM((length, 2 * width), BF16)],
        deps,
        order,
    )
    return results, weights


def attention_kernel(
    halving, head_dim, first_lane, place, q_ref, k_ref, v_ref, g_ref, qt_ref, kt_ref, vt_ref, gt_ref, bias_ref,
    mixed_ref, dq_ref, dkt_ref, dvt_ref, db_ref, kz, vz, plow, dslow, dsum,
):
    h = pl.program_id(0)
    samples, length, wide = q_ref.shape
    scale = head_dim ** (-0.5)
    off = pl.multiple_of(first_lane + h * head_dim, 16)
    lane = lax.broadcasted_iota(jnp.int32, (1, wide), 1)
    mask = ((lane >= off) & (lane < off + head_dim)).astype(BF16)

    @pl.when(h == 0)
    def _():
        mixed_ref[...] = jnp.zeros_like(mixed_ref)
        dq_ref[...] = jnp.zeros_like(dq_ref)

    kz[...] = jnp.zeros_like(kz)
    vz[...] = jnp.zeros_like(vz)
    for s in range(samples):
        kz[s, pl.ds(off, head_dim), :] = kt_ref[s]
        vz[s, pl.ds(off, head_dim), :] = vt_ref[s]
    parts, _, share, _ = bias_ref.shape
    if share % 16 == 0:
        bias = bias_ref[:, 0].reshape(length, length).astype(F32)
    else:
        bias = jnp.concatenate([bias_ref[p, 0].astype(F32) for p in range(parts)], axis=0)
    for s in range(samples):
        x = dot(q_ref[s], kz[s]) * scale + bias
        x = jnp.exp(x - jnp.max(x, axis=-1, keepdims=True))
        probs = x * (1.0 / jnp.sum(x, axis=-1, keepdims=True))
        low = probs.astype(BF16)
        plow[...] = low
        mixed = dot(low, v_ref[s] * mask)
        mixed_ref[s] += mixed
        grad = g_ref[s]
        delta = jnp.sum(grad.astype(F32) * mixed, axis=-1, keepdims=True)
        grad_scores = probs * (dot(grad, vz[s]) - delta)
        grad_low = (grad_scores * scale).astype(BF16)
        dslow[...] = grad_low
        total = grad_scores if s == 0 else dsum[...] + grad_scores
        if s < samples - 1:
            dsum[...] = total
        else:
            for p, (dest, _) in enumerate(halving.places()):
                for c in range(2):
                    at = (dest + c) * share
                    db_ref[2 * p + c, 0] = total[at : at + share].astype(BF16)
        dq_ref[s] += dot(grad_low, k_ref[s] * mask)
        dvt_ref[s] = dot(gt_ref[s], plow[...]).astype(BF16)
        dkt_ref[s] = dot(qt_ref[s], dslow[...]).astype(BF16)


def attention_call(chunk, nats, turned, bias, head_dim, halving, deps, order):
    _, samples, length, wide = nats[0].shape
    half = turned[0].shape[1]
    parts, heads, share, _ = bias.shape
    start = window_start(chunk, head_dim, half)
    nat = pl.BlockSpec((None, samples, length, wide), lambda h, core: (start // LANES, 0, 0, 0))
    turn = pl.BlockSpec((samples, head_dim, length), lambda h, core: (0, chunk * CHUNK_HEADS + h, 0))
    turn_out = pl.BlockSpec((samples, head_dim, length), lambda h, core: (0, h, 0))
    bias_in = pl.BlockSpec(
        (parts, 1, share, length), lambda h, core: (0, core[0] * (heads // 2) + chunk * CHUNK_HEADS + h, 0, 0)
    )
    bias_out = pl.BlockSpec((parts, 1, share, length), lambda h, core: (0, h, 0, 0))
    held = pl.BlockSpec((samples, length, wide), lambda h, core: (0, 0, 0))
    return call(
        "attention",
        functools.partial(attention_kernel, halving, head_dim, chunk * CHUNK_HEADS * head_dim - start),
        CHUNK_HEADS,
        [(a, nat) for a in nats] + [(a, turn) for a in turned] + [(bias, bias_in)],
        [((samples, length, wide), F32, held)] * 2
        + [((samples, CHUNK_HEADS * head_dim, length), BF16, turn_out)] * 2
        + [((parts, CHUNK_HEADS, share, length), BF16, bias_out)],
        [
            pltpu.VMEM((samples, wide, length), BF16),
            pltpu.VMEM((samples, wide, length), BF16),
            pltpu.VMEM((length, length), BF16),
            pltpu.VMEM((length, length), BF16),
            pltpu.VMEM((length, length), F32),
        ],
        deps,
        order,
        SHORT,
    )


def mixed_kernel(head_dim, chunks, place, *refs):
    (gate_ref, gated_grad_ref), refs = refs[:2], refs[2:]
    mixed_refs, refs = refs[:chunks], refs[chunks:]
    dq_refs, refs = refs[:chunks], refs[chunks:]
    dkt_refs, refs = refs[:chunks], refs[chunks:]
    dvt_refs, refs = refs[:chunks], refs[chunks:]
    gated_refs, joined_refs, q_bias_out = refs[:2], refs[2:4], refs[4]
    clear(pl.program_id(0), q_bias_out)
    samples, tokens, half = gate_ref.shape
    own_samples = samples // 2

    def join(window_refs):
        pieces = []
        for tile in range(half // LANES):
            held = [
                ref[:, :, tile * LANES - start : (tile + 1) * LANES - start]
                for chunk, ref in enumerate(window_refs)
                for start in [window_start(chunk, head_dim, half)]
                if start <= tile * LANES < start + WINDOW
            ]
            pieces.append(functools.reduce(jnp.add, held))
        return jnp.concatenate(pieces, axis=-1)

    def turn(turned_refs):
        joined = jnp.concatenate([ref[...] for ref in turned_refs], axis=1)
        return jnp.stack([joined[s].T for s in range(samples)], axis=0)

    mixed = join(mixed_refs)
    gate = gate_ref[...]
    gated = (gate * mixed).astype(BF16)
    grad_queries = join(dq_refs)
    q_bias_out[...] += column_sum(grad_queries)
    grad_gate = gated_grad_ref[...] * mixed * slope(gate)
    parts = [grad_queries.astype(BF16), turn(dkt_refs), turn(dvt_refs), grad_gate.astype(BF16)]
    for i in range(2):
        here = slice(i * own_samples, (i + 1) * own_samples)
        gated_refs[i][...] = gated[here]
        for j, part in enumerate(parts):
            joined_refs[i][:, :, j * half : (j + 1) * half] = part[here]


def mixed_call(gate, gated_grad, mixeds, dqs, dkts, dvts, head_dim, deps, order):
    samples, length, half = gate.shape
    chunks = len(mixeds)
    own_samples = samples // 2
    block = spec((samples, TOKENS, half), 1)
    window = spec((samples, TOKENS, WINDOW), 1)
    turned = spec((samples, half // chunks, TOKENS), 2)
    return call(
        "mixed",
        functools.partial(mixed_kernel, head_dim, chunks),
        length // TOKENS,
        [(a, block) for a in (gate, gated_grad)]
        + [(a, window) for a in mixeds + dqs]
        + [(a, turned) for a in dkts + dvts],
        [((own_samples, length, half), BF16, spec((own_samples, TOKENS, half), 1))] * 2
        + [((own_samples, length, 4 * half), BF16, spec((own_samples, TOKENS, 4 * half), 1))] * 2
        + [((1, half), F32, spec((1, half)))],
        [],
        deps,
        order,
    )


def qkvg_kernel(halving, place, first_ref, joined_ref, joined_other_ref, packed_out):
    step = pl.program_id(0)
    samples, length, width = first_ref.shape
    rows = samples * length // 2
    half = joined_ref.shape[2]
    grad = dot(first_ref[: samples // 2].reshape(rows, width), joined_ref[...].reshape(rows, half), 0, 0)
    grad += dot(first_ref[samples // 2 :].reshape(rows, width), joined_other_ref[...].reshape(rows, half), 0, 0)
    share = packed_out.shape[1] * halving.halves() // 4

    for block in range(4):

        @pl.when(step == block)
        def _():
            for p, (dest, part) in enumerate(halving.places()):
                piece = block - part * (4 // halving.halves())
                if 0 <= piece < 4 // halving.halves():
                    for c in range(2):
                        at = (dest + c) * share
                        packed_out[2 * p + c, piece * share : (piece + 1) * share] = grad[at : at + share].astype(BF16)


def qkvg_call(first, joined, joined_other, halving, deps, order):
    samples, length, width = first.shape
    half = joined.shape[2] // 4
    share = width // halving.counts["sample"]
    slabs = (2 * 2 ** len(halving.order), 4 // halving.halves() * share, half)
    block = spec((samples // 2, length, half), 2)
    (packed,) = call(
        "qkvg_grad",
        functools.partial(qkvg_kernel, halving),
        4,
        [(first, spec(first.shape)), (joined, block), (joined_other, block)],
        [(slabs, BF16, spec(slabs))],
        [],
        deps,
        order,
    )
    return packed


def outputs_kernel(place, acts_ref, cot_ref, partial_ref, acts_part_ref, zero_gate_ref, factor_ref, *refs):
    gated_refs, joined_refs, refs = refs[:2], refs[2:4], refs[4:]
    out_w_refs, qkvg_refs, refs = refs[:2], (refs[2:6], refs[6:10]), refs[10:]
    block_ref, acts_grad_ref, projected_ref, zero_low_ref, cond_b_out, zero_b_out, out_out = refs
    clear(pl.program_id(0), cond_b_out, zero_b_out, out_out)
    samples, tokens, width = acts_ref.shape
    rows = samples * tokens
    half = width // 2
    zero_gate = zero_gate_ref[...]
    factor = factor_ref[...]
    normed, inverse = layer_norm(acts_ref[...].astype(F32))
    grad_out = cot_ref[...].astype(F32)
    grad_att = (grad_out * zero_gate[None]).astype(BF16).reshape(rows, width)
    attended = grad_input = 0.0
    for i, half_at in enumerate((place[0], 1 - place[0])):
        gated = gated_refs[i][...].reshape(rows, half)
        attended += dot(gated, out_w_refs[i][...])
        out_out[pl.ds(pl.multiple_of(half_at * half, half), half), :] += dot(gated, grad_att, 0, 0)
        for j in range(4):
            grad_input += dot(
                joined_refs[i][:, :, j * half : (j + 1) * half].reshape(rows, half), qkvg_refs[i][j][...], 1, 1
            )
    attended = attended.reshape(samples, tokens, width)
    grad_input = grad_input.reshape(samples, tokens, width)
    block_ref[...] = (partial_ref[...] + zero_gate[None] * attended).astype(BF16)
    grad_zero = jnp.sum(grad_out * attended, axis=0) * slope(zero_gate)
    zero_b_out[...] += column_sum(grad_zero)
    zero_low_ref[...] = grad_zero.astype(BF16)
    grad_factor = jnp.sum(grad_input * normed, axis=0) * slope(factor)
    cond_b_out[...] += column_sum(grad_factor)
    projected_ref[:, :width] = grad_factor.astype(BF16)
    projected_ref[:, width:] = jnp.sum(grad_input, axis=0).astype(BF16)
    acts_grad_ref[...] = (
        grad_out + norm_back(grad_input * factor[None] + acts_part_ref[...], normed, inverse)
    ).astype(BF16)


def outputs_call(acts, cot, partial, acts_part, zero_gate, factor, gateds, joineds, out_w, qkvg_w, deps, order):
    samples, length, width = acts.shape
    half = width // 2
    block = spec((samples, TOKENS, width), 1)
    tokens = spec((TOKENS, width), 0)
    return call(
        "outputs",
        outputs_kernel,
        length // TOKENS,
        [(a, block) for a in (acts, cot, partial, acts_part)]
        + [(zero_gate, tokens), (factor, tokens)]
        + [(a, spec((samples, TOKENS, half), 1)) for a in gateds]
        + [(a, spec((samples, TOKENS, 4 * half), 1)) for a in joineds]
        + [(out_w, spec((half, width), at=(whose, 0))) for whose in (own, other)]
        + quarters(qkvg_w, own)
        + quarters(qkvg_w, other),
        [
            (acts.shape, BF16, block),
            (acts.shape, BF16, block),
            ((length, 2 * width), BF16, spec((TOKENS, 2 * width), 0)),
            ((length, width), BF16, tokens),
        ]
        + [(s, F32, spec(s)) for s in ((1, width), (1, width), (width, width))],
        [],
        deps,
        order,
    )


def conditions_kernel(
    rest, vector_parts, place, cond_ref, gain_ref, cond_w_ref, zero_w_ref, zero_low_ref, projected_ref,
    cond_gate_in, cond_norm_in, out_w_grad_ref, *refs
):
    vector_refs, (packed_out,) = refs[:vector_parts], refs[vector_parts:]
    cond_w_grad, zero_w_grad, gain_grad, cond_gate, cond_norm, cond_normed, cond_inverse = conditions_back(
        cond_ref, gain_ref, cond_w_ref, zero_w_ref, zero_low_ref[...], projected_ref[...]
    )
    cond_grad = (
        cond_gate + cond_gate_in[...] + norm_back(cond_norm + cond_norm_in[...], cond_normed, cond_inverse)
    )
    vectors = [gain_grad] + [ref[...] for ref in vector_refs[:-1]]
    q_bias = vector_refs[-1][...]
    vectors += [jnp.where(place[0] == 0, q_bias, 0.0), jnp.where(place[0] == 1, q_bias, 0.0)]
    pieces = [v[:, at : at + PIECE] for v in vectors for at in range(0, v.shape[1], PIECE)]
    rest.pack(packed_out, [out_w_grad_ref[...], cond_w_grad, zero_w_grad, cond_grad], pieces)


def conditions_call(cond, branch, zero_w, zero_low, projected, cond_gate, cond_norm, out_w_grad, vectors, rest, deps, order):
    cond_width = cond.shape[1]
    width = zero_low.shape[1]
    weights = [out_w_grad.shape, (cond_width, 2 * width), (cond_width, width), cond.shape]
    count, rows, columns = rest.slabs(weights)
    rows += (sum(v.shape[1] for v in vectors) + cond_width + width // 2) // PIECE
    rows += -rows % 16
    fixed = (zero_low, projected, cond_gate, cond_norm, out_w_grad, *vectors)
    (packed,) = call(
        "conditions",
        functools.partial(conditions_kernel, rest, len(vectors)),
        1,
        [(cond, spec(cond.shape))] + branch[:2] + [zero_w] + [(a, spec(a.shape)) for a in fixed],
        [((count, rows, columns), BF16, spec((count, rows, columns)))],
        [],
        deps,
        order,
    )
    return packed, weights


def results_kernel(
    early_halving, rest_halving, early_shapes, rest_shapes, halves, place, *refs
):
    early_refs, refs = refs[:halves], refs[halves:]
    qkvg_refs, refs = refs[: 2 * halves], refs[2 * halves :]
    (rest_ref, rest_got_ref, pair_sum_ref, pair_wt_ref, pair_gain_ref), refs = refs[:5], refs[5:]
    (cond_ref, cond_w_ref, zero_w_ref, qkvg_ref, out_w_ref, swiglu_ref, down_ref), refs = refs[:7], refs[7:]
    gains_ref, cond_b_ref, zero_b_ref, q_bias_ref, pair_gain_out, pair_w_out = refs
    bits = place.shape[0] - 1
    device = sum(place[bit] << bit for bit in range(bits))

    def columns(ref, pieces):
        for c, piece in enumerate(pieces):
            ref[:, c * PIECE : (c + 1) * PIECE] = piece.astype(F32)

    early = [early_halving.unpack(ref[...].astype(F32), early_shapes) for ref in early_refs]
    swiglu, down, cond_w_one, zero_w_one = [sum(parts, []) for parts in zip(*early)]
    before = rest_ref[...].astype(F32)
    total = before + rest_got_ref[...].astype(F32)
    out_w, cond_w_zero, zero_w_zero, _ = rest_halving.unpack(total, rest_shapes)
    columns(swiglu_ref, swiglu)
    columns(down_ref, down)
    columns(cond_w_ref, cond_w_zero + cond_w_one)
    columns(zero_w_ref, zero_w_zero + zero_w_one)
    columns(out_w_ref, out_w)
    columns(cond_ref, rest_halving.unpack(before, rest_shapes)[3])
    parts = []
    for i in range(2):
        held = [ref[...].astype(F32) for ref in qkvg_refs[i * halves : (i + 1) * halves]]
        if halves == 2:
            first = place[bits] == 0
            held = [jnp.where(first, held[0], held[1]), jnp.where(first, held[1], held[0])]
        parts.append(jnp.concatenate(held, axis=0))
    first = place[0] == 0
    parts = [jnp.where(first, parts[0], parts[1]), jnp.where(first, parts[1], parts[0])]
    rows = parts[0].shape[0] // 4
    columns(qkvg_ref, [part[j * rows : (j + 1) * rows] for j in range(4) for part in parts])
    at = sum(r * c for r, c in map(rest_halving.pieces, rest_shapes))
    for ref in (gains_ref, cond_b_ref, zero_b_ref, q_bias_ref):
        size = ref.shape[1]
        count = size * rest_halving.counts["sample"] // PIECE
        value = 0.0
        for c in range(count):
            source = lax.broadcasted_iota(jnp.int32, (PIECE, size), 0) + c * PIECE
            target = lax.broadcasted_iota(jnp.int32, (PIECE, size), 1) + device * size
            chosen = (source == target).astype(F32)
            value += lax.dot_general(
                total[at + c : at + c + 1],
                chosen,
                (((1,), (0,)), ((), ())),
                precision=lax.Precision.HIGHEST,
                preferred_element_type=F32,
            )
        ref[...] = value
        at += count
    size, heads = pair_w_out.shape
    channels = pair_sum_ref.shape[1]
    source = lax.broadcasted_iota(jnp.int32, (channels, size), 0)
    target = lax.broadcasted_iota(jnp.int32, (channels, size), 1) + device * size
    chosen = (source == target).astype(F32)

    def choose(array):
        return lax.dot_general(
            chosen,
            array,
            (((0,), (1,)), ((), ())),
            precision=lax.Precision.HIGHEST,
            preferred_element_type=F32,
        )

    grad = choose(pair_sum_ref[...])
    pair_w_out[...] = grad
    weighted = jnp.sum(grad * choose(pair_wt_ref[...].astype(F32)), axis=1, keepdims=True)
    pair_gain_out[...] = weighted / choose(pair_gain_ref[...])


def results_call(
    early, early_halving, early_shapes, qkvg, rest, rest_got, rest_halving, rest_shapes, pair_sum, pair_wt, pair_gain, order
):
    count = rest_halving.counts["sample"]
    heads, channels = pair_wt.shape
    swiglu, down, cond_w, zero_w = early_shapes
    out_w, _, _, cond = rest_shapes
    width = out_w[1]
    arrays = [cond, (cond_w[0], 2 * cond_w[1]), (zero_w[0], 2 * zero_w[1]), (width, 4 * width), out_w, swiglu, down]
    shapes = [(rows // count, columns) for rows, columns in arrays]
    shapes += [(1, size // count) for size in (2 * cond[1], 2 * width, 2 * width, width)]
    shapes += [(channels // count, 1), (channels // count, heads)]
    ins = [*early, *qkvg, rest, rest_got, pair_sum, pair_wt, pair_gain]
    return call(
        "results",
        functools.partial(
            results_kernel, early_halving, rest_halving, early_shapes, rest_shapes, early_halving.halves()
        ),
        1,
        [(a, spec(a.shape)) for a in ins],
        [(shape, F32, spec(shape)) for shape in shapes],
        [],
        [],
        order,
    )


def body(
    struct_count, sample_devices,
    acts, cond, pair, lengths, token_mask, cond_gains, cond_w, cond_bias, output_gate_weights, zero_bias,
    qkvg_w, q_bias, out_w, swiglu_w, down_w, pair_gain, pair_w, cotangent,
):
    acts, cond, pair, cotangent = acts[0], cond[0], pair[0], cotangent[0]
    samples, length, width = acts.shape
    cond_width = cond.shape[1]
    heads = pair_w.shape[1]
    head_dim = width // heads
    chunks = heads // 2 // CHUNK_HEADS
    counts = {"struct": struct_count, "sample": sample_devices}
    bits = sample_devices.bit_length() - 1
    pair_wt = pair_w.T
    device = lax.axis_index("sample")
    core = device & 1
    place = [(device >> bit) & 1 for bit in range(bits)] + [lax.axis_index("struct")]
    order = Order(jnp.stack(place).astype(jnp.int32))

    def swap(array):
        return lax.ppermute(array, "sample", [(i, i ^ 1) for i in range(sample_devices)])

    acts_other, cotangent_other = swap(acts), swap(cotangent)

    bias_rows = pair_forward(pair, pair_gain[None], pair_wt, token_mask, lengths, Order(jnp.zeros(bits + 1, jnp.int32)))
    bias = lax.all_gather(bias_rows, "sample", axis=0, tiled=False)

    rows = {}
    at = 0
    packed = [
        ("gain", cond_gains), ("cond_b", cond_bias), ("zero_b", zero_bias), ("q_bias", q_bias), ("pair", pair_gain)
    ]
    vector = jnp.concatenate([v for _, v in packed]).astype(F32)[None]
    for name, v in packed:
        rows[name] = vector[:, at : at + v.shape[0]]
        at += v.shape[0]

    def conditioning(b):
        return [
            (rows["gain"], spec((1, cond_width), at=(0, b))),
            (cond_w, spec((cond_width, 2 * width), at=(0, b))),
            (rows["cond_b"], spec((1, width), at=(0, b))),
        ]

    def zero(b):
        return [
            (output_gate_weights, spec((cond_width, width), at=(0, b))),
            (rows["zero_b"], spec((1, width), at=(0, b))),
        ]

    def path(*order):
        steps = [("struct", 0) if o == "y" else ("sample", o) for o in order]
        steps = [s for s in steps if s[0] == "sample" or struct_count == 2]
        return Halving(steps + [("sample", b) for b in range(4, bits)], counts)

    along_x = path(0, 1, 2, 3)
    along_y = path(0, "y", 2, 3, 1)
    chip_x = path(1, 2, 3)
    chip_y = path("y", 2, 3, 1)
    results, early_shapes = transition_call(
        acts, cotangent, cond, conditioning(1) + zero(1), swiglu_w, down_w, along_y, [], order
    )
    partial, acts_part, cond_gate, cond_norm, early, cond_b_one, zero_b_one, gain_one = results
    early = Running(along_y.run(early))
    first, gate, gated_grad, *rest = inputs_call(
        acts, acts_other, cotangent, cotangent_other, cond, conditioning(0) + zero(0), qkvg_w, rows["q_bias"], out_w,
        [], order,
    )
    nats, turned, (zero_gate, factor) = rest[:4], rest[4:8], rest[8:]

    mixeds, dqs, dkts, dvts, bias_sums = [], [], [], [], []
    deps = advance(order, early)
    for chunk in range(chunks):
        mixed, dq, dkt, dvt, db = attention_call(chunk, nats, turned, bias, head_dim, chip_x, deps, order)
        mixeds.append(mixed)
        dqs.append(dq)
        dkts.append(dkt)
        dvts.append(dvt)
        bias_sums.append(Running(chip_x.run(db, "swap")))
        deps = advance(order, *bias_sums, *([early] if chunk % 2 else []))

    gated, gated_sent, joined, joined_sent, q_bias_grad = mixed_call(
        gate, gated_grad, mixeds, dqs, dkts, dvts, head_dim, deps, order
    )
    gated_got, joined_got = swap(gated_sent), swap(joined_sent)
    deps = advance(order, *bias_sums)
    qkvg_sum = Running(
        chip_y.run(qkvg_call(first, joined, joined_sent, chip_y, deps, order), "cores")
    )
    deps = advance(order, *bias_sums, qkvg_sum, early)
    block_out, acts_grad, projected, zero_low, cond_b_zero, zero_b_zero, out_grad = outputs_call(
        acts, cotangent, partial, acts_part, zero_gate, factor, [gated, gated_got], [joined, joined_got],
        out_w, qkvg_w, deps, order,
    )
    deps = advance(order, *bias_sums, qkvg_sum)
    while any(b.result is None for b in bias_sums):
        deps += advance(order, *bias_sums)
    rest, rest_shapes = conditions_call(
        cond, conditioning(0), zero(0)[0], zero_low, projected, cond_gate, cond_norm, out_grad,
        [gain_one, cond_b_zero, cond_b_one, zero_b_zero, zero_b_one, q_bias_grad], along_x, deps, order,
    )
    rest = Running(along_x.run(rest, ""))
    share = length // sample_devices
    block = 16 if share % 16 == 0 else share
    turned_wt = jnp.where(core == 0, pair_wt, jnp.roll(pair_wt, heads // 2, axis=0))
    grads = [b.result[0] for b in bias_sums] + [b.result[1] for b in bias_sums]
    grad_pair, part = pair_backward(0, 1, block, None, pair, grads, rows["pair"], turned_wt, [], order)
    pair_parts = [part]
    if share > block:
        deps = advance(order, qkvg_sum, rest, early)
        grad_pair, part = pair_backward(
            1, share // block - 1, block, grad_pair, pair, grads, rows["pair"], turned_wt, deps, order
        )
        pair_parts.append(part)
    struct_bits = struct_count.bit_length() - 1

    def summed(array, *masks):
        found = [
            lax.ppermute(array, ("struct", "sample"), [(i, i ^ mask) for i in range(struct_count * sample_devices)])
            for mask in masks
        ]
        if len(found) == 1:
            return array + found[0]
        return (array + found[0]) + (found[1] + found[2])

    class Pair:
        asked = [[(p, p.shape[0], lambda place: 0) for p in pair_parts]]
        result = None

        def send(self, found):
            self.result = found[0]

    pair_grad = Pair()
    advance(order, pair_grad, qkvg_sum, rest, early)
    left = [bits + struct_bits - 1] + list(range(bits + struct_bits - 1)) if struct_bits else list(range(bits))
    pair_sum = pair_grad.result
    pair_sum = jnp.where(core == 0, pair_sum, jnp.roll(pair_sum, heads // 2, axis=0))
    while left:
        one = 1 << left.pop(0)
        two = 1 << left.pop(0) if left else 0
        pair_sum = summed(pair_sum, one, two, one | two) if two else summed(pair_sum, one)
    chains = (qkvg_sum, rest, early)
    while any(r.result is None for r in chains):
        advance(order, *chains)
    mine_qkvg, sent = qkvg_sum.result
    if chip_y.halves() == 2:
        across = [
            (s * sample_devices + i, (1 - s) * sample_devices + (i ^ 1))
            for s in range(2)
            for i in range(sample_devices)
        ]
        from_y = lax.ppermute(mine_qkvg, "struct", [(0, 1), (1, 0)])
        from_both = lax.ppermute(sent, ("struct", "sample"), across)
        qkvg = [mine_qkvg, from_y, swap(sent), from_both]
    else:
        for bit in range(struct_bits):
            mine_qkvg, sent = [summed(part, 1 << (bits + bit)) for part in (mine_qkvg, sent)]
        qkvg = [mine_qkvg, swap(sent)]
    early = list(early.result) if along_y.halves() == 2 else [early.result]
    rest_sum, rest_got = rest.result, jnp.zeros_like(rest.result)
    for bit in range(struct_bits):
        if bit:
            rest_sum = rest_sum + rest_got
        rest_got = lax.ppermute(
            rest_sum, "struct", [(i, i ^ (1 << bit)) for i in range(struct_count)]
        )
    (cond_sum, cond_w_sum, zero_w_sum, qkvg_total, out_sum, swiglu_sum, down_sum,
     gains, cond_b, zero_b, q_b, pair_g, pair_w_sum) = results_call(
        early, along_y, early_shapes, qkvg, rest_sum, rest_got, along_x, rest_shapes, pair_sum, pair_wt, rows["pair"], order
    )
    if struct_bits > 1:
        cond_sum = along_x.unpack(rest.result, rest_shapes)[3][0].astype(F32)
    return (
        block_out[None], acts_grad[None], cond_sum[None], grad_pair[None], gains[0], cond_w_sum, cond_b[0], zero_w_sum,
        zero_b[0], qkvg_total, q_b[0], out_sum, swiglu_sum, down_sum, pair_g[:, 0], pair_w_sum,
    )


def solution(mesh):
    per_struct = P("struct", "sample", None, None)
    in_specs = (
        (per_struct, P("struct", None, None), per_struct, P("struct"), P("struct", None))
        + (P(),) * 12
        + (per_struct,)
    )
    one, two = P("sample"), P("sample", None)
    out_specs = (
        per_struct, per_struct, P("struct", "sample", None), per_struct,
        one, two, one, two, one, two, one, two, two, two, one, two,
    )
    local = functools.partial(body, mesh.shape["struct"], mesh.shape["sample"])
    return jax.shard_map(local, mesh=mesh, in_specs=in_specs, out_specs=out_specs, check_vma=False)
```

```python
import functools

import jax
import jax.numpy as jnp
from jax import lax
from jax.experimental import pallas as pl
from jax.experimental.pallas import tpu as pltpu
from jax.sharding import PartitionSpec as P

EPS = 1e-05
MASKED = -1000000000.0
F32 = jnp.float32
BF16 = jnp.bfloat16
CHUNK_HEADS = 2
LANES = 128
PIECE = 384
LONG, SHORT = 10**11, 17 * 10**9
TOKENS = 128
HIDDEN = 768
VMEM_LIMIT = 63 * 2**20


def dot(left, right, left_dim=1, right_dim=0):
    return lax.dot_general(
        left, right, (((left_dim,), (right_dim,)), ((), ())), preferred_element_type=F32
    )


def layer_norm(values):
    center = values - jnp.mean(values, axis=-1, keepdims=True)
    inverse = lax.rsqrt(jnp.mean(center * center, axis=-1, keepdims=True) + EPS)
    return (center * inverse, inverse)


def norm_back(grad_in, normed, inverse):
    mean_grad = jnp.mean(grad_in, axis=-1, keepdims=True)
    mean_proj = jnp.mean(grad_in * normed, axis=-1, keepdims=True)
    return inverse * (grad_in - mean_grad - normed * mean_proj)


def slope(gate):
    return gate * (1.0 - gate)


def column_sum(values):
    return jnp.sum(values.reshape(-1, values.shape[-1]), axis=0, keepdims=True)


def clear(step, *refs):
    @pl.when(step == 0)
    def _():
        for ref in refs:
            ref[...] = jnp.zeros_like(ref)


def spec(block, along=None, at=None):
    rank = len(block)
    if along is not None:
        return pl.BlockSpec(block, lambda t, core: tuple(t if a == along else 0 for a in range(rank)))
    index = (0,) * rank if at is None else at
    return pl.BlockSpec(
        block,
        lambda t, core: tuple(i(core[0]) if callable(i) else i for i in index),
        pipeline_mode=pl.Buffered(1),
    )


class Order:
    def __init__(self, place):
        self.place = place
        self.last = []


def call(name, kernel, grid, ins, outs, scratch, deps, order, flops=LONG, aliases={}, vmem=VMEM_LIMIT):
    inputs = len(ins)
    deps = list(deps) + order.last

    def run(place_ref, *refs):
        kernel(place_ref, *refs[:inputs], *refs[inputs + len(deps) :])

    found = pl.pallas_call(
        run,
        grid_spec=pltpu.PrefetchScalarGridSpec(
            num_scalar_prefetch=1,
            grid=(grid,),
            in_specs=[s for _, s in ins] + [pl.BlockSpec(memory_space=pl.ANY)] * len(deps),
            out_specs=[s for _, _, s in outs],
            scratch_shapes=scratch,
        ),
        out_shape=[jax.ShapeDtypeStruct(shape, dtype) for shape, dtype, _ in outs],
        compiler_params=pltpu.CompilerParams(
            vmem_limit_bytes=vmem, dimension_semantics=("arbitrary",)
        ),
        cost_estimate=pl.CostEstimate(flops=flops, bytes_accessed=10**6, transcendentals=0),
        name=name,
        input_output_aliases=aliases,
    )(order.place, *[a for a, _ in ins], *deps)
    order.last = [max(found, key=lambda array: array.size)]
    return found


def combine(outputs, order, near=False):
    held = pl.BlockSpec(memory_space=pltpu.VMEM)
    ins, outs, plan = [], [], []
    for terms in outputs:
        if isinstance(terms, tuple):
            bit, *arrays = terms
            terms = [(array, array.shape[0], lambda place: 0, True) for array in arrays]
        else:
            bit = None
        array, slabs = terms[0][:2]
        shape = (slabs,) + array.shape[1:]
        rest = (0,) * (len(shape) - 1)
        sources = []
        for term, _, index, small in terms:
            if near and small:
                sources.append((len(ins), index, slabs))
                ins.append((term, held))
            else:
                sources.append((len(ins), None, slabs))
                ins.append(
                    (term, pl.BlockSpec(shape, lambda t, place, index=index, rest=rest: (index(place),) + rest))
                )
        plan.append((bit, sources))
        blocked = pl.BlockSpec(shape, lambda t, place, rank=len(shape): (0,) * rank)
        outs.append((shape, array.dtype, held if near else blocked))

    def kernel(place, *refs):
        for (bit, sources), out_ref in zip(plan, refs[len(ins) :]):
            values = [
                refs[i][...] if index is None else refs[i][pl.ds(index(place) * slabs, slabs)]
                for i, index, slabs in sources
            ]
            if bit is not None:
                out_ref[...] = jnp.where(place[bit] == 0, values[0], values[1])
            elif len(values) == 1:
                out_ref[...] = values[0]
            else:
                total = sum((v.astype(F32) for v in values[1:]), values[0].astype(F32))
                out_ref[...] = total.astype(out_ref.dtype)

    return call("combine", kernel, 1, ins, outs, [], [], order, vmem=16 * 2**20 if near else VMEM_LIMIT)


class Halving:
    def __init__(self, order, counts):
        self.order = order
        self.counts = counts

    def places(self):
        found = []
        for p in range(2 ** len(self.order)):
            dest, half = 0, 0
            for i, (axis, bit) in enumerate(self.order):
                value = (p >> (len(self.order) - 1 - i)) & 1
                if axis == "sample":
                    dest |= value << bit
                else:
                    half = value
            found.append((dest, half))
        return found

    def halves(self):
        return 2 if any(axis == "struct" for axis, _ in self.order) else 1

    def pieces(self, shape):
        rows, columns = shape
        return rows // self.counts["sample"], columns // self.halves() // PIECE

    def slabs(self, shapes):
        return (2 ** len(self.order), sum(r * c for r, c in map(self.pieces, shapes)), PIECE)

    def pack(self, out_ref, arrays, everywhere=()):
        for p, (dest, half) in enumerate(self.places()):
            held = []
            for array in arrays:
                rows, count = self.pieces(array.shape)
                for c in range(count):
                    at = (half * count + c) * PIECE
                    held.append(array[dest * rows : (dest + 1) * rows, at : at + PIECE])
            slab = jnp.concatenate(held + list(everywhere), axis=0)
            out_ref[p, : slab.shape[0]] = slab.astype(out_ref.dtype)
            if slab.shape[0] < out_ref.shape[1]:
                out_ref[p, slab.shape[0] :] = jnp.zeros(
                    (out_ref.shape[1] - slab.shape[0], PIECE), out_ref.dtype
                )

    def unpack(self, slab, shapes):
        found, at = [], 0
        for shape in shapes:
            rows, count = self.pieces(shape)
            found.append([slab[at + c * rows : at + (c + 1) * rows] for c in range(count)])
            at += rows * count
        return found

    def run(self, array, after="sum"):
        last = self.counts["sample"].bit_length() - 1

        def exchange(array, axis, bit):
            return lax.ppermute(array, axis, [(i, i ^ (1 << bit)) for i in range(self.counts[axis])])

        def halves(at, size):
            return [
                [
                    (p, size, lambda place, base=base, at=at, flip=flip: 2 * base(place) + (place[at] ^ flip), held)
                    for p, base, held in parts
                ]
                for flip in (1, 0)
            ]

        zero = lambda place: 0
        parts, size = [(array, zero, False)], array.shape[0]
        for axis, bit in self.order:
            at = bit if axis == "sample" else last
            size = size // 2
            if len(parts) == 1 and (axis, bit) == ("sample", 0):
                first = lambda place: place[0]
                parts = [(array, first, False), (exchange(array, axis, bit), first, False)]
                continue
            if len(parts) == 1:
                (sent,) = yield halves(at, size)[:1]
                parts = [(array, lambda place, at=at: place[at], False), (exchange(sent, axis, bit), zero, True)]
            else:
                sent, kept = yield halves(at, size)
                parts = [(kept, zero, True), (exchange(sent, axis, bit), zero, True)]
        if after in ("swap", "cores"):
            sent, kept = yield halves(0, size // 2)
            return kept[0], exchange(sent, "sample", 0)[0] if after == "swap" else sent[0]
        (held,) = yield [[(p, 1, base, near) for p, base, near in parts]]
        if not after:
            return held[0]
        if self.halves() == 2:
            received = exchange(held, "struct", 0)
            first, second = yield [(last, held, received), (last, received, held)]
            return first[0], second[0]
        for bit in range(self.counts["struct"].bit_length() - 1):
            received = exchange(held, "struct", bit)
            (held,) = yield [[(p, 1, zero, True) for p in (held, received)]]
        return held[0]

class Running:
    def __init__(self, steps):
        self.steps = steps
        self.result = None
        self.send(None)

    def send(self, found):
        try:
            self.asked = self.steps.send(found)
        except StopIteration as stop:
            self.asked = []
            self.result = stop.value


def advance(order, *running, near=False):
    running = [r for r in running if r.result is None]
    asked = [output for r in running for output in r.asked]
    if not asked:
        return []
    made = combine(asked, order, near)
    at = 0
    for r in running:
        count = len(r.asked)
        r.send(made[at : at + count])
        at += count
    return made


def pair_forward_kernel(place, pair_ref, gain_ref, weight_ref, mask_ref, lengths_ref, out_ref, terms):
    gain = gain_ref[...].astype(F32)
    rows, length, channels = pair_ref.shape
    average = jnp.full((channels, channels), 1.0 / channels, BF16)
    position = lax.broadcasted_iota(jnp.int32, (1, length), 1)
    valid = (position < lengths_ref[0]) & ((mask_ref[...] == 1) | (position == 0))
    for i in range(rows):
        values = pair_ref[i]
        center = values.astype(F32) - dot(values, average)
        inverse = lax.rsqrt(jnp.mean(center * center, axis=-1, keepdims=True) + EPS)
        affine = (center * inverse * gain).astype(BF16)
        terms[i] = jnp.where(valid, dot(weight_ref[...], affine, 1, 1), MASKED)
    for h in range(terms.shape[1]):
        out_ref[h] = terms[:, h, :].astype(BF16)


def pair_forward(pair, gain, weight_t, mask, lengths, order):
    rows, length, channels = pair.shape
    heads = weight_t.shape[0]
    block = 16 if rows % 16 == 0 else rows
    return call(
        "pair_forward",
        pair_forward_kernel,
        rows // block,
        [
            (pair, spec((block, length, channels), 0)),
            (gain, spec(gain.shape)),
            (weight_t, spec(weight_t.shape)),
            (mask, spec(mask.shape)),
            (lengths, pl.BlockSpec(memory_space=pltpu.SMEM)),
        ],
        [((heads, rows, length), BF16, spec((heads, block, length), 1))],
        [pltpu.VMEM((block, heads, length), F32)],
        [],
        order,
    )[0]


def pair_backward_kernel(chunks, place, pair_ref, gain_ref, weight_ref, *refs):
    grad_refs, (out_ref, weight_grad_ref, grads) = refs[:chunks], refs[-3:]
    gain = gain_ref[...]
    channels = pair_ref.shape[2]
    average = jnp.full((channels, channels), 1.0 / channels, BF16)
    clear(pl.program_id(0), weight_grad_ref)
    head = 0
    for ref in grad_refs:
        for h in range(ref.shape[0]):
            grads[:, head, :] = ref[h].astype(F32)
            head += 1
    scaled = weight_ref[...].astype(F32) * gain
    means = jnp.broadcast_to(jnp.mean(scaled, axis=-1, keepdims=True), scaled.shape)
    full = jnp.concatenate([scaled, means], axis=1)
    high = full.astype(BF16)
    parts = jnp.concatenate([high, (full - high.astype(F32)).astype(BF16)], axis=0)

    def row(i, carry):
        values = pair_ref[i]
        center = values.astype(F32) - dot(values, average)
        inverse = lax.rsqrt(jnp.mean(center * center, axis=-1, keepdims=True) + EPS)
        normed = center * inverse
        grad = grads[i].astype(BF16)
        weight_grad_ref[...] += dot(grad, (normed * gain).astype(BF16))
        both = dot(jnp.concatenate([grad, grad], axis=0), parts, 0, 0)
        grad_normed = both[:, :channels]
        mean_proj = jnp.mean(grad_normed * normed, axis=-1, keepdims=True)
        out_ref[i] = inverse * (grad_normed - both[:, channels:] - normed * mean_proj)
        return carry

    lax.fori_loop(0, pair_ref.shape[0], row, 0, unroll=8)

    @pl.when((pl.program_id(0) == pl.num_programs(0) - 1) & (place[0] == 1))
    def _():
        half = weight_grad_ref.shape[0] // 2
        total = weight_grad_ref[...]
        weight_grad_ref[...] = jnp.concatenate([total[half:], total[:half]], axis=0)


def pair_backward(first, count, block, out, pair, grads, gain, weight_t, deps, order):
    rows, length, channels = pair.shape
    heads = weight_t.shape[0]
    blocked = pl.BlockSpec((block, length, channels), lambda t, place: (first + t, 0, 0))
    ins = [(pair, blocked), (gain, spec(gain.shape)), (weight_t, spec(weight_t.shape))] + [
        (g, pl.BlockSpec((g.shape[0], block, length), lambda t, place: (0, first + t, 0))) for g in grads
    ]
    aliases = {}
    if out is not None:
        aliases = {1 + len(ins): 0}
        ins.append((out, pl.BlockSpec(memory_space=pl.ANY)))
    return call(
        "pair_backward",
        functools.partial(pair_backward_kernel, len(grads)),
        count,
        ins,
        [(pair.shape, F32, blocked), ((heads, channels), F32, spec((heads, channels)))],
        [pltpu.VMEM((block, heads, length), F32)],
        deps,
        order,
        LONG,
        aliases,
    )


def conditions(cond_ref, gain_ref, cond_w_ref, cond_b_ref, zero_w_ref, zero_b_ref, zero_gate_ref, factor_ref, shift_ref):
    cond = cond_ref[...]
    width = zero_gate_ref.shape[1]
    zero_gate_ref[...] = jax.nn.sigmoid(dot(cond, zero_w_ref[...]) + zero_b_ref[...])
    cond_normed, _ = layer_norm(cond.astype(F32))
    projected = dot((cond_normed * gain_ref[...]).astype(BF16), cond_w_ref[...])
    factor_ref[...] = jax.nn.sigmoid(projected[:, :width] + cond_b_ref[...])
    shift_ref[...] = projected[:, width:]


def conditions_back(cond_ref, gain_ref, cond_w_ref, zero_w_ref, zero_grad, projected):
    cond = cond_ref[...]
    cond_normed, cond_inverse = layer_norm(cond.astype(F32))
    scaled = (cond_normed * gain_ref[...]).astype(BF16)
    grad_scaled = dot(projected, cond_w_ref[...], 1, 1)
    return (
        dot(scaled, projected, 0, 0),
        dot(cond, zero_grad, 0, 0),
        column_sum(grad_scaled * cond_normed),
        dot(zero_grad, zero_w_ref[...], 1, 1),
        grad_scaled * gain_ref[...],
        cond_normed,
        cond_inverse,
    )


def step_rows(step, tokens):
    return pl.ds(pl.multiple_of(step * tokens, tokens), tokens)


def inputs_kernel(
    place, acts_ref, acts_other_ref, cot_ref, cot_other_ref,
    cond_ref, gain_ref, cond_w_ref, cond_b_ref, zero_w_ref, zero_b_ref,
    query_ref, key_ref, value_ref, gate_w_ref, q_bias_ref, out_w_ref,
    input_ref, gate_ref, gated_grad_ref, q_ref, k_ref, v_ref, g_ref, qt_ref, kt_ref, vt_ref, gt_ref,
    zero_gate_ref, factor_ref, shift_ref,
):
    step = pl.program_id(0)
    samples, tokens, half = gate_ref.shape
    width = acts_ref.shape[2]
    rows = samples * tokens

    @pl.when(step == 0)
    def _():
        conditions(
            cond_ref, gain_ref, cond_w_ref, cond_b_ref, zero_w_ref, zero_b_ref, zero_gate_ref, factor_ref, shift_ref
        )

    here = step_rows(step, tokens)
    acts = jnp.concatenate([acts_ref[...], acts_other_ref[...]], axis=0)
    normed, _ = layer_norm(acts.astype(F32))
    first = (factor_ref[here, :][None] * normed + shift_ref[here, :][None]).astype(BF16)
    input_ref[...] = first
    first = first.reshape(rows, width)
    cot = jnp.concatenate([cot_ref[...], cot_other_ref[...]], axis=0)
    grad_att = (cot.astype(F32) * zero_gate_ref[here, :][None]).astype(BF16)
    grad_gated = dot(grad_att.reshape(rows, width), out_w_ref[...], 1, 1)
    gated_grad_ref[...] = grad_gated.reshape(samples, tokens, half)
    gate = jax.nn.sigmoid(dot(first, gate_w_ref[...]))
    gate_ref[...] = gate.reshape(samples, tokens, half)

    def put(values, nat_ref, t_ref):
        low = values.astype(BF16).reshape(samples, tokens, half)
        chunks = nat_ref.shape[0]
        used = half // chunks
        for chunk in range(chunks):
            nat_ref[chunk, :, :, :used] = low[:, :, chunk * used : (chunk + 1) * used]
            nat_ref[chunk, :, :, used:] = jnp.zeros((samples, tokens, LANES - used), BF16)
        for s in range(samples):
            t_ref[s] = low[s].T

    put(grad_gated * gate, g_ref, gt_ref)
    put(dot(first, query_ref[...]) + q_bias_ref[...], q_ref, qt_ref)
    put(dot(first, key_ref[...]), k_ref, kt_ref)
    put(dot(first, value_ref[...]), v_ref, vt_ref)


def own(core):
    return core


def other(core):
    return 1 - core


def quarters(weight, whose):
    rows, columns = weight.shape
    return [
        (weight, spec((rows, columns // 8), at=(0, functools.partial(lambda j, core: 2 * j + whose(core), j))))
        for j in range(4)
    ]


def inputs_call(acts, acts_other, cot, cot_other, cond, branch, qkvg_w, q_bias, out_w, heads, deps, order):
    own_samples, length, width = acts.shape
    samples, half = 2 * own_samples, width // 2
    chunks = heads // 2 // CHUNK_HEADS
    block = spec((own_samples, TOKENS, width), 1)
    wide = spec((samples, TOKENS, width), 1)
    narrow = spec((samples, TOKENS, half), 1)
    nat = spec((chunks, samples, TOKENS, LANES), 2)
    turned = spec((samples, half, TOKENS), 2)
    return call(
        "inputs",
        inputs_kernel,
        length // TOKENS,
        [(a, block) for a in (acts, acts_other, cot, cot_other)]
        + [(cond, spec(cond.shape))]
        + branch
        + quarters(qkvg_w, own)
        + [(q_bias, spec((1, half), at=(0, own))), (out_w, spec((half, width), at=(own, 0)))],
        [
            ((samples, length, width), BF16, wide),
            ((samples, length, half), F32, narrow),
            ((samples, length, half), F32, narrow),
        ]
        + [((chunks, samples, length, LANES), BF16, nat)] * 4
        + [((samples, half, length), BF16, turned)] * 4
        + [((length, width), F32, spec((length, width)))] * 2,
        [pltpu.VMEM((length, width), F32)],
        deps,
        order,
    )


def transition_kernel(
    halving, place, acts_ref, cot_ref, cond_ref, gain_ref, cond_w_ref, cond_b_ref, zero_w_ref, zero_b_ref,
    swiglu_ref, down_ref,
    partial_ref, acts_grad_ref, cond_gate_ref, cond_norm_ref, packed_out, cond_b_out, zero_b_out, gain_out,
    swiglu_acc, down_acc, zero_gate_ref, factor_ref, shift_ref, zero_low, projected,
):
    step = pl.program_id(0)
    clear(step, swiglu_acc, down_acc, cond_b_out, zero_b_out)
    samples, tokens, width = acts_ref.shape
    rows = samples * tokens
    hidden_width = down_ref.shape[0]

    @pl.when(step == 0)
    def _():
        conditions(
            cond_ref, gain_ref, cond_w_ref, cond_b_ref, zero_w_ref, zero_b_ref, zero_gate_ref, factor_ref, shift_ref
        )

    here = step_rows(step, tokens)
    zero_gate = zero_gate_ref[here, :]
    factor = factor_ref[here, :]
    acts = acts_ref[...].astype(F32)
    normed, _ = layer_norm(acts)
    second = (factor[None] * normed + shift_ref[here, :][None]).astype(BF16).reshape(rows, width)
    grad_out = cot_ref[...].astype(F32)
    grad_tr = (grad_out * zero_gate[None]).astype(BF16).reshape(rows, width)
    transition = grad_input = 0.0
    second_t = second.T
    for at in range(0, hidden_width, HIDDEN):
        gate_at, up_at = slice(at, at + HIDDEN), slice(hidden_width + at, hidden_width + at + HIDDEN)
        gate_part = dot(second, swiglu_ref[:, gate_at])
        up_part = dot(second, swiglu_ref[:, up_at])
        gate_sig = jax.nn.sigmoid(gate_part)
        silu = gate_part * gate_sig
        product = (silu * up_part).astype(BF16)
        transition += dot(product, down_ref[gate_at, :])
        grad_product = dot(grad_tr, down_ref[gate_at, :], 1, 1)
        down_acc[gate_at, :] += dot(product, grad_tr, 0, 0)
        grad_up = (grad_product * silu).astype(BF16)
        grad_gate = (grad_product * up_part * gate_sig * (1.0 + gate_part * (1.0 - gate_sig))).astype(BF16)
        swiglu_acc[:, gate_at] += dot(second_t, grad_gate)
        swiglu_acc[:, up_at] += dot(second_t, grad_up)
        grad_input += dot(grad_gate, swiglu_ref[:, gate_at], 1, 1)
        grad_input += dot(grad_up, swiglu_ref[:, up_at], 1, 1)
    transition = transition.reshape(samples, tokens, width)
    grad_input = grad_input.reshape(samples, tokens, width)
    partial_ref[...] = acts + zero_gate[None] * transition
    grad_zero = jnp.sum(grad_out * transition, axis=0) * slope(zero_gate)
    zero_b_out[...] += column_sum(grad_zero)
    zero_low[here, :] = grad_zero.astype(BF16)
    grad_factor = jnp.sum(grad_input * normed, axis=0) * slope(factor)
    cond_b_out[...] += column_sum(grad_factor)
    projected[here, :width] = grad_factor.astype(BF16)
    projected[here, width:] = jnp.sum(grad_input, axis=0).astype(BF16)
    acts_grad_ref[...] = grad_input * factor[None]

    @pl.when(step == pl.num_programs(0) - 1)
    def _():
        cond_w_grad, zero_w_grad, gain_grad, cond_gate, cond_norm, _, _ = conditions_back(
            cond_ref, gain_ref, cond_w_ref, zero_w_ref, zero_low[...], projected[...]
        )
        gain_out[...] = gain_grad
        cond_gate_ref[...] = cond_gate
        cond_norm_ref[...] = cond_norm
        halving.pack(packed_out, [swiglu_acc, down_acc, cond_w_grad, zero_w_grad])


def transition_call(acts, cot, cond, branch, swiglu, down, halving, deps, order):
    samples, length, width = acts.shape
    cond_width = cond.shape[1]
    hidden = down.shape[0]
    rows = samples * length
    block = spec((samples, TOKENS, width), 1)
    weights = [(width, 2 * hidden), (hidden, width), (cond_width, 2 * width), (cond_width, width)]
    vectors = [(1, width), (1, width), (1, cond_width)]
    results = call(
        "transition",
        functools.partial(transition_kernel, halving),
        length // TOKENS,
        [(acts, block), (cot, block), (cond, spec(cond.shape))]
        + branch
        + [(swiglu, spec(swiglu.shape)), (down, spec(down.shape))],
        [(acts.shape, F32, block)] * 2
        + [(cond.shape, F32, spec(cond.shape))] * 2
        + [(halving.slabs(weights), BF16, spec(halving.slabs(weights)))]
        + [(s, F32, spec(s)) for s in vectors],
        [pltpu.VMEM(s, F32) for s in weights[:2]]
        + [pltpu.VMEM((length, width), F32)] * 3
        + [pltpu.VMEM((length, width), BF16), pltpu.VMEM((length, 2 * width), BF16)],
        deps,
        order,
    )
    return results, weights


def attention_kernel(
    halving, head_dim, place, q_ref, k_ref, v_ref, g_ref, qt_ref, kt_ref, vt_ref, gt_ref, bias_ref,
    mixed_ref, dq_ref, dkt_ref, dvt_ref, db_ref, kz, vz, plow, dslow, dsum,
):
    h = pl.program_id(0)
    samples, length, wide = q_ref.shape
    scale = head_dim ** (-0.5)
    off = pl.multiple_of(h * head_dim, 16)
    lane = lax.broadcasted_iota(jnp.int32, (1, wide), 1)
    mask = ((lane >= off) & (lane < off + head_dim)).astype(BF16)

    @pl.when(h == 0)
    def _():
        mixed_ref[...] = jnp.zeros_like(mixed_ref)
        dq_ref[...] = jnp.zeros_like(dq_ref)

    kz[...] = jnp.zeros_like(kz)
    vz[...] = jnp.zeros_like(vz)
    for s in range(samples):
        kz[s, pl.ds(off, head_dim), :] = kt_ref[s]
        vz[s, pl.ds(off, head_dim), :] = vt_ref[s]
    parts, _, share, _ = bias_ref.shape
    if share % 16 == 0:
        bias = bias_ref[:, 0].reshape(length, length).astype(F32)
    else:
        bias = jnp.concatenate([bias_ref[p, 0].astype(F32) for p in range(parts)], axis=0)
    for s in range(samples):
        x = dot(q_ref[s], kz[s]) * scale + bias
        x = jnp.exp(x - jnp.max(x, axis=-1, keepdims=True))
        probs = x * (1.0 / jnp.sum(x, axis=-1, keepdims=True))
        low = probs.astype(BF16)
        plow[s % 2] = low
        mixed = dot(low, v_ref[s] * mask)
        mixed_ref[s] += mixed
        grad = g_ref[s]
        delta = jnp.sum(grad.astype(F32) * mixed, axis=-1, keepdims=True)
        grad_scores = probs * (dot(grad, vz[s]) - delta)
        grad_low = grad_scores.astype(BF16)
        dslow[s % 2] = grad_low
        total = grad_scores if s == 0 else dsum[...] + grad_scores
        if s < samples - 1:
            dsum[...] = total
        else:
            for p, (dest, _) in enumerate(halving.places()):
                for c in range(2):
                    at = (dest + c) * share
                    db_ref[2 * p + c, 0] = total[at : at + share].astype(BF16)
        dq_ref[s] += dot(grad_low, k_ref[s] * mask) * scale
        dvt_ref[s] = dot(gt_ref[s], plow[s % 2]).astype(BF16)
        dkt_ref[s] = (dot(qt_ref[s], dslow[s % 2]) * scale).astype(BF16)


def attention_call(chunk, nats, turned, bias, head_dim, halving, deps, order):
    _, samples, length, wide = nats[0].shape
    parts, heads, share, _ = bias.shape
    nat = pl.BlockSpec((None, samples, length, wide), lambda h, core: (chunk, 0, 0, 0))
    turn = pl.BlockSpec((samples, head_dim, length), lambda h, core: (0, chunk * CHUNK_HEADS + h, 0))
    turn_out = pl.BlockSpec((samples, head_dim, length), lambda h, core: (0, h, 0))
    bias_in = pl.BlockSpec(
        (parts, 1, share, length), lambda h, core: (0, core[0] * (heads // 2) + chunk * CHUNK_HEADS + h, 0, 0)
    )
    bias_out = pl.BlockSpec((parts, 1, share, length), lambda h, core: (0, h, 0, 0))
    held = pl.BlockSpec((samples, length, wide), lambda h, core: (0, 0, 0))
    return call(
        "attention",
        functools.partial(attention_kernel, halving, head_dim),
        CHUNK_HEADS,
        [(a, nat) for a in nats] + [(a, turn) for a in turned] + [(bias, bias_in)],
        [((samples, length, wide), F32, held)] * 2
        + [((samples, CHUNK_HEADS * head_dim, length), BF16, turn_out)] * 2
        + [((parts, CHUNK_HEADS, share, length), BF16, bias_out)],
        [
            pltpu.VMEM((samples, wide, length), BF16),
            pltpu.VMEM((samples, wide, length), BF16),
            pltpu.VMEM((2, length, length), BF16),
            pltpu.VMEM((2, length, length), BF16),
            pltpu.VMEM((length, length), F32),
        ],
        deps,
        order,
        SHORT,
    )


def mixed_kernel(chunks, place, *refs):
    (gate_ref, gated_grad_ref), refs = refs[:2], refs[2:]
    mixed_refs, refs = refs[:chunks], refs[chunks:]
    dq_refs, refs = refs[:chunks], refs[chunks:]
    dkt_refs, refs = refs[:chunks], refs[chunks:]
    dvt_refs, refs = refs[:chunks], refs[chunks:]
    joined_refs, q_bias_out = refs[:2], refs[2]
    clear(pl.program_id(0), q_bias_out)
    samples, tokens, half = gate_ref.shape
    own_samples = samples // 2

    def join(refs):
        return jnp.concatenate([ref[:, :, : half // chunks] for ref in refs], axis=-1)

    def turn(turned_refs):
        joined = jnp.concatenate([ref[...] for ref in turned_refs], axis=1)
        return jnp.stack([joined[s].T for s in range(samples)], axis=0)

    mixed = join(mixed_refs)
    gate = gate_ref[...]
    gated = (gate * mixed).astype(BF16)
    grad_queries = join(dq_refs)
    q_bias_out[...] += column_sum(grad_queries)
    grad_gate = gated_grad_ref[...] * mixed * slope(gate)
    parts = [gated, grad_queries.astype(BF16), turn(dkt_refs), turn(dvt_refs), grad_gate.astype(BF16)]
    for i in range(2):
        here = slice(i * own_samples, (i + 1) * own_samples)
        for j, part in enumerate(parts):
            joined_refs[i][:, :, j * half : (j + 1) * half] = part[here]


def mixed_call(gate, gated_grad, mixeds, dqs, dkts, dvts, deps, order):
    samples, length, half = gate.shape
    chunks = len(mixeds)
    own_samples = samples // 2
    block = spec((samples, TOKENS, half), 1)
    window = spec((samples, TOKENS, LANES), 1)
    turned = spec((samples, half // chunks, TOKENS), 2)
    return call(
        "mixed",
        functools.partial(mixed_kernel, chunks),
        length // TOKENS,
        [(a, block) for a in (gate, gated_grad)]
        + [(a, window) for a in mixeds + dqs]
        + [(a, turned) for a in dkts + dvts],
        [((own_samples, length, 5 * half), BF16, spec((own_samples, TOKENS, 5 * half), 1))] * 2
        + [((1, half), F32, spec((1, half)))],
        [],
        deps,
        order,
    )


def qkvg_kernel(halving, place, first_ref, *refs):
    joined_refs, other_refs, packed_out = refs[:2], refs[2:4], refs[4]
    step = pl.program_id(0)
    samples, length, width = first_ref.shape
    rows = samples * length // 2
    half = joined_refs[0].shape[2]

    def both(pair):
        return jnp.concatenate([ref[...].reshape(rows, half) for ref in pair], axis=1)

    grad = dot(first_ref[: samples // 2].reshape(rows, width), both(joined_refs), 0, 0)
    grad += dot(first_ref[samples // 2 :].reshape(rows, width), both(other_refs), 0, 0)
    share = packed_out.shape[1] * halving.halves() // 4

    for block in range(4):

        @pl.when(step == block // 2)
        def _():
            column = block % 2 * half
            for p, (dest, part) in enumerate(halving.places()):
                piece = block - part * (4 // halving.halves())
                if 0 <= piece < 4 // halving.halves():
                    for c in range(2):
                        at = (dest + c) * share
                        packed_out[2 * p + c, piece * share : (piece + 1) * share] = grad[
                            at : at + share, column : column + half
                        ].astype(BF16)


def qkvg_call(first, joined, joined_other, halving, deps, order):
    samples, length, width = first.shape
    half = joined.shape[2] // 5
    share = width // halving.counts["sample"]
    slabs = (2 * 2 ** len(halving.order), 4 // halving.halves() * share, half)
    blocks = [
        pl.BlockSpec((samples // 2, length, half), lambda t, place, i=i: (0, 0, 1 + 2 * t + i)) for i in range(2)
    ]
    (packed,) = call(
        "qkvg_grad",
        functools.partial(qkvg_kernel, halving),
        2,
        [(first, spec(first.shape))] + [(a, b) for a in (joined, joined_other) for b in blocks],
        [(slabs, BF16, spec(slabs))],
        [],
        deps,
        order,
    )
    return packed


def outputs_kernel(place, acts_ref, cot_ref, partial_ref, acts_part_ref, zero_gate_ref, factor_ref, *refs):
    joined_refs, refs = refs[:2], refs[2:]
    out_w_refs, qkvg_refs, refs = refs[:2], (refs[2:6], refs[6:10]), refs[10:]
    block_ref, acts_grad_ref, projected_ref, zero_low_ref, cond_b_out, zero_b_out, out_out = refs
    clear(pl.program_id(0), cond_b_out, zero_b_out, out_out)
    samples, tokens, width = acts_ref.shape
    rows = samples * tokens
    half = width // 2
    zero_gate = zero_gate_ref[...]
    factor = factor_ref[...]
    normed, inverse = layer_norm(acts_ref[...].astype(F32))
    grad_out = cot_ref[...].astype(F32)
    grad_att = (grad_out * zero_gate[None]).astype(BF16).reshape(rows, width)
    attended = grad_input = 0.0
    for i, half_at in enumerate((place[0], 1 - place[0])):
        gated = joined_refs[i][:, :, :half].reshape(rows, half)
        attended += dot(gated, out_w_refs[i][...])
        out_out[pl.ds(pl.multiple_of(half_at * half, half), half), :] += dot(gated, grad_att, 0, 0)
        for j in range(4):
            grad_input += dot(
                joined_refs[i][:, :, (1 + j) * half : (2 + j) * half].reshape(rows, half), qkvg_refs[i][j][...], 1, 1
            )
    attended = attended.reshape(samples, tokens, width)
    grad_input = grad_input.reshape(samples, tokens, width)
    block_ref[...] = (partial_ref[...] + zero_gate[None] * attended).astype(BF16)
    grad_zero = jnp.sum(grad_out * attended, axis=0) * slope(zero_gate)
    zero_b_out[...] += column_sum(grad_zero)
    zero_low_ref[...] = grad_zero.astype(BF16)
    grad_factor = jnp.sum(grad_input * normed, axis=0) * slope(factor)
    cond_b_out[...] += column_sum(grad_factor)
    projected_ref[:, :width] = grad_factor.astype(BF16)
    projected_ref[:, width:] = jnp.sum(grad_input, axis=0).astype(BF16)
    acts_grad_ref[...] = (
        grad_out + norm_back(grad_input * factor[None] + acts_part_ref[...], normed, inverse)
    ).astype(BF16)


def outputs_call(acts, cot, partial, acts_part, zero_gate, factor, joineds, out_w, qkvg_w, deps, order):
    samples, length, width = acts.shape
    half = width // 2
    block = spec((samples, TOKENS, width), 1)
    tokens = spec((TOKENS, width), 0)
    return call(
        "outputs",
        outputs_kernel,
        length // TOKENS,
        [(a, block) for a in (acts, cot, partial, acts_part)]
        + [(zero_gate, tokens), (factor, tokens)]
        + [(a, spec((samples, TOKENS, 5 * half), 1)) for a in joineds]
        + [(out_w, spec((half, width), at=(whose, 0))) for whose in (own, other)]
        + quarters(qkvg_w, own)
        + quarters(qkvg_w, other),
        [
            (acts.shape, BF16, block),
            (acts.shape, BF16, block),
            ((length, 2 * width), BF16, spec((TOKENS, 2 * width), 0)),
            ((length, width), BF16, tokens),
        ]
        + [(s, F32, spec(s)) for s in ((1, width), (1, width), (width, width))],
        [],
        deps,
        order,
    )


def conditions_kernel(
    rest, vector_parts, place, cond_ref, gain_ref, cond_w_ref, zero_w_ref, zero_low_ref, projected_ref,
    cond_gate_in, cond_norm_in, out_w_grad_ref, *refs
):
    vector_refs, (packed_out,) = refs[:vector_parts], refs[vector_parts:]
    cond_w_grad, zero_w_grad, gain_grad, cond_gate, cond_norm, cond_normed, cond_inverse = conditions_back(
        cond_ref, gain_ref, cond_w_ref, zero_w_ref, zero_low_ref[...], projected_ref[...]
    )
    cond_grad = (
        cond_gate + cond_gate_in[...] + norm_back(cond_norm + cond_norm_in[...], cond_normed, cond_inverse)
    )
    vectors = [gain_grad] + [ref[...] for ref in vector_refs[:-1]]
    q_bias = vector_refs[-1][...]
    vectors += [jnp.where(place[0] == 0, q_bias, 0.0), jnp.where(place[0] == 1, q_bias, 0.0)]
    pieces = [v[:, at : at + PIECE] for v in vectors for at in range(0, v.shape[1], PIECE)]
    rest.pack(packed_out, [out_w_grad_ref[...], cond_w_grad, zero_w_grad, cond_grad], pieces)


def conditions_call(cond, branch, zero_w, zero_low, projected, cond_gate, cond_norm, out_w_grad, vectors, rest, deps, order):
    cond_width = cond.shape[1]
    width = zero_low.shape[1]
    weights = [out_w_grad.shape, (cond_width, 2 * width), (cond_width, width), cond.shape]
    count, rows, columns = rest.slabs(weights)
    rows += (sum(v.shape[1] for v in vectors) + cond_width + width // 2) // PIECE
    rows += -rows % 16
    fixed = (zero_low, projected, cond_gate, cond_norm, out_w_grad, *vectors)
    (packed,) = call(
        "conditions",
        functools.partial(conditions_kernel, rest, len(vectors)),
        1,
        [(cond, spec(cond.shape))] + branch[:2] + [zero_w] + [(a, spec(a.shape)) for a in fixed],
        [((count, rows, columns), BF16, spec((count, rows, columns)))],
        [],
        deps,
        order,
    )
    return packed, weights


def results_kernel(
    early_halving, rest_halving, early_shapes, rest_shapes, halves, place, *refs
):
    early_refs, refs = refs[:halves], refs[halves:]
    qkvg_refs, refs = refs[: 2 * halves], refs[2 * halves :]
    (rest_ref, rest_got_ref, pair_sum_ref, pair_wt_ref, pair_gain_ref), refs = refs[:5], refs[5:]
    (cond_ref, cond_w_ref, zero_w_ref, qkvg_ref, out_w_ref, swiglu_ref, down_ref), refs = refs[:7], refs[7:]
    gains_ref, cond_b_ref, zero_b_ref, q_bias_ref, pair_gain_out, pair_w_out = refs
    bits = place.shape[0] - 1
    device = sum(place[bit] << bit for bit in range(bits))

    def columns(ref, pieces):
        for c, piece in enumerate(pieces):
            ref[:, c * PIECE : (c + 1) * PIECE] = piece.astype(F32)

    early = [early_halving.unpack(ref[...].astype(F32), early_shapes) for ref in early_refs]
    swiglu, down, cond_w_one, zero_w_one = [sum(parts, []) for parts in zip(*early)]
    before = rest_ref[...].astype(F32)
    total = before + rest_got_ref[...].astype(F32)
    out_w, cond_w_zero, zero_w_zero, _ = rest_halving.unpack(total, rest_shapes)
    columns(swiglu_ref, swiglu)
    columns(down_ref, down)
    columns(cond_w_ref, cond_w_zero + cond_w_one)
    columns(zero_w_ref, zero_w_zero + zero_w_one)
    columns(out_w_ref, out_w)
    columns(cond_ref, rest_halving.unpack(before, rest_shapes)[3])
    parts = []
    for i in range(2):
        held = [ref[...].astype(F32) for ref in qkvg_refs[i * halves : (i + 1) * halves]]
        if halves == 2:
            first = place[bits] == 0
            held = [jnp.where(first, held[0], held[1]), jnp.where(first, held[1], held[0])]
        parts.append(jnp.concatenate(held, axis=0))
    first = place[0] == 0
    parts = [jnp.where(first, parts[0], parts[1]), jnp.where(first, parts[1], parts[0])]
    rows = parts[0].shape[0] // 4
    columns(qkvg_ref, [part[j * rows : (j + 1) * rows] for j in range(4) for part in parts])
    at = sum(r * c for r, c in map(rest_halving.pieces, rest_shapes))
    for ref in (gains_ref, cond_b_ref, zero_b_ref, q_bias_ref):
        size = ref.shape[1]
        count = size * rest_halving.counts["sample"] // PIECE
        value = 0.0
        for c in range(count):
            source = lax.broadcasted_iota(jnp.int32, (PIECE, size), 0) + c * PIECE
            target = lax.broadcasted_iota(jnp.int32, (PIECE, size), 1) + device * size
            chosen = (source == target).astype(F32)
            value += lax.dot_general(
                total[at + c : at + c + 1],
                chosen,
                (((1,), (0,)), ((), ())),
                precision=lax.Precision.HIGHEST,
                preferred_element_type=F32,
            )
        ref[...] = value
        at += count
    size, heads = pair_w_out.shape
    channels = pair_sum_ref.shape[1]
    source = lax.broadcasted_iota(jnp.int32, (channels, size), 0)
    target = lax.broadcasted_iota(jnp.int32, (channels, size), 1) + device * size
    chosen = (source == target).astype(F32)

    def choose(array):
        return lax.dot_general(
            chosen,
            array,
            (((0,), (1,)), ((), ())),
            precision=lax.Precision.HIGHEST,
            preferred_element_type=F32,
        )

    grad = choose(pair_sum_ref[...])
    pair_w_out[...] = grad
    weighted = grad * choose(pair_wt_ref[...].astype(F32))

    def across(left, right, right_dim):
        return lax.dot_general(
            left,
            right,
            (((1,), (right_dim,)), ((), ())),
            precision=lax.Precision.HIGHEST,
            preferred_element_type=F32,
        )

    pair_gain_out[...] = across(jnp.ones((1, heads), F32), weighted, 1) / across(pair_gain_ref[...], chosen, 0)


def results_call(
    early, early_halving, early_shapes, qkvg, rest, rest_got, rest_halving, rest_shapes, pair_sum, pair_wt, pair_gain, order
):
    count = rest_halving.counts["sample"]
    heads, channels = pair_wt.shape
    swiglu, down, cond_w, zero_w = early_shapes
    out_w, _, _, cond = rest_shapes
    width = out_w[1]
    arrays = [cond, (cond_w[0], 2 * cond_w[1]), (zero_w[0], 2 * zero_w[1]), (width, 4 * width), out_w, swiglu, down]
    shapes = [(rows // count, columns) for rows, columns in arrays]
    shapes += [(1, size // count) for size in (2 * cond[1], 2 * width, 2 * width, width)]
    shapes += [(1, channels // count), (channels // count, heads)]
    ins = [*early, *qkvg, rest, rest_got, pair_sum, pair_wt, pair_gain]
    return call(
        "results",
        functools.partial(
            results_kernel, early_halving, rest_halving, early_shapes, rest_shapes, early_halving.halves()
        ),
        1,
        [(a, spec(a.shape)) for a in ins],
        [(shape, F32, spec(shape)) for shape in shapes],
        [],
        [],
        order,
    )


def body(
    struct_count, sample_devices,
    acts, cond, pair, lengths, token_mask, cond_gains, cond_w, cond_bias, output_gate_weights, zero_bias,
    qkvg_w, q_bias, out_w, swiglu_w, down_w, pair_gain, pair_w, cotangent,
):
    acts, cond, pair, cotangent = acts[0], cond[0], pair[0], cotangent[0]
    samples, length, width = acts.shape
    cond_width = cond.shape[1]
    heads = pair_w.shape[1]
    head_dim = width // heads
    chunks = heads // 2 // CHUNK_HEADS
    counts = {"struct": struct_count, "sample": sample_devices}
    bits = sample_devices.bit_length() - 1
    pair_wt = pair_w.T
    device = lax.axis_index("sample")
    core = device & 1
    place = [(device >> bit) & 1 for bit in range(bits)] + [lax.axis_index("struct")]
    order = Order(jnp.stack(place).astype(jnp.int32))

    def swap(array):
        return lax.ppermute(array, "sample", [(i, i ^ 1) for i in range(sample_devices)])

    acts_other, cotangent_other = swap(acts), swap(cotangent)

    bias_rows = pair_forward(pair, pair_gain[None], pair_wt, token_mask, lengths, Order(jnp.zeros(bits + 1, jnp.int32)))
    bias = lax.all_gather(bias_rows, "sample", axis=0, tiled=False)

    rows = {}
    at = 0
    packed = [
        ("gain", cond_gains), ("cond_b", cond_bias), ("zero_b", zero_bias), ("q_bias", q_bias), ("pair", pair_gain)
    ]
    vector = jnp.concatenate([v for _, v in packed]).astype(F32)[None]
    for name, v in packed:
        rows[name] = vector[:, at : at + v.shape[0]]
        at += v.shape[0]

    def conditioning(b):
        return [
            (rows["gain"], spec((1, cond_width), at=(0, b))),
            (cond_w, spec((cond_width, 2 * width), at=(0, b))),
            (rows["cond_b"], spec((1, width), at=(0, b))),
        ]

    def zero(b):
        return [
            (output_gate_weights, spec((cond_width, width), at=(0, b))),
            (rows["zero_b"], spec((1, width), at=(0, b))),
        ]

    def path(*order):
        steps = [("struct", 0) if o == "y" else ("sample", o) for o in order]
        steps = [s for s in steps if s[0] == "sample" or struct_count == 2]
        return Halving(steps + [("sample", b) for b in range(4, bits)], counts)

    along_x = path(0, 1, 2, 3)
    along_y = path(0, "y", 2, 3, 1)
    chip_x = path(1, 2, 3)
    chip_y = path("y", 2, 3, 1)
    results, early_shapes = transition_call(
        acts, cotangent, cond, conditioning(1) + zero(1), swiglu_w, down_w, along_y, [], order
    )
    partial, acts_part, cond_gate, cond_norm, early, cond_b_one, zero_b_one, gain_one = results
    early = Running(along_y.run(early))
    first, gate, gated_grad, *rest = inputs_call(
        acts, acts_other, cotangent, cotangent_other, cond, conditioning(0) + zero(0), qkvg_w, rows["q_bias"], out_w,
        heads, [], order,
    )
    nats, turned, (zero_gate, factor) = rest[:4], rest[4:8], rest[8:]

    mixeds, dqs, dkts, dvts, bias_sums = [], [], [], [], []
    deps = advance(order, early)
    for chunk in range(chunks):
        mixed, dq, dkt, dvt, db = attention_call(chunk, nats, turned, bias, head_dim, chip_x, deps, order)
        mixeds.append(mixed)
        dqs.append(dq)
        dkts.append(dkt)
        dvts.append(dvt)
        bias_sums.append(Running(chip_x.run(db, "swap")))
        deps = advance(order, *bias_sums, *([early] if chunk % 2 else []))

    joined, joined_sent, q_bias_grad = mixed_call(
        gate, gated_grad, mixeds, dqs, dkts, dvts, deps, order
    )
    joined_got = swap(joined_sent)
    qkvg_sum = Running(
        chip_y.run(qkvg_call(first, joined, joined_sent, chip_y, [], order), "cores")
    )
    deps = advance(order, *bias_sums, qkvg_sum, early)
    block_out, acts_grad, projected, zero_low, cond_b_zero, zero_b_zero, out_grad = outputs_call(
        acts, cotangent, partial, acts_part, zero_gate, factor, [joined, joined_got],
        out_w, qkvg_w, deps, order,
    )
    deps = advance(order, *bias_sums, qkvg_sum)
    rest, rest_shapes = conditions_call(
        cond, conditioning(0), zero(0)[0], zero_low, projected, cond_gate, cond_norm, out_grad,
        [gain_one, cond_b_zero, cond_b_one, zero_b_zero, zero_b_one, q_bias_grad], along_x, deps, order,
    )
    rest = Running(along_x.run(rest, ""))
    while any(b.result is None for b in bias_sums):
        advance(order, *bias_sums)
    share = length // sample_devices
    block = 16 if share % 16 == 0 else share
    turned_wt = jnp.where(core == 0, pair_wt, jnp.roll(pair_wt, heads // 2, axis=0))
    grads = [b.result[0] for b in bias_sums] + [b.result[1] for b in bias_sums]
    grad_pair, part = pair_backward(0, 1, block, None, pair, grads, rows["pair"], turned_wt, [], order)
    pair_parts = [part]
    if share > block:
        deps = advance(order, qkvg_sum, rest, early)
        grad_pair, part = pair_backward(
            1, share // block - 1, block, grad_pair, pair, grads, rows["pair"], turned_wt, deps, order
        )
        pair_parts.append(part)
    struct_bits = struct_count.bit_length() - 1

    def summed(array, *masks):
        found = [
            lax.ppermute(array, ("struct", "sample"), [(i, i ^ mask) for i in range(struct_count * sample_devices)])
            for mask in masks
        ]
        if len(found) == 1:
            return array + found[0]
        return (array + found[0]) + (found[1] + found[2])

    class Pair:
        asked = [[(p, p.shape[0], lambda place: 0, True) for p in pair_parts]]
        result = None

        def send(self, found):
            self.result = found[0]

    pair_grad = Pair()
    advance(order, pair_grad, qkvg_sum, rest, early)
    left = [bits + struct_bits - 1] + list(range(bits + struct_bits - 1)) if struct_bits else list(range(bits))
    pair_sum = pair_grad.result
    while left:
        one = 1 << left.pop(0)
        two = 1 << left.pop(0) if left else 0
        pair_sum = summed(pair_sum, one, two, one | two) if two else summed(pair_sum, one)
    chains = (qkvg_sum, rest, early)
    while any(r.result is None for r in chains):
        advance(order, *chains, near=True)
    mine_qkvg, sent = qkvg_sum.result
    if chip_y.halves() == 2:
        across = [
            (s * sample_devices + i, (1 - s) * sample_devices + (i ^ 1))
            for s in range(2)
            for i in range(sample_devices)
        ]
        from_y = lax.ppermute(mine_qkvg, "struct", [(0, 1), (1, 0)])
        from_both = lax.ppermute(sent, ("struct", "sample"), across)
        qkvg = [mine_qkvg, from_y, swap(sent), from_both]
    else:
        for bit in range(struct_bits):
            mine_qkvg, sent = [summed(part, 1 << (bits + bit)) for part in (mine_qkvg, sent)]
        qkvg = [mine_qkvg, swap(sent)]
    early = list(early.result) if along_y.halves() == 2 else [early.result]
    rest_sum, rest_got = rest.result, jnp.zeros_like(rest.result)
    for bit in range(struct_bits):
        if bit:
            rest_sum = rest_sum + rest_got
        rest_got = lax.ppermute(
            rest_sum, "struct", [(i, i ^ (1 << bit)) for i in range(struct_count)]
        )
    (cond_sum, cond_w_sum, zero_w_sum, qkvg_total, out_sum, swiglu_sum, down_sum,
     gains, cond_b, zero_b, q_b, pair_g, pair_w_sum) = results_call(
        early, along_y, early_shapes, qkvg, rest_sum, rest_got, along_x, rest_shapes, pair_sum, pair_wt, rows["pair"], order
    )
    if struct_bits > 1:
        cond_sum = along_x.unpack(rest.result, rest_shapes)[3][0].astype(F32)
    return (
        block_out[None], acts_grad[None], cond_sum[None], grad_pair[None], gains[0], cond_w_sum, cond_b[0], zero_w_sum,
        zero_b[0], qkvg_total, q_b[0], out_sum, swiglu_sum, down_sum, pair_g[0], pair_w_sum,
    )


def solution(mesh):
    per_struct = P("struct", "sample", None, None)
    in_specs = (
        (per_struct, P("struct", None, None), per_struct, P("struct"), P("struct", None))
        + (P(),) * 12
        + (per_struct,)
    )
    one, two = P("sample"), P("sample", None)
    out_specs = (
        per_struct, per_struct, P("struct", "sample", None), per_struct,
        one, two, one, two, one, two, one, two, two, two, one, two,
    )
    local = functools.partial(body, mesh.shape["struct"], mesh.shape["sample"])
    return jax.shard_map(local, mesh=mesh, in_specs=in_specs, out_specs=out_specs, check_vma=False)
```

```python
import functools

import jax
import jax.numpy as jnp
from jax import lax
from jax.experimental import pallas as pl
from jax.experimental.pallas import tpu as pltpu
from jax.sharding import PartitionSpec as P

EPS = 1e-05
MASKED = -1000000000.0
F32 = jnp.float32
BF16 = jnp.bfloat16
CHUNK_HEADS = 2
LANES = 128
PIECE = 384
LONG, SHORT = 10**11, 17 * 10**9
TOKENS = 128
HIDDEN = 768
VMEM_LIMIT = 63 * 2**20


def dot(left, right, left_dim=1, right_dim=0):
    return lax.dot_general(
        left, right, (((left_dim,), (right_dim,)), ((), ())), preferred_element_type=F32
    )


def layer_norm(values):
    center = values - jnp.mean(values, axis=-1, keepdims=True)
    inverse = lax.rsqrt(jnp.mean(center * center, axis=-1, keepdims=True) + EPS)
    return (center * inverse, inverse)


def norm_back(grad_in, normed, inverse):
    mean_grad = jnp.mean(grad_in, axis=-1, keepdims=True)
    mean_proj = jnp.mean(grad_in * normed, axis=-1, keepdims=True)
    return inverse * (grad_in - mean_grad - normed * mean_proj)


def slope(gate):
    return gate * (1.0 - gate)


def column_sum(values):
    return jnp.sum(values.reshape(-1, values.shape[-1]), axis=0, keepdims=True)


def clear(step, *refs):
    @pl.when(step == 0)
    def _():
        for ref in refs:
            ref[...] = jnp.zeros_like(ref)


def spec(block, along=None, at=None):
    rank = len(block)
    if along is not None:
        return pl.BlockSpec(block, lambda t, core: tuple(t if a == along else 0 for a in range(rank)))
    index = (0,) * rank if at is None else at
    return pl.BlockSpec(
        block,
        lambda t, core: tuple(i(core[0]) if callable(i) else i for i in index),
        pipeline_mode=pl.Buffered(1),
    )


class Order:
    def __init__(self, place):
        self.place = place
        self.last = []


def call(name, kernel, grid, ins, outs, scratch, deps, order, flops=LONG, aliases={}, vmem=VMEM_LIMIT):
    inputs = len(ins)
    deps = list(deps) + order.last

    def run(place_ref, *refs):
        kernel(place_ref, *refs[:inputs], *refs[inputs + len(deps) :])

    found = pl.pallas_call(
        run,
        grid_spec=pltpu.PrefetchScalarGridSpec(
            num_scalar_prefetch=1,
            grid=(grid,),
            in_specs=[s for _, s in ins] + [pl.BlockSpec(memory_space=pl.ANY)] * len(deps),
            out_specs=[s for _, _, s in outs],
            scratch_shapes=scratch,
        ),
        out_shape=[jax.ShapeDtypeStruct(shape, dtype) for shape, dtype, _ in outs],
        compiler_params=pltpu.CompilerParams(
            vmem_limit_bytes=vmem, dimension_semantics=("arbitrary",)
        ),
        cost_estimate=pl.CostEstimate(flops=flops, bytes_accessed=10**6, transcendentals=0),
        name=name,
        input_output_aliases=aliases,
    )(order.place, *[a for a, _ in ins], *deps)
    order.last = [max(found, key=lambda array: array.size)]
    return found


def combine(outputs, order, near=False):
    held = pl.BlockSpec(memory_space=pltpu.VMEM)
    ins, outs, plan = [], [], []
    for terms in outputs:
        if isinstance(terms, tuple):
            bit, *arrays = terms
            terms = [(array, array.shape[0], lambda place: 0, True) for array in arrays]
        else:
            bit = None
        array, slabs = terms[0][:2]
        shape = (slabs,) + array.shape[1:]
        rest = (0,) * (len(shape) - 1)
        sources = []
        for term, _, index, small in terms:
            if near and small:
                sources.append((len(ins), index, slabs))
                ins.append((term, held))
            else:
                sources.append((len(ins), None, slabs))
                ins.append(
                    (term, pl.BlockSpec(shape, lambda t, place, index=index, rest=rest: (index(place),) + rest))
                )
        plan.append((bit, sources))
        blocked = pl.BlockSpec(shape, lambda t, place, rank=len(shape): (0,) * rank)
        outs.append((shape, array.dtype, held if near else blocked))

    def kernel(place, *refs):
        for (bit, sources), out_ref in zip(plan, refs[len(ins) :]):
            values = [
                refs[i][...] if index is None else refs[i][pl.ds(index(place) * slabs, slabs)]
                for i, index, slabs in sources
            ]
            if bit is not None:
                out_ref[...] = jnp.where(place[bit] == 0, values[0], values[1])
            elif len(values) == 1:
                out_ref[...] = values[0]
            else:
                total = sum((v.astype(F32) for v in values[1:]), values[0].astype(F32))
                out_ref[...] = total.astype(out_ref.dtype)

    return call("combine", kernel, 1, ins, outs, [], [], order, vmem=16 * 2**20 if near else VMEM_LIMIT)


class Halving:
    def __init__(self, order, counts):
        self.order = order
        self.counts = counts

    def places(self):
        found = []
        for p in range(2 ** len(self.order)):
            dest, half = 0, 0
            for i, (axis, bit) in enumerate(self.order):
                value = (p >> (len(self.order) - 1 - i)) & 1
                if axis == "sample":
                    dest |= value << bit
                else:
                    half = value
            found.append((dest, half))
        return found

    def halves(self):
        return 2 if any(axis == "struct" for axis, _ in self.order) else 1

    def pieces(self, shape):
        rows, columns = shape
        return rows // self.counts["sample"], columns // self.halves() // PIECE

    def slabs(self, shapes):
        return (2 ** len(self.order), sum(r * c for r, c in map(self.pieces, shapes)), PIECE)

    def pack(self, out_ref, arrays, everywhere=()):
        for p, (dest, half) in enumerate(self.places()):
            held = []
            for array in arrays:
                rows, count = self.pieces(array.shape)
                for c in range(count):
                    at = (half * count + c) * PIECE
                    held.append(array[dest * rows : (dest + 1) * rows, at : at + PIECE])
            slab = jnp.concatenate(held + list(everywhere), axis=0)
            out_ref[p, : slab.shape[0]] = slab.astype(out_ref.dtype)
            if slab.shape[0] < out_ref.shape[1]:
                out_ref[p, slab.shape[0] :] = jnp.zeros(
                    (out_ref.shape[1] - slab.shape[0], PIECE), out_ref.dtype
                )

    def unpack(self, slab, shapes):
        found, at = [], 0
        for shape in shapes:
            rows, count = self.pieces(shape)
            found.append([slab[at + c * rows : at + (c + 1) * rows] for c in range(count)])
            at += rows * count
        return found

    def run(self, array, after="sum", sent=None):
        last = self.counts["sample"].bit_length() - 1

        def exchange(array, axis, bit):
            return lax.ppermute(array, axis, [(i, i ^ (1 << bit)) for i in range(self.counts[axis])])

        def halves(at, size):
            return [
                [
                    (p, size, lambda place, base=base, at=at, flip=flip: 2 * base(place) + (place[at] ^ flip), held)
                    for p, base, held in parts
                ]
                for flip in (1, 0)
            ]

        zero = lambda place: 0
        parts, size = [(array, zero, False)], array.shape[0]
        order = self.order
        if sent is not None:
            parts.append((exchange(sent, *order[0]), zero, False))
            order = order[1:]
        for axis, bit in order:
            at = bit if axis == "sample" else last
            size = size // 2
            if len(parts) == 1 and (axis, bit) == ("sample", 0):
                first = lambda place: place[0]
                parts = [(array, first, False), (exchange(array, axis, bit), first, False)]
                continue
            if len(parts) == 1:
                (sent,) = yield halves(at, size)[:1]
                parts = [(array, lambda place, at=at: place[at], False), (exchange(sent, axis, bit), zero, True)]
            else:
                sent, kept = yield halves(at, size)
                parts = [(kept, zero, True), (exchange(sent, axis, bit), zero, True)]
        if after in ("swap", "cores"):
            sent, kept = yield halves(0, size // 2)
            return kept[0], exchange(sent, "sample", 0)[0] if after == "swap" else sent[0]
        (held,) = yield [[(p, 1, base, near) for p, base, near in parts]]
        if not after:
            return held[0]
        if self.halves() == 2:
            received = exchange(held, "struct", 0)
            first, second = yield [(last, held, received), (last, received, held)]
            return first[0], second[0]
        for bit in range(self.counts["struct"].bit_length() - 1):
            received = exchange(held, "struct", bit)
            (held,) = yield [[(p, 1, zero, True) for p in (held, received)]]
        return held[0]

class Running:
    def __init__(self, steps):
        self.steps = steps
        self.result = None
        self.send(None)

    def send(self, found):
        try:
            self.asked = self.steps.send(found)
        except StopIteration as stop:
            self.asked = []
            self.result = stop.value


def advance(order, *running, near=False):
    running = [r for r in running if r.result is None]
    asked = [output for r in running for output in r.asked]
    if not asked:
        return []
    made = combine(asked, order, near)
    at = 0
    for r in running:
        count = len(r.asked)
        r.send(made[at : at + count])
        at += count
    return made


def pair_forward_kernel(place, pair_ref, gain_ref, weight_ref, mask_ref, lengths_ref, out_ref, terms):
    gain = gain_ref[...].astype(F32)
    rows, length, channels = pair_ref.shape
    average = jnp.full((channels, channels), 1.0 / channels, BF16)
    position = lax.broadcasted_iota(jnp.int32, (1, length), 1)
    valid = (position < lengths_ref[0]) & ((mask_ref[...] == 1) | (position == 0))
    for i in range(rows):
        values = pair_ref[i]
        center = values.astype(F32) - dot(values, average)
        inverse = lax.rsqrt(jnp.mean(center * center, axis=-1, keepdims=True) + EPS)
        affine = (center * inverse * gain).astype(BF16)
        terms[i] = jnp.where(valid, dot(weight_ref[...], affine, 1, 1), MASKED)
    for h in range(terms.shape[1]):
        out_ref[h] = terms[:, h, :].astype(BF16)


def pair_forward(pair, gain, weight_t, mask, lengths, order):
    rows, length, channels = pair.shape
    heads = weight_t.shape[0]
    block = 16 if rows % 16 == 0 else rows
    return call(
        "pair_forward",
        pair_forward_kernel,
        rows // block,
        [
            (pair, spec((block, length, channels), 0)),
            (gain, spec(gain.shape)),
            (weight_t, spec(weight_t.shape)),
            (mask, spec(mask.shape)),
            (lengths, pl.BlockSpec(memory_space=pltpu.SMEM)),
        ],
        [((heads, rows, length), BF16, spec((heads, block, length), 1))],
        [pltpu.VMEM((block, heads, length), F32)],
        [],
        order,
    )[0]


def pair_backward_kernel(chunks, place, pair_ref, gain_ref, weight_ref, *refs):
    grad_refs, (out_ref, weight_grad_ref, grads) = refs[:chunks], refs[-3:]
    gain = gain_ref[...]
    channels = pair_ref.shape[2]
    average = jnp.full((channels, channels), 1.0 / channels, BF16)
    clear(pl.program_id(0), weight_grad_ref)
    head = 0
    for ref in grad_refs:
        for h in range(ref.shape[0]):
            grads[:, head, :] = ref[h].astype(F32)
            head += 1
    scaled = weight_ref[...].astype(F32) * gain
    means = jnp.broadcast_to(jnp.mean(scaled, axis=-1, keepdims=True), scaled.shape)
    full = jnp.concatenate([scaled, means], axis=1)
    high = full.astype(BF16)
    parts = jnp.concatenate([high, (full - high.astype(F32)).astype(BF16)], axis=0)

    def row(i, carry):
        values = pair_ref[i]
        center = values.astype(F32) - dot(values, average)
        inverse = lax.rsqrt(jnp.mean(center * center, axis=-1, keepdims=True) + EPS)
        normed = center * inverse
        grad = grads[i].astype(BF16)
        weight_grad_ref[...] += dot(grad, (normed * gain).astype(BF16))
        both = dot(jnp.concatenate([grad, grad], axis=0), parts, 0, 0)
        grad_normed = both[:, :channels]
        mean_proj = jnp.mean(grad_normed * normed, axis=-1, keepdims=True)
        out_ref[i] = inverse * (grad_normed - both[:, channels:] - normed * mean_proj)
        return carry

    lax.fori_loop(0, pair_ref.shape[0], row, 0, unroll=8)

    @pl.when((pl.program_id(0) == pl.num_programs(0) - 1) & (place[0] == 1))
    def _():
        half = weight_grad_ref.shape[0] // 2
        total = weight_grad_ref[...]
        weight_grad_ref[...] = jnp.concatenate([total[half:], total[:half]], axis=0)


def pair_backward(first, count, block, out, pair, grads, gain, weight_t, deps, order):
    rows, length, channels = pair.shape
    heads = weight_t.shape[0]
    blocked = pl.BlockSpec((block, length, channels), lambda t, place: (first + t, 0, 0))
    ins = [(pair, blocked), (gain, spec(gain.shape)), (weight_t, spec(weight_t.shape))] + [
        (g, pl.BlockSpec((g.shape[0], block, length), lambda t, place: (0, first + t, 0))) for g in grads
    ]
    aliases = {}
    if out is not None:
        aliases = {1 + len(ins): 0}
        ins.append((out, pl.BlockSpec(memory_space=pl.ANY)))
    return call(
        "pair_backward",
        functools.partial(pair_backward_kernel, len(grads)),
        count,
        ins,
        [(pair.shape, F32, blocked), ((heads, channels), F32, spec((heads, channels)))],
        [pltpu.VMEM((block, heads, length), F32)],
        deps,
        order,
        LONG,
        aliases,
    )


def conditions(cond_ref, gain_ref, cond_w_ref, cond_b_ref, zero_w_ref, zero_b_ref, zero_gate_ref, factor_ref, shift_ref):
    cond = cond_ref[...]
    width = zero_gate_ref.shape[1]
    zero_gate_ref[...] = jax.nn.sigmoid(dot(cond, zero_w_ref[...]) + zero_b_ref[...])
    cond_normed, _ = layer_norm(cond.astype(F32))
    projected = dot((cond_normed * gain_ref[...]).astype(BF16), cond_w_ref[...])
    factor_ref[...] = jax.nn.sigmoid(projected[:, :width] + cond_b_ref[...])
    shift_ref[...] = projected[:, width:]


def conditions_back(cond_ref, gain_ref, cond_w_ref, zero_w_ref, zero_grad, projected):
    cond = cond_ref[...]
    cond_normed, cond_inverse = layer_norm(cond.astype(F32))
    scaled = (cond_normed * gain_ref[...]).astype(BF16)
    grad_scaled = dot(projected, cond_w_ref[...], 1, 1)
    return (
        dot(scaled, projected, 0, 0),
        dot(cond, zero_grad, 0, 0),
        column_sum(grad_scaled * cond_normed),
        dot(zero_grad, zero_w_ref[...], 1, 1),
        grad_scaled * gain_ref[...],
        cond_normed,
        cond_inverse,
    )


def step_rows(step, tokens):
    return pl.ds(pl.multiple_of(step * tokens, tokens), tokens)


def inputs_kernel(
    place, acts_ref, acts_other_ref, cot_ref, cot_other_ref,
    cond_ref, gain_ref, cond_w_ref, cond_b_ref, zero_w_ref, zero_b_ref,
    query_ref, key_ref, value_ref, gate_w_ref, q_bias_ref, out_w_ref,
    input_ref, gate_ref, gated_grad_ref, q_ref, k_ref, v_ref, g_ref, qt_ref, kt_ref, vt_ref, gt_ref,
    zero_gate_ref, factor_ref, shift_ref,
):
    step = pl.program_id(0)
    samples, tokens, half = gate_ref.shape
    width = acts_ref.shape[2]
    rows = samples * tokens

    @pl.when(step == 0)
    def _():
        conditions(
            cond_ref, gain_ref, cond_w_ref, cond_b_ref, zero_w_ref, zero_b_ref, zero_gate_ref, factor_ref, shift_ref
        )

    here = step_rows(step, tokens)
    acts = jnp.concatenate([acts_ref[...], acts_other_ref[...]], axis=0)
    normed, _ = layer_norm(acts.astype(F32))
    first = (factor_ref[here, :][None] * normed + shift_ref[here, :][None]).astype(BF16)
    input_ref[...] = first
    first = first.reshape(rows, width)
    cot = jnp.concatenate([cot_ref[...], cot_other_ref[...]], axis=0)
    grad_att = (cot.astype(F32) * zero_gate_ref[here, :][None]).astype(BF16)
    grad_gated = dot(grad_att.reshape(rows, width), out_w_ref[...], 1, 1)
    gated_grad_ref[...] = grad_gated.reshape(samples, tokens, half)
    gate = jax.nn.sigmoid(dot(first, gate_w_ref[...]))
    gate_ref[...] = gate.reshape(samples, tokens, half)

    def put(values, nat_ref, t_ref):
        low = values.astype(BF16).reshape(samples, tokens, half)
        chunks = nat_ref.shape[0]
        used = half // chunks
        for chunk in range(chunks):
            nat_ref[chunk, :, :, :used] = low[:, :, chunk * used : (chunk + 1) * used]
            nat_ref[chunk, :, :, used:] = jnp.zeros((samples, tokens, LANES - used), BF16)
        for s in range(samples):
            t_ref[s] = low[s].T

    put(grad_gated * gate, g_ref, gt_ref)
    put(dot(first, query_ref[...]) + q_bias_ref[...], q_ref, qt_ref)
    put(dot(first, key_ref[...]), k_ref, kt_ref)
    put(dot(first, value_ref[...]), v_ref, vt_ref)


def own(core):
    return core


def other(core):
    return 1 - core


def quarters(weight, whose):
    rows, columns = weight.shape
    return [
        (weight, spec((rows, columns // 8), at=(0, functools.partial(lambda j, core: 2 * j + whose(core), j))))
        for j in range(4)
    ]


def inputs_call(acts, acts_other, cot, cot_other, cond, branch, qkvg_w, q_bias, out_w, heads, deps, order):
    own_samples, length, width = acts.shape
    samples, half = 2 * own_samples, width // 2
    chunks = heads // 2 // CHUNK_HEADS
    block = spec((own_samples, TOKENS, width), 1)
    wide = spec((samples, TOKENS, width), 1)
    narrow = spec((samples, TOKENS, half), 1)
    nat = spec((chunks, samples, TOKENS, LANES), 2)
    turned = spec((samples, half, TOKENS), 2)
    return call(
        "inputs",
        inputs_kernel,
        length // TOKENS,
        [(a, block) for a in (acts, acts_other, cot, cot_other)]
        + [(cond, spec(cond.shape))]
        + branch
        + quarters(qkvg_w, own)
        + [(q_bias, spec((1, half), at=(0, own))), (out_w, spec((half, width), at=(own, 0)))],
        [
            ((samples, length, width), BF16, wide),
            ((samples, length, half), F32, narrow),
            ((samples, length, half), F32, narrow),
        ]
        + [((chunks, samples, length, LANES), BF16, nat)] * 4
        + [((samples, half, length), BF16, turned)] * 4
        + [((length, width), F32, spec((length, width)))] * 2,
        [pltpu.VMEM((length, width), F32)],
        deps,
        order,
    )


def transition_kernel(
    halving, place, acts_ref, cot_ref, cond_ref, gain_ref, cond_w_ref, cond_b_ref, zero_w_ref, zero_b_ref,
    swiglu_ref, down_ref,
    partial_ref, acts_grad_ref, cond_gate_ref, cond_norm_ref, packed_out, cond_b_out, zero_b_out, gain_out,
    swiglu_acc, down_acc, zero_gate_ref, factor_ref, shift_ref, zero_low, projected,
):
    step = pl.program_id(0)
    clear(step, swiglu_acc, down_acc, cond_b_out, zero_b_out)
    samples, tokens, width = acts_ref.shape
    rows = samples * tokens
    hidden_width = down_ref.shape[0]

    @pl.when(step == 0)
    def _():
        conditions(
            cond_ref, gain_ref, cond_w_ref, cond_b_ref, zero_w_ref, zero_b_ref, zero_gate_ref, factor_ref, shift_ref
        )

    here = step_rows(step, tokens)
    zero_gate = zero_gate_ref[here, :]
    factor = factor_ref[here, :]
    acts = acts_ref[...].astype(F32)
    normed, _ = layer_norm(acts)
    second = (factor[None] * normed + shift_ref[here, :][None]).astype(BF16).reshape(rows, width)
    grad_out = cot_ref[...].astype(F32)
    grad_tr = (grad_out * zero_gate[None]).astype(BF16).reshape(rows, width)
    transition = grad_input = 0.0
    second_t = second.T
    for at in range(0, hidden_width, HIDDEN):
        gate_at, up_at = slice(at, at + HIDDEN), slice(hidden_width + at, hidden_width + at + HIDDEN)
        gate_part = dot(second, swiglu_ref[:, gate_at])
        up_part = dot(second, swiglu_ref[:, up_at])
        gate_sig = jax.nn.sigmoid(gate_part)
        silu = gate_part * gate_sig
        product = (silu * up_part).astype(BF16)
        transition += dot(product, down_ref[gate_at, :])
        grad_product = dot(grad_tr, down_ref[gate_at, :], 1, 1)
        down_acc[gate_at, :] += dot(product, grad_tr, 0, 0)
        grad_up = (grad_product * silu).astype(BF16)
        grad_gate = (grad_product * up_part * gate_sig * (1.0 + gate_part * (1.0 - gate_sig))).astype(BF16)
        swiglu_acc[:, gate_at] += dot(second_t, grad_gate)
        swiglu_acc[:, up_at] += dot(second_t, grad_up)
        grad_input += dot(grad_gate, swiglu_ref[:, gate_at], 1, 1)
        grad_input += dot(grad_up, swiglu_ref[:, up_at], 1, 1)
    transition = transition.reshape(samples, tokens, width)
    grad_input = grad_input.reshape(samples, tokens, width)
    partial_ref[...] = acts + zero_gate[None] * transition
    grad_zero = jnp.sum(grad_out * transition, axis=0) * slope(zero_gate)
    zero_b_out[...] += column_sum(grad_zero)
    zero_low[here, :] = grad_zero.astype(BF16)
    grad_factor = jnp.sum(grad_input * normed, axis=0) * slope(factor)
    cond_b_out[...] += column_sum(grad_factor)
    projected[here, :width] = grad_factor.astype(BF16)
    projected[here, width:] = jnp.sum(grad_input, axis=0).astype(BF16)
    acts_grad_ref[...] = grad_input * factor[None]

    @pl.when(step == pl.num_programs(0) - 1)
    def _():
        cond_w_grad, zero_w_grad, gain_grad, cond_gate, cond_norm, _, _ = conditions_back(
            cond_ref, gain_ref, cond_w_ref, zero_w_ref, zero_low[...], projected[...]
        )
        gain_out[...] = gain_grad
        cond_gate_ref[...] = cond_gate
        cond_norm_ref[...] = cond_norm
        halving.pack(packed_out, [swiglu_acc, down_acc, cond_w_grad, zero_w_grad])


def transition_call(acts, cot, cond, branch, swiglu, down, halving, deps, order):
    samples, length, width = acts.shape
    cond_width = cond.shape[1]
    hidden = down.shape[0]
    rows = samples * length
    block = spec((samples, TOKENS, width), 1)
    weights = [(width, 2 * hidden), (hidden, width), (cond_width, 2 * width), (cond_width, width)]
    vectors = [(1, width), (1, width), (1, cond_width)]
    results = call(
        "transition",
        functools.partial(transition_kernel, halving),
        length // TOKENS,
        [(acts, block), (cot, block), (cond, spec(cond.shape))]
        + branch
        + [(swiglu, spec(swiglu.shape)), (down, spec(down.shape))],
        [(acts.shape, F32, block)] * 2
        + [(cond.shape, F32, spec(cond.shape))] * 2
        + [(halving.slabs(weights), BF16, spec(halving.slabs(weights)))]
        + [(s, F32, spec(s)) for s in vectors],
        [pltpu.VMEM(s, F32) for s in weights[:2]]
        + [pltpu.VMEM((length, width), F32)] * 3
        + [pltpu.VMEM((length, width), BF16), pltpu.VMEM((length, 2 * width), BF16)],
        deps,
        order,
    )
    return results, weights


def attention_kernel(
    halving, head_dim, place, q_ref, k_ref, v_ref, g_ref, qt_ref, kt_ref, vt_ref, gt_ref, bias_ref,
    mixed_ref, dq_ref, dkt_ref, dvt_ref, sent_ref, kept_ref, kz, vz, plow, dslow, dsum, dlow,
):
    h = pl.program_id(0)
    samples, length, wide = q_ref.shape
    scale = head_dim ** (-0.5)
    off = pl.multiple_of(h * head_dim, 16)
    lane = lax.broadcasted_iota(jnp.int32, (1, wide), 1)
    mask = ((lane >= off) & (lane < off + head_dim)).astype(BF16)

    @pl.when(h == 0)
    def _():
        mixed_ref[...] = jnp.zeros_like(mixed_ref)
        dq_ref[...] = jnp.zeros_like(dq_ref)

    kz[...] = jnp.zeros_like(kz)
    vz[...] = jnp.zeros_like(vz)
    for s in range(samples):
        kz[s, pl.ds(off, head_dim), :] = kt_ref[s]
        vz[s, pl.ds(off, head_dim), :] = vt_ref[s]
    parts, _, share, _ = bias_ref.shape
    if share % 16 == 0:
        bias = bias_ref[:, 0].reshape(length, length).astype(F32)
    else:
        bias = jnp.concatenate([bias_ref[p, 0].astype(F32) for p in range(parts)], axis=0)
    for s in range(samples):
        x = dot(q_ref[s], kz[s]) * scale + bias
        x = jnp.exp(x - jnp.max(x, axis=-1, keepdims=True))
        probs = x * (1.0 / jnp.sum(x, axis=-1, keepdims=True))
        low = probs.astype(BF16)
        plow[s % 2] = low
        mixed = dot(low, v_ref[s] * mask)
        mixed_ref[s] += mixed
        grad = g_ref[s]
        delta = jnp.sum(grad.astype(F32) * mixed, axis=-1, keepdims=True)
        grad_scores = probs * (dot(grad, vz[s]) - delta)
        grad_low = grad_scores.astype(BF16)
        dslow[s % 2] = grad_low
        total = grad_scores if s == 0 else dsum[...] + grad_scores
        if s < samples - 1:
            dsum[...] = total
        else:
            dlow[...] = total.astype(dlow.dtype)
            bit = halving.order[0][1]
            slabs = halving.places()[: sent_ref.shape[0] // 2]
            for ref, value in ((sent_ref, 1 - place[bit]), (kept_ref, place[bit])):
                for p, (dest, _) in enumerate(slabs):
                    for c in range(2):
                        at = (dest + c) * share + value * (share << bit)
                        ref[2 * p + c, 0] = dlow[pl.ds(pl.multiple_of(at, 16 if share % 16 == 0 else 8), share), :].astype(BF16)
        dq_ref[s] += dot(grad_low, k_ref[s] * mask) * scale
        dvt_ref[s] = dot(gt_ref[s], plow[s % 2]).astype(BF16)
        dkt_ref[s] = (dot(qt_ref[s], dslow[s % 2]) * scale).astype(BF16)


def attention_call(chunk, nats, turned, bias, head_dim, halving, deps, order):
    _, samples, length, wide = nats[0].shape
    parts, heads, share, _ = bias.shape
    nat = pl.BlockSpec((None, samples, length, wide), lambda h, core: (chunk, 0, 0, 0))
    turn = pl.BlockSpec((samples, head_dim, length), lambda h, core: (0, chunk * CHUNK_HEADS + h, 0))
    turn_out = pl.BlockSpec((samples, head_dim, length), lambda h, core: (0, h, 0))
    bias_in = pl.BlockSpec(
        (parts, 1, share, length), lambda h, core: (0, core[0] * (heads // 2) + chunk * CHUNK_HEADS + h, 0, 0)
    )
    bias_out = pl.BlockSpec((parts // 2, 1, share, length), lambda h, core: (0, h, 0, 0))
    aligned = share % 16 == 0
    held = pl.BlockSpec((samples, length, wide), lambda h, core: (0, 0, 0))
    return call(
        "attention",
        functools.partial(attention_kernel, halving, head_dim),
        CHUNK_HEADS,
        [(a, nat) for a in nats] + [(a, turn) for a in turned] + [(bias, bias_in)],
        [((samples, length, wide), F32, held)] * 2
        + [((samples, CHUNK_HEADS * head_dim, length), BF16, turn_out)] * 2
        + [((parts // 2, CHUNK_HEADS, share, length), BF16, bias_out)] * 2,
        [
            pltpu.VMEM((samples, wide, length), BF16),
            pltpu.VMEM((samples, wide, length), BF16),
            pltpu.VMEM((2, length, length), BF16),
            pltpu.VMEM((2, length, length), BF16),
            pltpu.VMEM((length, length), F32),
            pltpu.VMEM((length, length), BF16 if aligned else F32),
        ],
        deps,
        order,
        SHORT,
    )


def mixed_kernel(chunks, place, *refs):
    (gate_ref, gated_grad_ref), refs = refs[:2], refs[2:]
    mixed_refs, refs = refs[:chunks], refs[chunks:]
    dq_refs, refs = refs[:chunks], refs[chunks:]
    dkt_refs, refs = refs[:chunks], refs[chunks:]
    dvt_refs, refs = refs[:chunks], refs[chunks:]
    joined_refs, q_bias_out = refs[:2], refs[2]
    clear(pl.program_id(0), q_bias_out)
    samples, tokens, half = gate_ref.shape
    own_samples = samples // 2

    def join(refs):
        return jnp.concatenate([ref[:, :, : half // chunks] for ref in refs], axis=-1)

    def turn(turned_refs):
        joined = jnp.concatenate([ref[...] for ref in turned_refs], axis=1)
        return jnp.stack([joined[s].T for s in range(samples)], axis=0)

    mixed = join(mixed_refs)
    gate = gate_ref[...]
    gated = (gate * mixed).astype(BF16)
    grad_queries = join(dq_refs)
    q_bias_out[...] += column_sum(grad_queries)
    grad_gate = gated_grad_ref[...] * mixed * slope(gate)
    parts = [gated, grad_queries.astype(BF16), turn(dkt_refs), turn(dvt_refs), grad_gate.astype(BF16)]
    for i in range(2):
        here = slice(i * own_samples, (i + 1) * own_samples)
        for j, part in enumerate(parts):
            joined_refs[i][:, :, j * half : (j + 1) * half] = part[here]


def mixed_call(gate, gated_grad, mixeds, dqs, dkts, dvts, deps, order):
    samples, length, half = gate.shape
    chunks = len(mixeds)
    own_samples = samples // 2
    block = spec((samples, TOKENS, half), 1)
    window = spec((samples, TOKENS, LANES), 1)
    turned = spec((samples, half // chunks, TOKENS), 2)
    return call(
        "mixed",
        functools.partial(mixed_kernel, chunks),
        length // TOKENS,
        [(a, block) for a in (gate, gated_grad)]
        + [(a, window) for a in mixeds + dqs]
        + [(a, turned) for a in dkts + dvts],
        [((own_samples, length, 5 * half), BF16, spec((own_samples, TOKENS, 5 * half), 1))] * 2
        + [((1, half), F32, spec((1, half)))],
        [],
        deps,
        order,
    )


def qkvg_kernel(halving, place, first_ref, *refs):
    joined_refs, other_refs, packed_out = refs[:2], refs[2:4], refs[4]
    step = pl.program_id(0)
    samples, length, width = first_ref.shape
    rows = samples * length // 2
    half = joined_refs[0].shape[2]

    def both(pair):
        return jnp.concatenate([ref[...].reshape(rows, half) for ref in pair], axis=1)

    grad = dot(first_ref[: samples // 2].reshape(rows, width), both(joined_refs), 0, 0)
    grad += dot(first_ref[samples // 2 :].reshape(rows, width), both(other_refs), 0, 0)
    share = packed_out.shape[1] * halving.halves() // 4

    for block in range(4):

        @pl.when(step == block // 2)
        def _():
            column = block % 2 * half
            for p, (dest, part) in enumerate(halving.places()):
                piece = block - part * (4 // halving.halves())
                if 0 <= piece < 4 // halving.halves():
                    for c in range(2):
                        at = (dest + c) * share
                        packed_out[2 * p + c, piece * share : (piece + 1) * share] = grad[
                            at : at + share, column : column + half
                        ].astype(BF16)


def qkvg_call(first, joined, joined_other, halving, deps, order):
    samples, length, width = first.shape
    half = joined.shape[2] // 5
    share = width // halving.counts["sample"]
    slabs = (2 * 2 ** len(halving.order), 4 // halving.halves() * share, half)
    blocks = [
        pl.BlockSpec((samples // 2, length, half), lambda t, place, i=i: (0, 0, 1 + 2 * t + i)) for i in range(2)
    ]
    (packed,) = call(
        "qkvg_grad",
        functools.partial(qkvg_kernel, halving),
        2,
        [(first, spec(first.shape))] + [(a, b) for a in (joined, joined_other) for b in blocks],
        [(slabs, BF16, spec(slabs))],
        [],
        deps,
        order,
    )
    return packed


def outputs_kernel(place, acts_ref, cot_ref, partial_ref, acts_part_ref, zero_gate_ref, factor_ref, *refs):
    joined_refs, refs = refs[:2], refs[2:]
    out_w_refs, qkvg_refs, refs = refs[:2], (refs[2:6], refs[6:10]), refs[10:]
    block_ref, acts_grad_ref, projected_ref, zero_low_ref, cond_b_out, zero_b_out, out_out = refs
    clear(pl.program_id(0), cond_b_out, zero_b_out, out_out)
    samples, tokens, width = acts_ref.shape
    rows = samples * tokens
    half = width // 2
    zero_gate = zero_gate_ref[...]
    factor = factor_ref[...]
    normed, inverse = layer_norm(acts_ref[...].astype(F32))
    grad_out = cot_ref[...].astype(F32)
    grad_att = (grad_out * zero_gate[None]).astype(BF16).reshape(rows, width)
    attended = grad_input = 0.0
    for i, half_at in enumerate((place[0], 1 - place[0])):
        gated = joined_refs[i][:, :, :half].reshape(rows, half)
        attended += dot(gated, out_w_refs[i][...])
        out_out[pl.ds(pl.multiple_of(half_at * half, half), half), :] += dot(gated, grad_att, 0, 0)
        for j in range(4):
            grad_input += dot(
                joined_refs[i][:, :, (1 + j) * half : (2 + j) * half].reshape(rows, half), qkvg_refs[i][j][...], 1, 1
            )
    attended = attended.reshape(samples, tokens, width)
    grad_input = grad_input.reshape(samples, tokens, width)
    block_ref[...] = (partial_ref[...] + zero_gate[None] * attended).astype(BF16)
    grad_zero = jnp.sum(grad_out * attended, axis=0) * slope(zero_gate)
    zero_b_out[...] += column_sum(grad_zero)
    zero_low_ref[...] = grad_zero.astype(BF16)
    grad_factor = jnp.sum(grad_input * normed, axis=0) * slope(factor)
    cond_b_out[...] += column_sum(grad_factor)
    projected_ref[:, :width] = grad_factor.astype(BF16)
    projected_ref[:, width:] = jnp.sum(grad_input, axis=0).astype(BF16)
    acts_grad_ref[...] = (
        grad_out + norm_back(grad_input * factor[None] + acts_part_ref[...], normed, inverse)
    ).astype(BF16)


def outputs_call(acts, cot, partial, acts_part, zero_gate, factor, joineds, out_w, qkvg_w, deps, order):
    samples, length, width = acts.shape
    half = width // 2
    block = spec((samples, TOKENS, width), 1)
    tokens = spec((TOKENS, width), 0)
    return call(
        "outputs",
        outputs_kernel,
        length // TOKENS,
        [(a, block) for a in (acts, cot, partial, acts_part)]
        + [(zero_gate, tokens), (factor, tokens)]
        + [(a, spec((samples, TOKENS, 5 * half), 1)) for a in joineds]
        + [(out_w, spec((half, width), at=(whose, 0))) for whose in (own, other)]
        + quarters(qkvg_w, own)
        + quarters(qkvg_w, other),
        [
            (acts.shape, BF16, block),
            (acts.shape, BF16, block),
            ((length, 2 * width), BF16, spec((TOKENS, 2 * width), 0)),
            ((length, width), BF16, tokens),
        ]
        + [(s, F32, spec(s)) for s in ((1, width), (1, width), (width, width))],
        [],
        deps,
        order,
    )


def conditions_kernel(
    rest, vector_parts, place, cond_ref, gain_ref, cond_w_ref, zero_w_ref, zero_low_ref, projected_ref,
    cond_gate_in, cond_norm_in, out_w_grad_ref, *refs
):
    vector_refs, (packed_out,) = refs[:vector_parts], refs[vector_parts:]
    cond_w_grad, zero_w_grad, gain_grad, cond_gate, cond_norm, cond_normed, cond_inverse = conditions_back(
        cond_ref, gain_ref, cond_w_ref, zero_w_ref, zero_low_ref[...], projected_ref[...]
    )
    cond_grad = (
        cond_gate + cond_gate_in[...] + norm_back(cond_norm + cond_norm_in[...], cond_normed, cond_inverse)
    )
    vectors = [gain_grad] + [ref[...] for ref in vector_refs[:-1]]
    q_bias = vector_refs[-1][...]
    vectors += [jnp.where(place[0] == 0, q_bias, 0.0), jnp.where(place[0] == 1, q_bias, 0.0)]
    pieces = [v[:, at : at + PIECE] for v in vectors for at in range(0, v.shape[1], PIECE)]
    rest.pack(packed_out, [out_w_grad_ref[...], cond_w_grad, zero_w_grad, cond_grad], pieces)


def conditions_call(cond, branch, zero_w, zero_low, projected, cond_gate, cond_norm, out_w_grad, vectors, rest, deps, order):
    cond_width = cond.shape[1]
    width = zero_low.shape[1]
    weights = [out_w_grad.shape, (cond_width, 2 * width), (cond_width, width), cond.shape]
    count, rows, columns = rest.slabs(weights)
    rows += (sum(v.shape[1] for v in vectors) + cond_width + width // 2) // PIECE
    rows += -rows % 16
    fixed = (zero_low, projected, cond_gate, cond_norm, out_w_grad, *vectors)
    (packed,) = call(
        "conditions",
        functools.partial(conditions_kernel, rest, len(vectors)),
        1,
        [(cond, spec(cond.shape))] + branch[:2] + [zero_w] + [(a, spec(a.shape)) for a in fixed],
        [((count, rows, columns), BF16, spec((count, rows, columns)))],
        [],
        deps,
        order,
    )
    return packed, weights


def results_kernel(
    early_halving, rest_halving, early_shapes, rest_shapes, halves, place, *refs
):
    early_refs, refs = refs[:halves], refs[halves:]
    qkvg_refs, refs = refs[: 2 * halves], refs[2 * halves :]
    (rest_ref, rest_got_ref, pair_sum_ref, pair_wt_ref, pair_gain_ref), refs = refs[:5], refs[5:]
    (cond_ref, cond_w_ref, zero_w_ref, qkvg_ref, out_w_ref, swiglu_ref, down_ref), refs = refs[:7], refs[7:]
    gains_ref, cond_b_ref, zero_b_ref, q_bias_ref, pair_gain_out, pair_w_out = refs
    bits = place.shape[0] - 1
    device = sum(place[bit] << bit for bit in range(bits))

    def columns(ref, pieces):
        for c, piece in enumerate(pieces):
            ref[:, c * PIECE : (c + 1) * PIECE] = piece.astype(F32)

    early = [early_halving.unpack(ref[...].astype(F32), early_shapes) for ref in early_refs]
    swiglu, down, cond_w_one, zero_w_one = [sum(parts, []) for parts in zip(*early)]
    before = rest_ref[...].astype(F32)
    total = before + rest_got_ref[...].astype(F32)
    out_w, cond_w_zero, zero_w_zero, _ = rest_halving.unpack(total, rest_shapes)
    columns(swiglu_ref, swiglu)
    columns(down_ref, down)
    columns(cond_w_ref, cond_w_zero + cond_w_one)
    columns(zero_w_ref, zero_w_zero + zero_w_one)
    columns(out_w_ref, out_w)
    columns(cond_ref, rest_halving.unpack(before, rest_shapes)[3])
    parts = []
    for i in range(2):
        held = [ref[...].astype(F32) for ref in qkvg_refs[i * halves : (i + 1) * halves]]
        if halves == 2:
            first = place[bits] == 0
            held = [jnp.where(first, held[0], held[1]), jnp.where(first, held[1], held[0])]
        parts.append(jnp.concatenate(held, axis=0))
    first = place[0] == 0
    parts = [jnp.where(first, parts[0], parts[1]), jnp.where(first, parts[1], parts[0])]
    rows = parts[0].shape[0] // 4
    columns(qkvg_ref, [part[j * rows : (j + 1) * rows] for j in range(4) for part in parts])
    at = sum(r * c for r, c in map(rest_halving.pieces, rest_shapes))
    for ref in (gains_ref, cond_b_ref, zero_b_ref, q_bias_ref):
        size = ref.shape[1]
        count = size * rest_halving.counts["sample"] // PIECE
        value = 0.0
        for c in range(count):
            source = lax.broadcasted_iota(jnp.int32, (PIECE, size), 0) + c * PIECE
            target = lax.broadcasted_iota(jnp.int32, (PIECE, size), 1) + device * size
            chosen = (source == target).astype(F32)
            value += lax.dot_general(
                total[at + c : at + c + 1],
                chosen,
                (((1,), (0,)), ((), ())),
                precision=lax.Precision.HIGHEST,
                preferred_element_type=F32,
            )
        ref[...] = value
        at += count
    size, heads = pair_w_out.shape
    channels = pair_sum_ref.shape[1]
    source = lax.broadcasted_iota(jnp.int32, (channels, size), 0)
    target = lax.broadcasted_iota(jnp.int32, (channels, size), 1) + device * size
    chosen = (source == target).astype(F32)

    def choose(array):
        return lax.dot_general(
            chosen,
            array,
            (((0,), (1,)), ((), ())),
            precision=lax.Precision.HIGHEST,
            preferred_element_type=F32,
        )

    grad = choose(pair_sum_ref[...])
    pair_w_out[...] = grad
    weighted = grad * choose(pair_wt_ref[...].astype(F32))

    def across(left, right, right_dim):
        return lax.dot_general(
            left,
            right,
            (((1,), (right_dim,)), ((), ())),
            precision=lax.Precision.HIGHEST,
            preferred_element_type=F32,
        )

    pair_gain_out[...] = across(jnp.ones((1, heads), F32), weighted, 1) / across(pair_gain_ref[...], chosen, 0)


def results_call(
    early, early_halving, early_shapes, qkvg, rest, rest_got, rest_halving, rest_shapes, pair_sum, pair_wt, pair_gain, order
):
    count = rest_halving.counts["sample"]
    heads, channels = pair_wt.shape
    swiglu, down, cond_w, zero_w = early_shapes
    out_w, _, _, cond = rest_shapes
    width = out_w[1]
    arrays = [cond, (cond_w[0], 2 * cond_w[1]), (zero_w[0], 2 * zero_w[1]), (width, 4 * width), out_w, swiglu, down]
    shapes = [(rows // count, columns) for rows, columns in arrays]
    shapes += [(1, size // count) for size in (2 * cond[1], 2 * width, 2 * width, width)]
    shapes += [(1, channels // count), (channels // count, heads)]
    ins = [*early, *qkvg, rest, rest_got, pair_sum, pair_wt, pair_gain]
    return call(
        "results",
        functools.partial(
            results_kernel, early_halving, rest_halving, early_shapes, rest_shapes, early_halving.halves()
        ),
        1,
        [(a, spec(a.shape)) for a in ins],
        [(shape, F32, spec(shape)) for shape in shapes],
        [],
        [],
        order,
    )


def body(
    struct_count, sample_devices,
    acts, cond, pair, lengths, token_mask, cond_gains, cond_w, cond_bias, output_gate_weights, zero_bias,
    qkvg_w, q_bias, out_w, swiglu_w, down_w, pair_gain, pair_w, cotangent,
):
    acts, cond, pair, cotangent = acts[0], cond[0], pair[0], cotangent[0]
    samples, length, width = acts.shape
    cond_width = cond.shape[1]
    heads = pair_w.shape[1]
    head_dim = width // heads
    chunks = heads // 2 // CHUNK_HEADS
    counts = {"struct": struct_count, "sample": sample_devices}
    bits = sample_devices.bit_length() - 1
    pair_wt = pair_w.T
    device = lax.axis_index("sample")
    core = device & 1
    place = [(device >> bit) & 1 for bit in range(bits)] + [lax.axis_index("struct")]
    order = Order(jnp.stack(place).astype(jnp.int32))

    def swap(array):
        return lax.ppermute(array, "sample", [(i, i ^ 1) for i in range(sample_devices)])

    acts_other, cotangent_other = swap(acts), swap(cotangent)

    bias_rows = pair_forward(pair, pair_gain[None], pair_wt, token_mask, lengths, Order(jnp.zeros(bits + 1, jnp.int32)))
    bias = lax.all_gather(bias_rows, "sample", axis=0, tiled=False)

    rows = {}
    at = 0
    packed = [
        ("gain", cond_gains), ("cond_b", cond_bias), ("zero_b", zero_bias), ("q_bias", q_bias), ("pair", pair_gain)
    ]
    vector = jnp.concatenate([v for _, v in packed]).astype(F32)[None]
    for name, v in packed:
        rows[name] = vector[:, at : at + v.shape[0]]
        at += v.shape[0]

    def conditioning(b):
        return [
            (rows["gain"], spec((1, cond_width), at=(0, b))),
            (cond_w, spec((cond_width, 2 * width), at=(0, b))),
            (rows["cond_b"], spec((1, width), at=(0, b))),
        ]

    def zero(b):
        return [
            (output_gate_weights, spec((cond_width, width), at=(0, b))),
            (rows["zero_b"], spec((1, width), at=(0, b))),
        ]

    def path(*order):
        steps = [("struct", 0) if o == "y" else ("sample", o) for o in order]
        steps = [s for s in steps if s[0] == "sample" or struct_count == 2]
        return Halving(steps + [("sample", b) for b in range(4, bits)], counts)

    along_x = path(0, 1, 2, 3)
    along_y = path(0, "y", 2, 3, 1)
    chip_x = path(1, 2, 3)
    chip_y = path("y", 2, 3, 1)
    results, early_shapes = transition_call(
        acts, cotangent, cond, conditioning(1) + zero(1), swiglu_w, down_w, along_y, [], order
    )
    partial, acts_part, cond_gate, cond_norm, early, cond_b_one, zero_b_one, gain_one = results
    early = Running(along_y.run(early))
    first, gate, gated_grad, *rest = inputs_call(
        acts, acts_other, cotangent, cotangent_other, cond, conditioning(0) + zero(0), qkvg_w, rows["q_bias"], out_w,
        heads, [], order,
    )
    nats, turned, (zero_gate, factor) = rest[:4], rest[4:8], rest[8:]

    mixeds, dqs, dkts, dvts, bias_sums = [], [], [], [], []
    deps = advance(order, early)
    for chunk in range(chunks):
        mixed, dq, dkt, dvt, sent, kept = attention_call(chunk, nats, turned, bias, head_dim, chip_x, deps, order)
        mixeds.append(mixed)
        dqs.append(dq)
        dkts.append(dkt)
        dvts.append(dvt)
        deps = advance(order, *bias_sums, *([early] if chunk % 2 else []))
        bias_sums.append(Running(chip_x.run(kept, "swap", sent)))

    joined, joined_sent, q_bias_grad = mixed_call(
        gate, gated_grad, mixeds, dqs, dkts, dvts, deps, order
    )
    joined_got = swap(joined_sent)
    qkvg_sum = Running(
        chip_y.run(qkvg_call(first, joined, joined_sent, chip_y, [], order), "cores")
    )
    deps = advance(order, *bias_sums, qkvg_sum)
    block_out, acts_grad, projected, zero_low, cond_b_zero, zero_b_zero, out_grad = outputs_call(
        acts, cotangent, partial, acts_part, zero_gate, factor, [joined, joined_got],
        out_w, qkvg_w, deps, order,
    )
    deps = advance(order, *bias_sums, qkvg_sum, early)
    rest, rest_shapes = conditions_call(
        cond, conditioning(0), zero(0)[0], zero_low, projected, cond_gate, cond_norm, out_grad,
        [gain_one, cond_b_zero, cond_b_one, zero_b_zero, zero_b_one, q_bias_grad], along_x, deps, order,
    )
    rest = Running(along_x.run(rest, ""))
    while any(b.result is None for b in bias_sums):
        advance(order, *bias_sums)
    share = length // sample_devices
    block = 16 if share % 16 == 0 else share
    turned_wt = jnp.where(core == 0, pair_wt, jnp.roll(pair_wt, heads // 2, axis=0))
    grads = [b.result[0] for b in bias_sums] + [b.result[1] for b in bias_sums]
    grad_pair, part = pair_backward(0, 1, block, None, pair, grads, rows["pair"], turned_wt, [], order)
    pair_parts = [part]
    if share > block:
        deps = advance(order, qkvg_sum, rest, early)
        grad_pair, part = pair_backward(
            1, share // block - 1, block, grad_pair, pair, grads, rows["pair"], turned_wt, deps, order
        )
        pair_parts.append(part)
    struct_bits = struct_count.bit_length() - 1

    def summed(array, *masks):
        found = [
            lax.ppermute(array, ("struct", "sample"), [(i, i ^ mask) for i in range(struct_count * sample_devices)])
            for mask in masks
        ]
        if len(found) == 1:
            return array + found[0]
        return (array + found[0]) + (found[1] + found[2])

    class Pair:
        asked = [[(p, p.shape[0], lambda place: 0, True) for p in pair_parts]]
        result = None

        def send(self, found):
            self.result = found[0]

    pair_grad = Pair()
    advance(order, pair_grad, qkvg_sum, rest, early)
    left = [bits + struct_bits - 1] + list(range(bits + struct_bits - 1)) if struct_bits else list(range(bits))
    pair_sum = pair_grad.result
    while left:
        one = 1 << left.pop(0)
        two = 1 << left.pop(0) if left else 0
        pair_sum = summed(pair_sum, one, two, one | two) if two else summed(pair_sum, one)
    chains = (qkvg_sum, rest, early)
    while any(r.result is None for r in chains):
        advance(order, *chains, near=True)
    mine_qkvg, sent = qkvg_sum.result
    if chip_y.halves() == 2:
        across = [
            (s * sample_devices + i, (1 - s) * sample_devices + (i ^ 1))
            for s in range(2)
            for i in range(sample_devices)
        ]
        from_y = lax.ppermute(mine_qkvg, "struct", [(0, 1), (1, 0)])
        from_both = lax.ppermute(sent, ("struct", "sample"), across)
        qkvg = [mine_qkvg, from_y, swap(sent), from_both]
    else:
        for bit in range(struct_bits):
            mine_qkvg, sent = [summed(part, 1 << (bits + bit)) for part in (mine_qkvg, sent)]
        qkvg = [mine_qkvg, swap(sent)]
    early = list(early.result) if along_y.halves() == 2 else [early.result]
    rest_sum, rest_got = rest.result, jnp.zeros_like(rest.result)
    for bit in range(struct_bits):
        if bit:
            rest_sum = rest_sum + rest_got
        rest_got = lax.ppermute(
            rest_sum, "struct", [(i, i ^ (1 << bit)) for i in range(struct_count)]
        )
    (cond_sum, cond_w_sum, zero_w_sum, qkvg_total, out_sum, swiglu_sum, down_sum,
     gains, cond_b, zero_b, q_b, pair_g, pair_w_sum) = results_call(
        early, along_y, early_shapes, qkvg, rest_sum, rest_got, along_x, rest_shapes, pair_sum, pair_wt, rows["pair"], order
    )
    if struct_bits > 1:
        cond_sum = along_x.unpack(rest.result, rest_shapes)[3][0].astype(F32)
    return (
        block_out[None], acts_grad[None], cond_sum[None], grad_pair[None], gains[0], cond_w_sum, cond_b[0], zero_w_sum,
        zero_b[0], qkvg_total, q_b[0], out_sum, swiglu_sum, down_sum, pair_g[0], pair_w_sum,
    )


def solution(mesh):
    per_struct = P("struct", "sample", None, None)
    in_specs = (
        (per_struct, P("struct", None, None), per_struct, P("struct"), P("struct", None))
        + (P(),) * 12
        + (per_struct,)
    )
    one, two = P("sample"), P("sample", None)
    out_specs = (
        per_struct, per_struct, P("struct", "sample", None), per_struct,
        one, two, one, two, one, two, one, two, two, two, one, two,
    )
    local = functools.partial(body, mesh.shape["struct"], mesh.shape["sample"])
    return jax.shard_map(local, mesh=mesh, in_specs=in_specs, out_specs=out_specs, check_vma=False)
```

```python
import functools

import jax
import jax.numpy as jnp
from jax import lax
from jax.experimental import pallas as pl
from jax.experimental.pallas import tpu as pltpu
from jax.sharding import PartitionSpec as P

EPS = 1e-05
MASKED = -1000000000.0
F32 = jnp.float32
BF16 = jnp.bfloat16
CHUNK_HEADS = 2
LANES = 128
PIECE = 384
LONG, SHORT = 10**11, 17 * 10**9
TOKENS = 128
HIDDEN = 768
VMEM_LIMIT = 64 * 2**20 - 2**17


def dot(left, right, left_dim=1, right_dim=0):
    return lax.dot_general(
        left, right, (((left_dim,), (right_dim,)), ((), ())), preferred_element_type=F32
    )


def layer_norm(values):
    center = values - jnp.mean(values, axis=-1, keepdims=True)
    inverse = lax.rsqrt(jnp.mean(center * center, axis=-1, keepdims=True) + EPS)
    return (center * inverse, inverse)


def norm_back(grad_in, normed, inverse):
    mean_grad = jnp.mean(grad_in, axis=-1, keepdims=True)
    mean_proj = jnp.mean(grad_in * normed, axis=-1, keepdims=True)
    return inverse * (grad_in - mean_grad - normed * mean_proj)


def slope(gate):
    return gate * (1.0 - gate)


def column_sum(values):
    return jnp.sum(values.reshape(-1, values.shape[-1]), axis=0, keepdims=True)


def clear(step, *refs):
    @pl.when(step == 0)
    def _():
        for ref in refs:
            ref[...] = jnp.zeros_like(ref)


def spec(block, along=None, at=None):
    rank = len(block)
    if along is not None:
        return pl.BlockSpec(block, lambda t, core: tuple(t if a == along else 0 for a in range(rank)))
    index = (0,) * rank if at is None else at
    return pl.BlockSpec(
        block,
        lambda t, core: tuple(i(core[0]) if callable(i) else i for i in index),
        pipeline_mode=pl.Buffered(1),
    )


class Order:
    def __init__(self, place):
        self.place = place
        self.last = []


def call(name, kernel, grid, ins, outs, scratch, deps, order, flops=LONG, aliases={}, vmem=VMEM_LIMIT):
    inputs = len(ins)
    deps = list(deps) + order.last

    def run(place_ref, *refs):
        kernel(place_ref, *refs[:inputs], *refs[inputs + len(deps) :])

    found = pl.pallas_call(
        run,
        grid_spec=pltpu.PrefetchScalarGridSpec(
            num_scalar_prefetch=1,
            grid=(grid,),
            in_specs=[s for _, s in ins] + [pl.BlockSpec(memory_space=pl.ANY)] * len(deps),
            out_specs=[s for _, _, s in outs],
            scratch_shapes=scratch,
        ),
        out_shape=[jax.ShapeDtypeStruct(shape, dtype) for shape, dtype, _ in outs],
        compiler_params=pltpu.CompilerParams(
            vmem_limit_bytes=vmem, dimension_semantics=("arbitrary",)
        ),
        cost_estimate=pl.CostEstimate(flops=flops, bytes_accessed=10**6, transcendentals=0),
        name=name,
        input_output_aliases=aliases,
    )(order.place, *[a for a, _ in ins], *deps)
    order.last = [max(found, key=lambda array: array.size)]
    return found


def combine(outputs, order, near=False):
    held = pl.BlockSpec(memory_space=pltpu.VMEM)
    ins, outs, plan = [], [], []
    for terms in outputs:
        if isinstance(terms, tuple):
            bit, *arrays = terms
            terms = [(array, array.shape[0], lambda place: 0, True) for array in arrays]
        else:
            bit = None
        array, slabs = terms[0][:2]
        shape = (slabs,) + array.shape[1:]
        rest = (0,) * (len(shape) - 1)
        sources = []
        for term, _, index, small in terms:
            if near and small:
                sources.append((len(ins), index, slabs))
                ins.append((term, held))
            else:
                sources.append((len(ins), None, slabs))
                ins.append(
                    (term, pl.BlockSpec(shape, lambda t, place, index=index, rest=rest: (index(place),) + rest))
                )
        plan.append((bit, sources))
        blocked = pl.BlockSpec(shape, lambda t, place, rank=len(shape): (0,) * rank)
        outs.append((shape, array.dtype, held if near else blocked))

    def kernel(place, *refs):
        for (bit, sources), out_ref in zip(plan, refs[len(ins) :]):
            values = [
                refs[i][...] if index is None else refs[i][pl.ds(index(place) * slabs, slabs)]
                for i, index, slabs in sources
            ]
            if bit is not None:
                out_ref[...] = jnp.where(place[bit] == 0, values[0], values[1])
            elif len(values) == 1:
                out_ref[...] = values[0]
            else:
                total = sum((v.astype(F32) for v in values[1:]), values[0].astype(F32))
                out_ref[...] = total.astype(out_ref.dtype)

    return call("combine", kernel, 1, ins, outs, [], [], order, vmem=16 * 2**20 if near else VMEM_LIMIT)


class Halving:
    def __init__(self, order, counts):
        self.order = order
        self.counts = counts

    def places(self):
        found = []
        for p in range(2 ** len(self.order)):
            dest, half = 0, 0
            for i, (axis, bit) in enumerate(self.order):
                value = (p >> (len(self.order) - 1 - i)) & 1
                if axis == "sample":
                    dest |= value << bit
                else:
                    half = value
            found.append((dest, half))
        return found

    def halves(self):
        return 2 if any(axis == "struct" for axis, _ in self.order) else 1

    def pieces(self, shape):
        rows, columns = shape
        return rows // self.counts["sample"], columns // self.halves() // PIECE

    def slabs(self, shapes):
        return (2 ** len(self.order), sum(r * c for r, c in map(self.pieces, shapes)), PIECE)

    def pack(self, out_ref, arrays, everywhere=()):
        for p, (dest, half) in enumerate(self.places()):
            held = []
            for array in arrays:
                rows, count = self.pieces(array.shape)
                for c in range(count):
                    at = (half * count + c) * PIECE
                    held.append(array[dest * rows : (dest + 1) * rows, at : at + PIECE])
            slab = jnp.concatenate(held + list(everywhere), axis=0)
            out_ref[p, : slab.shape[0]] = slab.astype(out_ref.dtype)
            if slab.shape[0] < out_ref.shape[1]:
                out_ref[p, slab.shape[0] :] = jnp.zeros(
                    (out_ref.shape[1] - slab.shape[0], PIECE), out_ref.dtype
                )

    def unpack(self, slab, shapes):
        found, at = [], 0
        for shape in shapes:
            rows, count = self.pieces(shape)
            found.append([slab[at + c * rows : at + (c + 1) * rows] for c in range(count)])
            at += rows * count
        return found

    def run(self, array, after="sum", sent=None):
        last = self.counts["sample"].bit_length() - 1

        def exchange(array, axis, bit):
            return lax.ppermute(array, axis, [(i, i ^ (1 << bit)) for i in range(self.counts[axis])])

        def halves(at, size):
            return [
                [
                    (p, size, lambda place, base=base, at=at, flip=flip: 2 * base(place) + (place[at] ^ flip), held)
                    for p, base, held in parts
                ]
                for flip in (1, 0)
            ]

        zero = lambda place: 0
        parts, size = [(array, zero, False)], array.shape[0]
        order = self.order
        if sent is not None:
            parts.append((exchange(sent, *order[0]), zero, False))
            order = order[1:]
        for axis, bit in order:
            at = bit if axis == "sample" else last
            size = size // 2
            if len(parts) == 1 and (axis, bit) == ("sample", 0):
                first = lambda place: place[0]
                parts = [(array, first, False), (exchange(array, axis, bit), first, False)]
                continue
            if len(parts) == 1:
                (sent,) = yield halves(at, size)[:1]
                parts = [(array, lambda place, at=at: place[at], False), (exchange(sent, axis, bit), zero, True)]
            else:
                sent, kept = yield halves(at, size)
                parts = [(kept, zero, True), (exchange(sent, axis, bit), zero, True)]
        if after in ("swap", "cores"):
            sent, kept = yield halves(0, size // 2)
            return kept[0], exchange(sent, "sample", 0)[0] if after == "swap" else sent[0]
        (held,) = yield [[(p, 1, base, near) for p, base, near in parts]]
        if not after:
            return held[0]
        if self.halves() == 2:
            received = exchange(held, "struct", 0)
            first, second = yield [(last, held, received), (last, received, held)]
            return first[0], second[0]
        for bit in range(self.counts["struct"].bit_length() - 1):
            received = exchange(held, "struct", bit)
            (held,) = yield [[(p, 1, zero, True) for p in (held, received)]]
        return held[0]

class Running:
    def __init__(self, steps):
        self.steps = steps
        self.result = None
        self.send(None)

    def send(self, found):
        try:
            self.asked = self.steps.send(found)
        except StopIteration as stop:
            self.asked = []
            self.result = stop.value


def advance(order, *running, near=False):
    running = [r for r in running if r.result is None]
    asked = [output for r in running for output in r.asked]
    if not asked:
        return []
    made = combine(asked, order, near)
    at = 0
    for r in running:
        count = len(r.asked)
        r.send(made[at : at + count])
        at += count
    return made


def pair_forward_kernel(place, pair_ref, gain_ref, weight_ref, mask_ref, lengths_ref, out_ref, terms):
    gain = gain_ref[...].astype(F32)
    rows, length, channels = pair_ref.shape
    average = jnp.full((channels, channels), 1.0 / channels, BF16)
    position = lax.broadcasted_iota(jnp.int32, (1, length), 1)
    valid = (position < lengths_ref[0]) & ((mask_ref[...] == 1) | (position == 0))
    for i in range(rows):
        values = pair_ref[i]
        center = values.astype(F32) - dot(values, average)
        inverse = lax.rsqrt(jnp.mean(center * center, axis=-1, keepdims=True) + EPS)
        affine = (center * inverse * gain).astype(BF16)
        terms[i] = jnp.where(valid, dot(weight_ref[...], affine, 1, 1), MASKED)
    for h in range(terms.shape[1]):
        out_ref[h] = terms[:, h, :].astype(BF16)


def pair_forward(pair, gain, weight_t, mask, lengths, order):
    rows, length, channels = pair.shape
    heads = weight_t.shape[0]
    block = 16 if rows % 16 == 0 else rows
    return call(
        "pair_forward",
        pair_forward_kernel,
        rows // block,
        [
            (pair, spec((block, length, channels), 0)),
            (gain, spec(gain.shape)),
            (weight_t, spec(weight_t.shape)),
            (mask, spec(mask.shape)),
            (lengths, pl.BlockSpec(memory_space=pltpu.SMEM)),
        ],
        [((heads, rows, length), BF16, spec((heads, block, length), 1))],
        [pltpu.VMEM((block, heads, length), F32)],
        [],
        order,
    )[0]


def pair_backward_kernel(chunks, first, place, pair_ref, gain_ref, weight_ref, *refs):
    grad_refs, (out_ref, weight_grad_ref, grads) = refs[:chunks], refs[-3:]
    gain = gain_ref[...]
    channels = pair_ref.shape[2]
    average = jnp.full((channels, channels), 1.0 / channels, BF16)
    clear(pl.program_id(0), weight_grad_ref)
    step = pl.program_id(0)
    rows = pair_ref.shape[0]

    @pl.when(step == 0)
    def _():
        head = 0
        for ref in grad_refs:
            for h in range(ref.shape[0]):
                grads[:, head, :] = ref[h, first : first + grads.shape[0]].astype(F32)
                head += 1

    scaled = weight_ref[...].astype(F32) * gain
    means = jnp.broadcast_to(jnp.mean(scaled, axis=-1, keepdims=True), scaled.shape)
    full = jnp.concatenate([scaled, means], axis=1)
    high = full.astype(BF16)
    parts = jnp.concatenate([high, (full - high.astype(F32)).astype(BF16)], axis=0)

    def row(i, carry):
        values = pair_ref[i]
        center = values.astype(F32) - dot(values, average)
        inverse = lax.rsqrt(jnp.mean(center * center, axis=-1, keepdims=True) + EPS)
        normed = center * inverse
        grad = grads[step * rows + i].astype(BF16)
        weight_grad_ref[...] += dot(grad, (normed * gain).astype(BF16))
        both = dot(jnp.concatenate([grad, grad], axis=0), parts, 0, 0)
        grad_normed = both[:, :channels]
        mean_proj = jnp.mean(grad_normed * normed, axis=-1, keepdims=True)
        out_ref[i] = inverse * (grad_normed - both[:, channels:] - normed * mean_proj)
        return carry

    lax.fori_loop(0, pair_ref.shape[0], row, 0, unroll=8)

    @pl.when((pl.program_id(0) == pl.num_programs(0) - 1) & (place[0] == 1))
    def _():
        half = weight_grad_ref.shape[0] // 2
        total = weight_grad_ref[...]
        weight_grad_ref[...] = jnp.concatenate([total[half:], total[:half]], axis=0)


def pair_backward(first, count, out, pair, grads, gain, weight_t, deps, order):
    rows, length, channels = pair.shape
    heads = weight_t.shape[0]
    block = 8
    blocked = pl.BlockSpec((block, length, channels), lambda t, place: (first // block + t, 0, 0))
    ins = [(pair, blocked), (gain, spec(gain.shape)), (weight_t, spec(weight_t.shape))]
    ins += [(g, spec(g.shape)) for g in grads]
    aliases = {}
    if out is not None:
        aliases = {1 + len(ins): 0}
        ins.append((out, pl.BlockSpec(memory_space=pl.ANY)))
    return call(
        "pair_backward",
        functools.partial(pair_backward_kernel, len(grads), first),
        count // block,
        ins,
        [(pair.shape, F32, blocked), ((heads, channels), F32, spec((heads, channels)))],
        [pltpu.VMEM((count, heads, length), F32)],
        deps,
        order,
        LONG,
        aliases,
    )


def conditions(cond_ref, gain_ref, cond_w_ref, cond_b_ref, zero_w_ref, zero_b_ref, zero_gate_ref, factor_ref, shift_ref):
    cond = cond_ref[...]
    width = zero_gate_ref.shape[1]
    zero_gate_ref[...] = jax.nn.sigmoid(dot(cond, zero_w_ref[...]) + zero_b_ref[...])
    cond_normed, _ = layer_norm(cond.astype(F32))
    projected = dot((cond_normed * gain_ref[...]).astype(BF16), cond_w_ref[...])
    factor_ref[...] = jax.nn.sigmoid(projected[:, :width] + cond_b_ref[...])
    shift_ref[...] = projected[:, width:]


def conditions_back(cond_ref, gain_ref, cond_w_ref, zero_w_ref, zero_grad, projected):
    cond = cond_ref[...]
    cond_normed, cond_inverse = layer_norm(cond.astype(F32))
    scaled = (cond_normed * gain_ref[...]).astype(BF16)
    grad_scaled = dot(projected, cond_w_ref[...], 1, 1)
    return (
        dot(scaled, projected, 0, 0),
        dot(cond, zero_grad, 0, 0),
        column_sum(grad_scaled * cond_normed),
        dot(zero_grad, zero_w_ref[...], 1, 1),
        grad_scaled * gain_ref[...],
        cond_normed,
        cond_inverse,
    )


def step_rows(step, tokens):
    return pl.ds(pl.multiple_of(step * tokens, tokens), tokens)


def inputs_kernel(
    place, acts_ref, acts_other_ref, cot_ref, cot_other_ref,
    cond_ref, gain_ref, cond_w_ref, cond_b_ref, zero_w_ref, zero_b_ref,
    query_ref, key_ref, value_ref, gate_w_ref, q_bias_ref, out_w_ref,
    input_ref, gate_ref, gated_grad_ref, q_ref, k_ref, v_ref, g_ref, qt_ref, kt_ref, vt_ref, gt_ref,
    zero_gate_ref, factor_ref, shift_ref,
):
    step = pl.program_id(0)
    samples, tokens, half = gate_ref.shape
    width = acts_ref.shape[2]
    rows = samples * tokens

    @pl.when(step == 0)
    def _():
        conditions(
            cond_ref, gain_ref, cond_w_ref, cond_b_ref, zero_w_ref, zero_b_ref, zero_gate_ref, factor_ref, shift_ref
        )

    here = step_rows(step, tokens)
    acts = jnp.concatenate([acts_ref[...], acts_other_ref[...]], axis=0)
    normed, _ = layer_norm(acts.astype(F32))
    first = (factor_ref[here, :][None] * normed + shift_ref[here, :][None]).astype(BF16)
    input_ref[...] = first
    first = first.reshape(rows, width)
    cot = jnp.concatenate([cot_ref[...], cot_other_ref[...]], axis=0)
    grad_att = (cot.astype(F32) * zero_gate_ref[here, :][None]).astype(BF16)
    grad_gated = dot(grad_att.reshape(rows, width), out_w_ref[...], 1, 1)
    gated_grad_ref[...] = grad_gated.reshape(samples, tokens, half)
    gate = jax.nn.sigmoid(dot(first, gate_w_ref[...]))
    gate_ref[...] = gate.reshape(samples, tokens, half)

    def put(values, nat_ref, t_ref):
        low = values.astype(BF16).reshape(samples, tokens, half)
        chunks = nat_ref.shape[0]
        used = half // chunks
        for chunk in range(chunks):
            nat_ref[chunk, :, :, :used] = low[:, :, chunk * used : (chunk + 1) * used]
            nat_ref[chunk, :, :, used:] = jnp.zeros((samples, tokens, LANES - used), BF16)
        for s in range(samples):
            t_ref[s] = low[s].T

    put(grad_gated * gate, g_ref, gt_ref)
    put(dot(first, query_ref[...]) + q_bias_ref[...], q_ref, qt_ref)
    put(dot(first, key_ref[...]), k_ref, kt_ref)
    put(dot(first, value_ref[...]), v_ref, vt_ref)


def own(core):
    return core


def other(core):
    return 1 - core


def quarters(weight, whose):
    rows, columns = weight.shape
    return [
        (weight, spec((rows, columns // 8), at=(0, functools.partial(lambda j, core: 2 * j + whose(core), j))))
        for j in range(4)
    ]


def inputs_call(acts, acts_other, cot, cot_other, cond, branch, qkvg_w, q_bias, out_w, heads, deps, order):
    own_samples, length, width = acts.shape
    samples, half = 2 * own_samples, width // 2
    chunks = heads // 2 // CHUNK_HEADS
    block = spec((own_samples, TOKENS, width), 1)
    wide = spec((samples, TOKENS, width), 1)
    narrow = spec((samples, TOKENS, half), 1)
    nat = spec((chunks, samples, TOKENS, LANES), 2)
    turned = spec((samples, half, TOKENS), 2)
    return call(
        "inputs",
        inputs_kernel,
        length // TOKENS,
        [(a, block) for a in (acts, acts_other, cot, cot_other)]
        + [(cond, spec(cond.shape))]
        + branch
        + quarters(qkvg_w, own)
        + [(q_bias, spec((1, half), at=(0, own))), (out_w, spec((half, width), at=(own, 0)))],
        [
            ((samples, length, width), BF16, wide),
            ((samples, length, half), F32, narrow),
            ((samples, length, half), F32, narrow),
        ]
        + [((chunks, samples, length, LANES), BF16, nat)] * 4
        + [((samples, half, length), BF16, turned)] * 4
        + [((length, width), F32, spec((length, width)))] * 2,
        [pltpu.VMEM((length, width), F32)],
        deps,
        order,
    )


def transition_kernel(
    halving, place, acts_ref, cot_ref, cond_ref, gain_ref, cond_w_ref, cond_b_ref, zero_w_ref, zero_b_ref,
    swiglu_ref, down_ref,
    partial_ref, acts_grad_ref, cond_gate_ref, cond_norm_ref, packed_out, cond_b_out, zero_b_out, gain_out,
    swiglu_acc, down_acc, zero_gate_ref, factor_ref, shift_ref, zero_low, projected,
):
    step = pl.program_id(0)
    clear(step, swiglu_acc, down_acc, cond_b_out, zero_b_out)
    samples, tokens, width = acts_ref.shape
    rows = samples * tokens
    hidden_width = down_ref.shape[0]

    @pl.when(step == 0)
    def _():
        conditions(
            cond_ref, gain_ref, cond_w_ref, cond_b_ref, zero_w_ref, zero_b_ref, zero_gate_ref, factor_ref, shift_ref
        )

    here = step_rows(step, tokens)
    zero_gate = zero_gate_ref[here, :]
    factor = factor_ref[here, :]
    acts = acts_ref[...].astype(F32)
    normed, _ = layer_norm(acts)
    second = (factor[None] * normed + shift_ref[here, :][None]).astype(BF16).reshape(rows, width)
    grad_out = cot_ref[...].astype(F32)
    grad_tr = (grad_out * zero_gate[None]).astype(BF16).reshape(rows, width)
    transition = grad_input = 0.0
    second_t = second.T
    for at in range(0, hidden_width, HIDDEN):
        gate_at, up_at = slice(at, at + HIDDEN), slice(hidden_width + at, hidden_width + at + HIDDEN)
        gate_part = dot(second, swiglu_ref[:, gate_at])
        up_part = dot(second, swiglu_ref[:, up_at])
        gate_sig = jax.nn.sigmoid(gate_part)
        silu = gate_part * gate_sig
        product = (silu * up_part).astype(BF16)
        transition += dot(product, down_ref[gate_at, :])
        grad_product = dot(grad_tr, down_ref[gate_at, :], 1, 1)
        down_acc[gate_at, :] += dot(product, grad_tr, 0, 0)
        grad_up = (grad_product * silu).astype(BF16)
        grad_gate = (grad_product * up_part * gate_sig * (1.0 + gate_part * (1.0 - gate_sig))).astype(BF16)
        swiglu_acc[:, gate_at] += dot(second_t, grad_gate)
        swiglu_acc[:, up_at] += dot(second_t, grad_up)
        grad_input += dot(grad_gate, swiglu_ref[:, gate_at], 1, 1)
        grad_input += dot(grad_up, swiglu_ref[:, up_at], 1, 1)
    transition = transition.reshape(samples, tokens, width)
    grad_input = grad_input.reshape(samples, tokens, width)
    partial_ref[...] = acts + zero_gate[None] * transition
    grad_zero = jnp.sum(grad_out * transition, axis=0) * slope(zero_gate)
    zero_b_out[...] += column_sum(grad_zero)
    zero_low[here, :] = grad_zero.astype(BF16)
    grad_factor = jnp.sum(grad_input * normed, axis=0) * slope(factor)
    cond_b_out[...] += column_sum(grad_factor)
    projected[here, :width] = grad_factor.astype(BF16)
    projected[here, width:] = jnp.sum(grad_input, axis=0).astype(BF16)
    acts_grad_ref[...] = grad_input * factor[None]

    @pl.when(step == pl.num_programs(0) - 1)
    def _():
        cond_w_grad, zero_w_grad, gain_grad, cond_gate, cond_norm, _, _ = conditions_back(
            cond_ref, gain_ref, cond_w_ref, zero_w_ref, zero_low[...], projected[...]
        )
        gain_out[...] = gain_grad
        cond_gate_ref[...] = cond_gate
        cond_norm_ref[...] = cond_norm
        halving.pack(packed_out, [swiglu_acc, down_acc, cond_w_grad, zero_w_grad])


def transition_call(acts, cot, cond, branch, swiglu, down, halving, deps, order):
    samples, length, width = acts.shape
    cond_width = cond.shape[1]
    hidden = down.shape[0]
    rows = samples * length
    block = spec((samples, TOKENS, width), 1)
    weights = [(width, 2 * hidden), (hidden, width), (cond_width, 2 * width), (cond_width, width)]
    vectors = [(1, width), (1, width), (1, cond_width)]
    results = call(
        "transition",
        functools.partial(transition_kernel, halving),
        length // TOKENS,
        [(acts, block), (cot, block), (cond, spec(cond.shape))]
        + branch
        + [(swiglu, spec(swiglu.shape)), (down, spec(down.shape))],
        [(acts.shape, F32, block)] * 2
        + [(cond.shape, F32, spec(cond.shape))] * 2
        + [(halving.slabs(weights), BF16, spec(halving.slabs(weights)))]
        + [(s, F32, spec(s)) for s in vectors],
        [pltpu.VMEM(s, F32) for s in weights[:2]]
        + [pltpu.VMEM((length, width), F32)] * 3
        + [pltpu.VMEM((length, width), BF16), pltpu.VMEM((length, 2 * width), BF16)],
        deps,
        order,
    )
    return results, weights


def attention_kernel(
    halving, head_dim, place, q_ref, k_ref, v_ref, g_ref, qt_ref, kt_ref, vt_ref, gt_ref, bias_ref,
    mixed_ref, dq_ref, dkt_ref, dvt_ref, sent_ref, kept_ref, kz, vz, plow, dslow, dsum, dlow,
):
    h = pl.program_id(0)
    samples, length, wide = q_ref.shape
    scale = head_dim ** (-0.5)
    off = pl.multiple_of(h * head_dim, 16)
    lane = lax.broadcasted_iota(jnp.int32, (1, wide), 1)
    mask = ((lane >= off) & (lane < off + head_dim)).astype(BF16)

    @pl.when(h == 0)
    def _():
        mixed_ref[...] = jnp.zeros_like(mixed_ref)
        dq_ref[...] = jnp.zeros_like(dq_ref)

    kz[...] = jnp.zeros_like(kz)
    vz[...] = jnp.zeros_like(vz)
    for s in range(samples):
        kz[s, pl.ds(off, head_dim), :] = kt_ref[s]
        vz[s, pl.ds(off, head_dim), :] = vt_ref[s]
    parts, _, share, _ = bias_ref.shape
    if share % 16 == 0:
        bias = bias_ref[:, 0].reshape(length, length).astype(F32)
    else:
        bias = jnp.concatenate([bias_ref[p, 0].astype(F32) for p in range(parts)], axis=0)
    for s in range(samples):
        x = dot(q_ref[s], kz[s]) * scale + bias
        x = jnp.exp(x - jnp.max(x, axis=-1, keepdims=True))
        probs = x * (1.0 / jnp.sum(x, axis=-1, keepdims=True))
        low = probs.astype(BF16)
        plow[s % 2] = low
        mixed = dot(low, v_ref[s] * mask)
        mixed_ref[s] += mixed
        grad = g_ref[s]
        delta = jnp.sum(grad.astype(F32) * mixed, axis=-1, keepdims=True)
        grad_scores = probs * (dot(grad, vz[s]) - delta)
        grad_low = grad_scores.astype(BF16)
        dslow[s % 2] = grad_low
        total = grad_scores if s == 0 else dsum[...] + grad_scores
        if s < samples - 1:
            dsum[...] = total
        else:
            dlow[...] = total.astype(dlow.dtype)
            bit = halving.order[0][1]
            slabs = halving.places()[: sent_ref.shape[0] // 2]
            for ref, value in ((sent_ref, 1 - place[bit]), (kept_ref, place[bit])):
                for p, (dest, _) in enumerate(slabs):
                    for c in range(2):
                        at = (dest + c) * share + value * (share << bit)
                        ref[2 * p + c, 0] = dlow[pl.ds(pl.multiple_of(at, 16 if share % 16 == 0 else 8), share), :].astype(BF16)
        dq_ref[s] += (dot(grad_low, k_ref[s] * mask) * scale).astype(BF16)
        dvt_ref[s] = dot(gt_ref[s], plow[s % 2]).astype(BF16)
        dkt_ref[s] = (dot(qt_ref[s], dslow[s % 2]) * scale).astype(BF16)


def attention_call(chunk, nats, turned, bias, head_dim, halving, deps, order):
    _, samples, length, wide = nats[0].shape
    parts, heads, share, _ = bias.shape
    nat = pl.BlockSpec((None, samples, length, wide), lambda h, core: (chunk, 0, 0, 0))
    turn = pl.BlockSpec((samples, head_dim, length), lambda h, core: (0, chunk * CHUNK_HEADS + h, 0))
    turn_out = pl.BlockSpec((samples, head_dim, length), lambda h, core: (0, h, 0))
    bias_in = pl.BlockSpec(
        (parts, 1, share, length), lambda h, core: (0, core[0] * (heads // 2) + chunk * CHUNK_HEADS + h, 0, 0)
    )
    bias_out = pl.BlockSpec((parts // 2, 1, share, length), lambda h, core: (0, h, 0, 0))
    aligned = share % 16 == 0
    held = pl.BlockSpec((samples, length, wide), lambda h, core: (0, 0, 0))
    return call(
        "attention",
        functools.partial(attention_kernel, halving, head_dim),
        CHUNK_HEADS,
        [(a, nat) for a in nats] + [(a, turn) for a in turned] + [(bias, bias_in)],
        [((samples, length, wide), F32, held), ((samples, length, wide), BF16, held)]
        + [((samples, CHUNK_HEADS * head_dim, length), BF16, turn_out)] * 2
        + [((parts // 2, CHUNK_HEADS, share, length), BF16, bias_out)] * 2,
        [
            pltpu.VMEM((samples, wide, length), BF16),
            pltpu.VMEM((samples, wide, length), BF16),
            pltpu.VMEM((2, length, length), BF16),
            pltpu.VMEM((2, length, length), BF16),
            pltpu.VMEM((length, length), F32),
            pltpu.VMEM((length, length), BF16 if aligned else F32),
        ],
        deps,
        order,
        SHORT,
    )


def mixed_kernel(chunks, place, *refs):
    (gate_ref, gated_grad_ref), refs = refs[:2], refs[2:]
    mixed_refs, refs = refs[:chunks], refs[chunks:]
    dq_refs, refs = refs[:chunks], refs[chunks:]
    dkt_refs, refs = refs[:chunks], refs[chunks:]
    dvt_refs, refs = refs[:chunks], refs[chunks:]
    joined_refs, q_bias_out = refs[:2], refs[2]
    clear(pl.program_id(0), q_bias_out)
    samples, tokens, half = gate_ref.shape
    own_samples = samples // 2

    def join(refs):
        return jnp.concatenate([ref[:, :, : half // chunks] for ref in refs], axis=-1)

    def turn(turned_refs):
        joined = jnp.concatenate([ref[...] for ref in turned_refs], axis=1)
        return jnp.stack([joined[s].T for s in range(samples)], axis=0)

    mixed = join(mixed_refs)
    gate = gate_ref[...]
    gated = (gate * mixed).astype(BF16)
    grad_queries = join(dq_refs)
    q_bias_out[...] += column_sum(grad_queries.astype(F32))
    grad_gate = gated_grad_ref[...] * mixed * slope(gate)
    parts = [gated, grad_queries, turn(dkt_refs), turn(dvt_refs), grad_gate.astype(BF16)]
    for i in range(2):
        here = slice(i * own_samples, (i + 1) * own_samples)
        for j, part in enumerate(parts):
            joined_refs[i][:, :, j * half : (j + 1) * half] = part[here]


def mixed_call(gate, gated_grad, mixeds, dqs, dkts, dvts, deps, order):
    samples, length, half = gate.shape
    chunks = len(mixeds)
    own_samples = samples // 2
    block = spec((samples, TOKENS, half), 1)
    window = spec((samples, TOKENS, LANES), 1)
    turned = spec((samples, half // chunks, TOKENS), 2)
    return call(
        "mixed",
        functools.partial(mixed_kernel, chunks),
        length // TOKENS,
        [(a, block) for a in (gate, gated_grad)]
        + [(a, window) for a in mixeds + dqs]
        + [(a, turned) for a in dkts + dvts],
        [((own_samples, length, 5 * half), BF16, spec((own_samples, TOKENS, 5 * half), 1))] * 2
        + [((1, half), F32, spec((1, half)))],
        [],
        deps,
        order,
    )


def qkvg_kernel(halving, place, first_ref, *refs):
    joined_refs, other_refs, packed_out = refs[:2], refs[2:4], refs[4]
    step = pl.program_id(0)
    samples, length, width = first_ref.shape
    rows = samples * length // 2
    half = joined_refs[0].shape[2]

    def both(pair):
        return jnp.concatenate([ref[...].reshape(rows, half) for ref in pair], axis=1)

    grad = dot(first_ref[: samples // 2].reshape(rows, width), both(joined_refs), 0, 0)
    grad += dot(first_ref[samples // 2 :].reshape(rows, width), both(other_refs), 0, 0)
    share = packed_out.shape[1] * halving.halves() // 4

    for block in range(4):

        @pl.when(step == block // 2)
        def _():
            column = block % 2 * half
            for p, (dest, part) in enumerate(halving.places()):
                piece = block - part * (4 // halving.halves())
                if 0 <= piece < 4 // halving.halves():
                    for c in range(2):
                        at = (dest + c) * share
                        packed_out[2 * p + c, piece * share : (piece + 1) * share] = grad[
                            at : at + share, column : column + half
                        ].astype(BF16)


def qkvg_call(first, joined, joined_other, halving, deps, order):
    samples, length, width = first.shape
    half = joined.shape[2] // 5
    share = width // halving.counts["sample"]
    slabs = (2 * 2 ** len(halving.order), 4 // halving.halves() * share, half)
    blocks = [
        pl.BlockSpec((samples // 2, length, half), lambda t, place, i=i: (0, 0, 1 + 2 * t + i)) for i in range(2)
    ]
    (packed,) = call(
        "qkvg_grad",
        functools.partial(qkvg_kernel, halving),
        2,
        [(first, spec(first.shape))] + [(a, b) for a in (joined, joined_other) for b in blocks],
        [(slabs, BF16, spec(slabs))],
        [],
        deps,
        order,
    )
    return packed


def outputs_kernel(place, acts_ref, cot_ref, partial_ref, acts_part_ref, zero_gate_ref, factor_ref, *refs):
    joined_refs, refs = refs[:2], refs[2:]
    out_w_refs, qkvg_refs, refs = refs[:2], (refs[2:6], refs[6:10]), refs[10:]
    block_ref, acts_grad_ref, projected_ref, zero_low_ref, cond_b_out, zero_b_out, out_out = refs
    clear(pl.program_id(0), cond_b_out, zero_b_out, out_out)
    samples, tokens, width = acts_ref.shape
    rows = samples * tokens
    half = width // 2
    zero_gate = zero_gate_ref[...]
    factor = factor_ref[...]
    normed, inverse = layer_norm(acts_ref[...].astype(F32))
    grad_out = cot_ref[...].astype(F32)
    grad_att = (grad_out * zero_gate[None]).astype(BF16).reshape(rows, width)
    attended = grad_input = 0.0
    for i, half_at in enumerate((place[0], 1 - place[0])):
        gated = joined_refs[i][:, :, :half].reshape(rows, half)
        attended += dot(gated, out_w_refs[i][...])
        out_out[pl.ds(pl.multiple_of(half_at * half, half), half), :] += dot(gated, grad_att, 0, 0)
        for j in range(4):
            grad_input += dot(
                joined_refs[i][:, :, (1 + j) * half : (2 + j) * half].reshape(rows, half), qkvg_refs[i][j][...], 1, 1
            )
    attended = attended.reshape(samples, tokens, width)
    grad_input = grad_input.reshape(samples, tokens, width)
    block_ref[...] = (partial_ref[...] + zero_gate[None] * attended).astype(BF16)
    grad_zero = jnp.sum(grad_out * attended, axis=0) * slope(zero_gate)
    zero_b_out[...] += column_sum(grad_zero)
    zero_low_ref[...] = grad_zero.astype(BF16)
    grad_factor = jnp.sum(grad_input * normed, axis=0) * slope(factor)
    cond_b_out[...] += column_sum(grad_factor)
    projected_ref[:, :width] = grad_factor.astype(BF16)
    projected_ref[:, width:] = jnp.sum(grad_input, axis=0).astype(BF16)
    acts_grad_ref[...] = (
        grad_out + norm_back(grad_input * factor[None] + acts_part_ref[...], normed, inverse)
    ).astype(BF16)


def outputs_call(acts, cot, partial, acts_part, zero_gate, factor, joineds, out_w, qkvg_w, deps, order):
    samples, length, width = acts.shape
    half = width // 2
    block = spec((samples, TOKENS, width), 1)
    tokens = spec((TOKENS, width), 0)
    return call(
        "outputs",
        outputs_kernel,
        length // TOKENS,
        [(a, block) for a in (acts, cot, partial, acts_part)]
        + [(zero_gate, tokens), (factor, tokens)]
        + [(a, spec((samples, TOKENS, 5 * half), 1)) for a in joineds]
        + [(out_w, spec((half, width), at=(whose, 0))) for whose in (own, other)]
        + quarters(qkvg_w, own)
        + quarters(qkvg_w, other),
        [
            (acts.shape, BF16, block),
            (acts.shape, BF16, block),
            ((length, 2 * width), BF16, spec((TOKENS, 2 * width), 0)),
            ((length, width), BF16, tokens),
        ]
        + [(s, F32, spec(s)) for s in ((1, width), (1, width), (width, width))],
        [],
        deps,
        order,
    )


def conditions_kernel(
    rest, vector_parts, place, cond_ref, gain_ref, cond_w_ref, zero_w_ref, zero_low_ref, projected_ref,
    cond_gate_in, cond_norm_in, out_w_grad_ref, *refs
):
    vector_refs, (packed_out,) = refs[:vector_parts], refs[vector_parts:]
    cond_w_grad, zero_w_grad, gain_grad, cond_gate, cond_norm, cond_normed, cond_inverse = conditions_back(
        cond_ref, gain_ref, cond_w_ref, zero_w_ref, zero_low_ref[...], projected_ref[...]
    )
    cond_grad = (
        cond_gate + cond_gate_in[...] + norm_back(cond_norm + cond_norm_in[...], cond_normed, cond_inverse)
    )
    vectors = [gain_grad] + [ref[...] for ref in vector_refs[:-1]]
    q_bias = vector_refs[-1][...]
    vectors += [jnp.where(place[0] == 0, q_bias, 0.0), jnp.where(place[0] == 1, q_bias, 0.0)]
    pieces = [v[:, at : at + PIECE] for v in vectors for at in range(0, v.shape[1], PIECE)]
    rest.pack(packed_out, [out_w_grad_ref[...], cond_w_grad, zero_w_grad, cond_grad], pieces)


def conditions_call(cond, branch, zero_w, zero_low, projected, cond_gate, cond_norm, out_w_grad, vectors, rest, deps, order):
    cond_width = cond.shape[1]
    width = zero_low.shape[1]
    weights = [out_w_grad.shape, (cond_width, 2 * width), (cond_width, width), cond.shape]
    count, rows, columns = rest.slabs(weights)
    rows += (sum(v.shape[1] for v in vectors) + cond_width + width // 2) // PIECE
    rows += -rows % 16
    fixed = (zero_low, projected, cond_gate, cond_norm, out_w_grad, *vectors)
    (packed,) = call(
        "conditions",
        functools.partial(conditions_kernel, rest, len(vectors)),
        1,
        [(cond, spec(cond.shape))] + branch[:2] + [zero_w] + [(a, spec(a.shape)) for a in fixed],
        [((count, rows, columns), BF16, spec((count, rows, columns)))],
        [],
        deps,
        order,
    )
    return packed, weights


def results_kernel(
    early_halving, rest_halving, early_shapes, rest_shapes, halves, place, *refs
):
    early_refs, refs = refs[:halves], refs[halves:]
    qkvg_refs, refs = refs[: 2 * halves], refs[2 * halves :]
    (rest_ref, rest_got_ref, pair_sum_ref, pair_wt_ref, pair_gain_ref), refs = refs[:5], refs[5:]
    (cond_ref, cond_w_ref, zero_w_ref, qkvg_ref, out_w_ref, swiglu_ref, down_ref), refs = refs[:7], refs[7:]
    gains_ref, cond_b_ref, zero_b_ref, q_bias_ref, pair_gain_out, pair_w_out = refs
    bits = place.shape[0] - 1
    device = sum(place[bit] << bit for bit in range(bits))

    def columns(ref, pieces):
        for c, piece in enumerate(pieces):
            ref[:, c * PIECE : (c + 1) * PIECE] = piece.astype(F32)

    early = [early_halving.unpack(ref[...].astype(F32), early_shapes) for ref in early_refs]
    swiglu, down, cond_w_one, zero_w_one = [sum(parts, []) for parts in zip(*early)]
    before = rest_ref[...].astype(F32)
    total = before + rest_got_ref[...].astype(F32)
    out_w, cond_w_zero, zero_w_zero, _ = rest_halving.unpack(total, rest_shapes)
    columns(swiglu_ref, swiglu)
    columns(down_ref, down)
    columns(cond_w_ref, cond_w_zero + cond_w_one)
    columns(zero_w_ref, zero_w_zero + zero_w_one)
    columns(out_w_ref, out_w)
    columns(cond_ref, rest_halving.unpack(before, rest_shapes)[3])
    parts = []
    for i in range(2):
        held = [ref[...].astype(F32) for ref in qkvg_refs[i * halves : (i + 1) * halves]]
        if halves == 2:
            first = place[bits] == 0
            held = [jnp.where(first, held[0], held[1]), jnp.where(first, held[1], held[0])]
        parts.append(jnp.concatenate(held, axis=0))
    first = place[0] == 0
    parts = [jnp.where(first, parts[0], parts[1]), jnp.where(first, parts[1], parts[0])]
    rows = parts[0].shape[0] // 4
    columns(qkvg_ref, [part[j * rows : (j + 1) * rows] for j in range(4) for part in parts])
    at = sum(r * c for r, c in map(rest_halving.pieces, rest_shapes))
    for ref in (gains_ref, cond_b_ref, zero_b_ref, q_bias_ref):
        size = ref.shape[1]
        count = size * rest_halving.counts["sample"] // PIECE
        value = 0.0
        for c in range(count):
            source = lax.broadcasted_iota(jnp.int32, (PIECE, size), 0) + c * PIECE
            target = lax.broadcasted_iota(jnp.int32, (PIECE, size), 1) + device * size
            chosen = (source == target).astype(F32)
            value += lax.dot_general(
                total[at + c : at + c + 1],
                chosen,
                (((1,), (0,)), ((), ())),
                precision=lax.Precision.HIGHEST,
                preferred_element_type=F32,
            )
        ref[...] = value
        at += count
    size, heads = pair_w_out.shape
    channels = pair_sum_ref.shape[1]
    source = lax.broadcasted_iota(jnp.int32, (channels, size), 0)
    target = lax.broadcasted_iota(jnp.int32, (channels, size), 1) + device * size
    chosen = (source == target).astype(F32)

    def choose(array):
        return lax.dot_general(
            chosen,
            array,
            (((0,), (1,)), ((), ())),
            precision=lax.Precision.HIGHEST,
            preferred_element_type=F32,
        )

    grad = choose(pair_sum_ref[...])
    pair_w_out[...] = grad
    weighted = grad * choose(pair_wt_ref[...].astype(F32))

    def across(left, right, right_dim):
        return lax.dot_general(
            left,
            right,
            (((1,), (right_dim,)), ((), ())),
            precision=lax.Precision.HIGHEST,
            preferred_element_type=F32,
        )

    pair_gain_out[...] = across(jnp.ones((1, heads), F32), weighted, 1) / across(pair_gain_ref[...], chosen, 0)


def results_call(
    early, early_halving, early_shapes, qkvg, rest, rest_got, rest_halving, rest_shapes, pair_sum, pair_wt, pair_gain, order
):
    count = rest_halving.counts["sample"]
    heads, channels = pair_wt.shape
    swiglu, down, cond_w, zero_w = early_shapes
    out_w, _, _, cond = rest_shapes
    width = out_w[1]
    arrays = [cond, (cond_w[0], 2 * cond_w[1]), (zero_w[0], 2 * zero_w[1]), (width, 4 * width), out_w, swiglu, down]
    shapes = [(rows // count, columns) for rows, columns in arrays]
    shapes += [(1, size // count) for size in (2 * cond[1], 2 * width, 2 * width, width)]
    shapes += [(1, channels // count), (channels // count, heads)]
    ins = [*early, *qkvg, rest, rest_got, pair_sum, pair_wt, pair_gain]
    return call(
        "results",
        functools.partial(
            results_kernel, early_halving, rest_halving, early_shapes, rest_shapes, early_halving.halves()
        ),
        1,
        [(a, spec(a.shape)) for a in ins],
        [(shape, F32, spec(shape)) for shape in shapes],
        [],
        [],
        order,
    )


def body(
    struct_count, sample_devices,
    acts, cond, pair, lengths, token_mask, cond_gains, cond_w, cond_bias, output_gate_weights, zero_bias,
    qkvg_w, q_bias, out_w, swiglu_w, down_w, pair_gain, pair_w, cotangent,
):
    acts, cond, pair, cotangent = acts[0], cond[0], pair[0], cotangent[0]
    samples, length, width = acts.shape
    cond_width = cond.shape[1]
    heads = pair_w.shape[1]
    head_dim = width // heads
    chunks = heads // 2 // CHUNK_HEADS
    counts = {"struct": struct_count, "sample": sample_devices}
    bits = sample_devices.bit_length() - 1
    pair_wt = pair_w.T
    device = lax.axis_index("sample")
    core = device & 1
    place = [(device >> bit) & 1 for bit in range(bits)] + [lax.axis_index("struct")]
    order = Order(jnp.stack(place).astype(jnp.int32))

    def swap(array):
        return lax.ppermute(array, "sample", [(i, i ^ 1) for i in range(sample_devices)])

    acts_other, cotangent_other = swap(acts), swap(cotangent)

    bias_rows = pair_forward(pair, pair_gain[None], pair_wt, token_mask, lengths, Order(jnp.zeros(bits + 1, jnp.int32)))
    bias = lax.all_gather(bias_rows, "sample", axis=0, tiled=False)

    rows = {}
    at = 0
    packed = [
        ("gain", cond_gains), ("cond_b", cond_bias), ("zero_b", zero_bias), ("q_bias", q_bias), ("pair", pair_gain)
    ]
    vector = jnp.concatenate([v for _, v in packed]).astype(F32)[None]
    for name, v in packed:
        rows[name] = vector[:, at : at + v.shape[0]]
        at += v.shape[0]

    def conditioning(b):
        return [
            (rows["gain"], spec((1, cond_width), at=(0, b))),
            (cond_w, spec((cond_width, 2 * width), at=(0, b))),
            (rows["cond_b"], spec((1, width), at=(0, b))),
        ]

    def zero(b):
        return [
            (output_gate_weights, spec((cond_width, width), at=(0, b))),
            (rows["zero_b"], spec((1, width), at=(0, b))),
        ]

    def path(*order):
        steps = [("struct", 0) if o == "y" else ("sample", o) for o in order]
        steps = [s for s in steps if s[0] == "sample" or struct_count == 2]
        return Halving(steps + [("sample", b) for b in range(4, bits)], counts)

    along_x = path(0, 1, 2, 3)
    along_y = path(0, "y", 2, 3, 1)
    chip_x = path(1, 2, 3)
    chip_y = path("y", 2, 3, 1)
    results, early_shapes = transition_call(
        acts, cotangent, cond, conditioning(1) + zero(1), swiglu_w, down_w, along_y, [], order
    )
    partial, acts_part, cond_gate, cond_norm, early, cond_b_one, zero_b_one, gain_one = results
    early = Running(along_y.run(early))
    first, gate, gated_grad, *rest = inputs_call(
        acts, acts_other, cotangent, cotangent_other, cond, conditioning(0) + zero(0), qkvg_w, rows["q_bias"], out_w,
        heads, [], order,
    )
    nats, turned, (zero_gate, factor) = rest[:4], rest[4:8], rest[8:]

    mixeds, dqs, dkts, dvts, bias_sums = [], [], [], [], []
    deps = advance(order, early)
    for chunk in range(chunks):
        mixed, dq, dkt, dvt, sent, kept = attention_call(chunk, nats, turned, bias, head_dim, chip_x, deps, order)
        mixeds.append(mixed)
        dqs.append(dq)
        dkts.append(dkt)
        dvts.append(dvt)
        deps = advance(order, *bias_sums, *([early] if chunk % 2 else []))
        bias_sums.append(Running(chip_x.run(kept, "swap", sent)))

    joined, joined_sent, q_bias_grad = mixed_call(
        gate, gated_grad, mixeds, dqs, dkts, dvts, deps, order
    )
    joined_got = swap(joined_sent)
    qkvg_sum = Running(
        chip_y.run(qkvg_call(first, joined, joined_sent, chip_y, [], order), "cores")
    )
    deps = advance(order, *bias_sums, qkvg_sum)
    block_out, acts_grad, projected, zero_low, cond_b_zero, zero_b_zero, out_grad = outputs_call(
        acts, cotangent, partial, acts_part, zero_gate, factor, [joined, joined_got],
        out_w, qkvg_w, deps, order,
    )
    deps = advance(order, *bias_sums, qkvg_sum, early)
    rest, rest_shapes = conditions_call(
        cond, conditioning(0), zero(0)[0], zero_low, projected, cond_gate, cond_norm, out_grad,
        [gain_one, cond_b_zero, cond_b_one, zero_b_zero, zero_b_one, q_bias_grad], along_x, deps, order,
    )
    rest = Running(along_x.run(rest, ""))
    while any(b.result is None for b in bias_sums):
        advance(order, *bias_sums)
    share = length // sample_devices
    block = 16 if share % 16 == 0 else share
    turned_wt = jnp.where(core == 0, pair_wt, jnp.roll(pair_wt, heads // 2, axis=0))
    grads = [b.result[0] for b in bias_sums] + [b.result[1] for b in bias_sums]
    grad_pair, part = pair_backward(0, block, None, pair, grads, rows["pair"], turned_wt, [], order)
    pair_parts = [part]
    if share > block:
        deps = advance(order, qkvg_sum, rest, early)
        grad_pair, part = pair_backward(
            block, share - block, grad_pair, pair, grads, rows["pair"], turned_wt, deps, order
        )
        pair_parts.append(part)
    struct_bits = struct_count.bit_length() - 1

    def summed(array, *masks):
        found = [
            lax.ppermute(array, ("struct", "sample"), [(i, i ^ mask) for i in range(struct_count * sample_devices)])
            for mask in masks
        ]
        if len(found) == 1:
            return array + found[0]
        return (array + found[0]) + (found[1] + found[2])

    class Pair:
        asked = [[(p, p.shape[0], lambda place: 0, True) for p in pair_parts]]
        result = None

        def send(self, found):
            self.result = found[0]

    pair_grad = Pair()
    advance(order, pair_grad, qkvg_sum, rest, early)
    left = [bits + struct_bits - 1] + list(range(bits + struct_bits - 1)) if struct_bits else list(range(bits))
    pair_sum = pair_grad.result
    while left:
        one = 1 << left.pop(0)
        two = 1 << left.pop(0) if left else 0
        pair_sum = summed(pair_sum, one, two, one | two) if two else summed(pair_sum, one)
    chains = (qkvg_sum, rest, early)
    while any(r.result is None for r in chains):
        advance(order, *chains, near=True)
    mine_qkvg, sent = qkvg_sum.result
    if chip_y.halves() == 2:
        across = [
            (s * sample_devices + i, (1 - s) * sample_devices + (i ^ 1))
            for s in range(2)
            for i in range(sample_devices)
        ]
        from_y = lax.ppermute(mine_qkvg, "struct", [(0, 1), (1, 0)])
        from_both = lax.ppermute(sent, ("struct", "sample"), across)
        qkvg = [mine_qkvg, from_y, swap(sent), from_both]
    else:
        for bit in range(struct_bits):
            mine_qkvg, sent = [summed(part, 1 << (bits + bit)) for part in (mine_qkvg, sent)]
        qkvg = [mine_qkvg, swap(sent)]
    early = list(early.result) if along_y.halves() == 2 else [early.result]
    rest_sum, rest_got = rest.result, jnp.zeros_like(rest.result)
    for bit in range(struct_bits):
        if bit:
            rest_sum = rest_sum + rest_got
        rest_got = lax.ppermute(
            rest_sum, "struct", [(i, i ^ (1 << bit)) for i in range(struct_count)]
        )
    (cond_sum, cond_w_sum, zero_w_sum, qkvg_total, out_sum, swiglu_sum, down_sum,
     gains, cond_b, zero_b, q_b, pair_g, pair_w_sum) = results_call(
        early, along_y, early_shapes, qkvg, rest_sum, rest_got, along_x, rest_shapes, pair_sum, pair_wt, rows["pair"], order
    )
    if struct_bits > 1:
        cond_sum = along_x.unpack(rest.result, rest_shapes)[3][0].astype(F32)
    return (
        block_out[None], acts_grad[None], cond_sum[None], grad_pair[None], gains[0], cond_w_sum, cond_b[0], zero_w_sum,
        zero_b[0], qkvg_total, q_b[0], out_sum, swiglu_sum, down_sum, pair_g[0], pair_w_sum,
    )


def solution(mesh):
    per_struct = P("struct", "sample", None, None)
    in_specs = (
        (per_struct, P("struct", None, None), per_struct, P("struct"), P("struct", None))
        + (P(),) * 12
        + (per_struct,)
    )
    one, two = P("sample"), P("sample", None)
    out_specs = (
        per_struct, per_struct, P("struct", "sample", None), per_struct,
        one, two, one, two, one, two, one, two, two, two, one, two,
    )
    local = functools.partial(body, mesh.shape["struct"], mesh.shape["sample"])
    return jax.shard_map(local, mesh=mesh, in_specs=in_specs, out_specs=out_specs, check_vma=False)
```

```python
import functools

import jax
import jax.numpy as jnp
from jax import lax
from jax.experimental import pallas as pl
from jax.experimental.pallas import tpu as pltpu
from jax.sharding import PartitionSpec as P

EPS = 1e-05
MASKED = -1000000000.0
F32 = jnp.float32
BF16 = jnp.bfloat16
CHUNK_HEADS = 2
LANES = 128
PIECE = 384
LOG2E = 1.4426950408889634
LONG, SHORT = 10**11, 17 * 10**9
TOKENS = 128
HIDDEN = 768
VMEM_LIMIT = 64 * 2**20 - 2**17


def dot(left, right, left_dim=1, right_dim=0):
    return lax.dot_general(
        left, right, (((left_dim,), (right_dim,)), ((), ())), preferred_element_type=F32
    )


def layer_norm(values):
    center = values - jnp.mean(values, axis=-1, keepdims=True)
    inverse = lax.rsqrt(jnp.mean(center * center, axis=-1, keepdims=True) + EPS)
    return (center * inverse, inverse)


def norm_back(grad_in, normed, inverse):
    mean_grad = jnp.mean(grad_in, axis=-1, keepdims=True)
    mean_proj = jnp.mean(grad_in * normed, axis=-1, keepdims=True)
    return inverse * (grad_in - mean_grad - normed * mean_proj)


def slope(gate):
    return gate * (1.0 - gate)


def column_sum(values):
    return jnp.sum(values.reshape(-1, values.shape[-1]), axis=0, keepdims=True)


def clear(step, *refs):
    @pl.when(step == 0)
    def _():
        for ref in refs:
            ref[...] = jnp.zeros_like(ref)


def spec(block, along=None, at=None):
    rank = len(block)
    if along is not None:
        return pl.BlockSpec(block, lambda t, core: tuple(t if a == along else 0 for a in range(rank)))
    index = (0,) * rank if at is None else at
    return pl.BlockSpec(
        block,
        lambda t, core: tuple(i(core[0]) if callable(i) else i for i in index),
        pipeline_mode=pl.Buffered(1),
    )


class Order:
    def __init__(self, place):
        self.place = place
        self.last = []


def call(name, kernel, grid, ins, outs, scratch, deps, order, flops=LONG, aliases={}, vmem=VMEM_LIMIT):
    inputs = len(ins)
    deps = list(deps) + order.last

    def run(place_ref, *refs):
        kernel(place_ref, *refs[:inputs], *refs[inputs + len(deps) :])

    found = pl.pallas_call(
        run,
        grid_spec=pltpu.PrefetchScalarGridSpec(
            num_scalar_prefetch=1,
            grid=(grid,),
            in_specs=[s for _, s in ins] + [pl.BlockSpec(memory_space=pl.ANY)] * len(deps),
            out_specs=[s for _, _, s in outs],
            scratch_shapes=scratch,
        ),
        out_shape=[jax.ShapeDtypeStruct(shape, dtype) for shape, dtype, _ in outs],
        compiler_params=pltpu.CompilerParams(
            vmem_limit_bytes=vmem, dimension_semantics=("arbitrary",)
        ),
        cost_estimate=pl.CostEstimate(flops=flops, bytes_accessed=10**6, transcendentals=0),
        name=name,
        input_output_aliases=aliases,
    )(order.place, *[a for a, _ in ins], *deps)
    order.last = [max(found, key=lambda array: array.size)]
    return found


def combine(outputs, order, near=False):
    held = pl.BlockSpec(memory_space=pltpu.VMEM)
    ins, outs, plan = [], [], []
    for terms in outputs:
        if isinstance(terms, tuple):
            bit, *arrays = terms
            terms = [(array, array.shape[0], lambda place: 0, True) for array in arrays]
        else:
            bit = None
        array, slabs = terms[0][:2]
        shape = (slabs,) + array.shape[1:]
        rest = (0,) * (len(shape) - 1)
        sources = []
        for term, _, index, small in terms:
            if near and small:
                sources.append((len(ins), index, slabs))
                ins.append((term, held))
            else:
                sources.append((len(ins), None, slabs))
                ins.append(
                    (term, pl.BlockSpec(shape, lambda t, place, index=index, rest=rest: (index(place),) + rest))
                )
        plan.append((bit, sources))
        blocked = pl.BlockSpec(shape, lambda t, place, rank=len(shape): (0,) * rank)
        outs.append((shape, array.dtype, held if near else blocked))

    def kernel(place, *refs):
        for (bit, sources), out_ref in zip(plan, refs[len(ins) :]):
            values = [
                refs[i][...] if index is None else refs[i][pl.ds(index(place) * slabs, slabs)]
                for i, index, slabs in sources
            ]
            if bit is not None:
                out_ref[...] = jnp.where(place[bit] == 0, values[0], values[1])
            elif len(values) == 1:
                out_ref[...] = values[0]
            else:
                total = sum((v.astype(F32) for v in values[1:]), values[0].astype(F32))
                out_ref[...] = total.astype(out_ref.dtype)

    return call("combine", kernel, 1, ins, outs, [], [], order, vmem=16 * 2**20 if near else VMEM_LIMIT)


class Halving:
    def __init__(self, order, counts):
        self.order = order
        self.counts = counts

    def places(self):
        found = []
        for p in range(2 ** len(self.order)):
            dest, half = 0, 0
            for i, (axis, bit) in enumerate(self.order):
                value = (p >> (len(self.order) - 1 - i)) & 1
                if axis == "sample":
                    dest |= value << bit
                else:
                    half = value
            found.append((dest, half))
        return found

    def halves(self):
        return 2 if any(axis == "struct" for axis, _ in self.order) else 1

    def pieces(self, shape):
        rows, columns = shape
        return rows // self.counts["sample"], columns // self.halves() // PIECE

    def slabs(self, shapes):
        return (2 ** len(self.order), sum(r * c for r, c in map(self.pieces, shapes)), PIECE)

    def pack(self, out_ref, arrays, everywhere=()):
        for p, (dest, half) in enumerate(self.places()):
            held = []
            for array in arrays:
                rows, count = self.pieces(array.shape)
                for c in range(count):
                    at = (half * count + c) * PIECE
                    held.append(array[dest * rows : (dest + 1) * rows, at : at + PIECE])
            slab = jnp.concatenate(held + list(everywhere), axis=0)
            out_ref[p, : slab.shape[0]] = slab.astype(out_ref.dtype)
            if slab.shape[0] < out_ref.shape[1]:
                out_ref[p, slab.shape[0] :] = jnp.zeros(
                    (out_ref.shape[1] - slab.shape[0], PIECE), out_ref.dtype
                )

    def unpack(self, slab, shapes):
        found, at = [], 0
        for shape in shapes:
            rows, count = self.pieces(shape)
            found.append([slab[at + c * rows : at + (c + 1) * rows] for c in range(count)])
            at += rows * count
        return found

    def run(self, array, after="sum", sent=None):
        last = self.counts["sample"].bit_length() - 1

        def exchange(array, axis, bit):
            return lax.ppermute(array, axis, [(i, i ^ (1 << bit)) for i in range(self.counts[axis])])

        def halves(at, size):
            return [
                [
                    (p, size, lambda place, base=base, at=at, flip=flip: 2 * base(place) + (place[at] ^ flip), held)
                    for p, base, held in parts
                ]
                for flip in (1, 0)
            ]

        zero = lambda place: 0
        parts, size = [(array, zero, False)], array.shape[0]
        order = self.order
        if sent is not None:
            parts.append((exchange(sent, *order[0]), zero, False))
            order = order[1:]
        for axis, bit in order:
            at = bit if axis == "sample" else last
            size = size // 2
            if len(parts) == 1 and (axis, bit) == ("sample", 0):
                first = lambda place: place[0]
                parts = [(array, first, False), (exchange(array, axis, bit), first, False)]
                continue
            if len(parts) == 1:
                (sent,) = yield halves(at, size)[:1]
                parts = [(array, lambda place, at=at: place[at], False), (exchange(sent, axis, bit), zero, True)]
            else:
                sent, kept = yield halves(at, size)
                parts = [(kept, zero, True), (exchange(sent, axis, bit), zero, True)]
        if after in ("swap", "cores"):
            sent, kept = yield halves(0, size // 2)
            return kept[0], exchange(sent, "sample", 0)[0] if after == "swap" else sent[0]
        (held,) = yield [[(p, 1, base, near) for p, base, near in parts]]
        if not after:
            return held[0]
        if self.halves() == 2:
            received = exchange(held, "struct", 0)
            first, second = yield [(last, held, received), (last, received, held)]
            return first[0], second[0]
        for bit in range(self.counts["struct"].bit_length() - 1):
            received = exchange(held, "struct", bit)
            (held,) = yield [[(p, 1, zero, True) for p in (held, received)]]
        return held[0]

class Running:
    def __init__(self, steps):
        self.steps = steps
        self.result = None
        self.send(None)

    def send(self, found):
        try:
            self.asked = self.steps.send(found)
        except StopIteration as stop:
            self.asked = []
            self.result = stop.value


def advance(order, *running, near=False):
    running = [r for r in running if r.result is None]
    asked = [output for r in running for output in r.asked]
    if not asked:
        return []
    made = combine(asked, order, near)
    at = 0
    for r in running:
        count = len(r.asked)
        r.send(made[at : at + count])
        at += count
    return made


def pair_forward_kernel(place, pair_ref, gain_ref, weight_ref, mask_ref, lengths_ref, out_ref, terms):
    gain = gain_ref[...].astype(F32)
    rows, length, channels = pair_ref.shape
    average = jnp.full((channels, channels), 1.0 / channels, BF16)
    position = lax.broadcasted_iota(jnp.int32, (1, length), 1)
    valid = (position < lengths_ref[0]) & ((mask_ref[...] == 1) | (position == 0))
    for i in range(rows):
        values = pair_ref[i]
        center = values.astype(F32) - dot(values, average)
        inverse = lax.rsqrt(jnp.mean(center * center, axis=-1, keepdims=True) + EPS)
        affine = (center * inverse * gain).astype(BF16)
        terms[i] = jnp.where(valid, dot(weight_ref[...], affine, 1, 1), MASKED)
    for h in range(terms.shape[1]):
        out_ref[h] = terms[:, h, :].astype(BF16)


def pair_forward(pair, gain, weight_t, mask, lengths, order):
    rows, length, channels = pair.shape
    heads = weight_t.shape[0]
    block = 16 if rows % 16 == 0 else rows
    return call(
        "pair_forward",
        pair_forward_kernel,
        rows // block,
        [
            (pair, spec((block, length, channels), 0)),
            (gain, spec(gain.shape)),
            (weight_t, spec(weight_t.shape)),
            (mask, spec(mask.shape)),
            (lengths, pl.BlockSpec(memory_space=pltpu.SMEM)),
        ],
        [((heads, rows, length), BF16, spec((heads, block, length), 1))],
        [pltpu.VMEM((block, heads, length), F32)],
        [],
        order,
    )[0]


def pair_backward_kernel(chunks, first, place, pair_ref, gain_ref, weight_ref, *refs):
    grad_refs, (out_ref, weight_grad_ref, grads) = refs[:chunks], refs[-3:]
    gain = gain_ref[...]
    channels = pair_ref.shape[2]
    average = jnp.full((channels, channels), 1.0 / channels, BF16)
    clear(pl.program_id(0), weight_grad_ref)
    step = pl.program_id(0)
    rows = pair_ref.shape[0]

    @pl.when(step == 0)
    def _():
        head = 0
        for ref in grad_refs:
            for h in range(ref.shape[0]):
                grads[:, head, :] = ref[h, first : first + grads.shape[0]].astype(F32)
                head += 1

    scaled = weight_ref[...].astype(F32) * gain
    means = jnp.broadcast_to(jnp.mean(scaled, axis=-1, keepdims=True), scaled.shape)
    full = jnp.concatenate([scaled, means], axis=1)
    high = full.astype(BF16)
    parts = jnp.concatenate([high, (full - high.astype(F32)).astype(BF16)], axis=0)

    def row(i, carry):
        values = pair_ref[i]
        center = values.astype(F32) - dot(values, average)
        inverse = lax.rsqrt(jnp.mean(center * center, axis=-1, keepdims=True) + EPS)
        normed = center * inverse
        grad = grads[step * rows + i].astype(BF16)
        weight_grad_ref[...] += dot(grad, (normed * gain).astype(BF16))
        both = dot(jnp.concatenate([grad, grad], axis=0), parts, 0, 0)
        grad_normed = both[:, :channels]
        mean_proj = jnp.mean(grad_normed * normed, axis=-1, keepdims=True)
        out_ref[i] = inverse * (grad_normed - both[:, channels:] - normed * mean_proj)
        return carry

    lax.fori_loop(0, pair_ref.shape[0], row, 0, unroll=8)

    @pl.when((pl.program_id(0) == pl.num_programs(0) - 1) & (place[0] == 1))
    def _():
        half = weight_grad_ref.shape[0] // 2
        total = weight_grad_ref[...]
        weight_grad_ref[...] = jnp.concatenate([total[half:], total[:half]], axis=0)


def pair_backward(first, count, out, pair, grads, gain, weight_t, deps, order):
    rows, length, channels = pair.shape
    heads = weight_t.shape[0]
    block = 8
    blocked = pl.BlockSpec((block, length, channels), lambda t, place: (first // block + t, 0, 0))
    ins = [(pair, blocked), (gain, spec(gain.shape)), (weight_t, spec(weight_t.shape))]
    ins += [(g, spec(g.shape)) for g in grads]
    aliases = {}
    if out is not None:
        aliases = {1 + len(ins): 0}
        ins.append((out, pl.BlockSpec(memory_space=pl.ANY)))
    return call(
        "pair_backward",
        functools.partial(pair_backward_kernel, len(grads), first),
        count // block,
        ins,
        [(pair.shape, F32, blocked), ((heads, channels), F32, spec((heads, channels)))],
        [pltpu.VMEM((count, heads, length), F32)],
        deps,
        order,
        LONG,
        aliases,
    )


def conditions(cond_ref, gain_ref, cond_w_ref, cond_b_ref, zero_w_ref, zero_b_ref, zero_gate_ref, factor_ref, shift_ref):
    cond = cond_ref[...]
    width = zero_gate_ref.shape[1]
    zero_gate_ref[...] = jax.nn.sigmoid(dot(cond, zero_w_ref[...]) + zero_b_ref[...])
    cond_normed, _ = layer_norm(cond.astype(F32))
    projected = dot((cond_normed * gain_ref[...]).astype(BF16), cond_w_ref[...])
    factor_ref[...] = jax.nn.sigmoid(projected[:, :width] + cond_b_ref[...])
    shift_ref[...] = projected[:, width:]


def conditions_back(cond_ref, gain_ref, cond_w_ref, zero_w_ref, zero_grad, projected):
    cond = cond_ref[...]
    cond_normed, cond_inverse = layer_norm(cond.astype(F32))
    scaled = (cond_normed * gain_ref[...]).astype(BF16)
    grad_scaled = dot(projected, cond_w_ref[...], 1, 1)
    return (
        dot(scaled, projected, 0, 0),
        dot(cond, zero_grad, 0, 0),
        column_sum(grad_scaled * cond_normed),
        dot(zero_grad, zero_w_ref[...], 1, 1),
        grad_scaled * gain_ref[...],
        cond_normed,
        cond_inverse,
    )


def step_rows(step, tokens):
    return pl.ds(pl.multiple_of(step * tokens, tokens), tokens)


def inputs_kernel(
    place, acts_ref, acts_other_ref, cot_ref, cot_other_ref,
    cond_ref, gain_ref, cond_w_ref, cond_b_ref, zero_w_ref, zero_b_ref,
    query_ref, key_ref, value_ref, gate_w_ref, q_bias_ref, out_w_ref,
    input_ref, gate_ref, gated_grad_ref, q_ref, k_ref, v_ref, g_ref, qt_ref, kt_ref, vt_ref, gt_ref,
    zero_gate_ref, factor_ref, shift_ref,
):
    step = pl.program_id(0)
    samples, tokens, half = gate_ref.shape
    width = acts_ref.shape[2]
    rows = samples * tokens

    @pl.when(step == 0)
    def _():
        conditions(
            cond_ref, gain_ref, cond_w_ref, cond_b_ref, zero_w_ref, zero_b_ref, zero_gate_ref, factor_ref, shift_ref
        )

    here = step_rows(step, tokens)
    acts = jnp.concatenate([acts_ref[...], acts_other_ref[...]], axis=0)
    normed, _ = layer_norm(acts.astype(F32))
    first = (factor_ref[here, :][None] * normed + shift_ref[here, :][None]).astype(BF16)
    input_ref[...] = first
    first = first.reshape(rows, width)
    cot = jnp.concatenate([cot_ref[...], cot_other_ref[...]], axis=0)
    grad_att = (cot.astype(F32) * zero_gate_ref[here, :][None]).astype(BF16)
    grad_gated = dot(grad_att.reshape(rows, width), out_w_ref[...], 1, 1)
    gated_grad_ref[...] = grad_gated.reshape(samples, tokens, half)
    gate = jax.nn.sigmoid(dot(first, gate_w_ref[...]))
    gate_ref[...] = gate.reshape(samples, tokens, half)

    def put(values, nat_ref, t_ref):
        low = values.astype(BF16).reshape(samples, tokens, half)
        chunks = nat_ref.shape[0]
        used = half // chunks
        for chunk in range(chunks):
            nat_ref[chunk, :, :, :used] = low[:, :, chunk * used : (chunk + 1) * used]
            nat_ref[chunk, :, :, used:] = jnp.zeros((samples, tokens, LANES - used), BF16)
        for s in range(samples):
            t_ref[s] = low[s].T

    put(grad_gated * gate, g_ref, gt_ref)
    put(dot(first, query_ref[...]) + q_bias_ref[...], q_ref, qt_ref)
    put(dot(first, key_ref[...]), k_ref, kt_ref)
    put(dot(first, value_ref[...]), v_ref, vt_ref)


def own(core):
    return core


def other(core):
    return 1 - core


def quarters(weight, whose):
    rows, columns = weight.shape
    return [
        (weight, spec((rows, columns // 8), at=(0, functools.partial(lambda j, core: 2 * j + whose(core), j))))
        for j in range(4)
    ]


def inputs_call(acts, acts_other, cot, cot_other, cond, branch, qkvg_w, q_bias, out_w, heads, deps, order):
    own_samples, length, width = acts.shape
    samples, half = 2 * own_samples, width // 2
    chunks = heads // 2 // CHUNK_HEADS
    block = spec((own_samples, TOKENS, width), 1)
    wide = spec((samples, TOKENS, width), 1)
    narrow = spec((samples, TOKENS, half), 1)
    nat = spec((chunks, samples, TOKENS, LANES), 2)
    turned = spec((samples, half, TOKENS), 2)
    return call(
        "inputs",
        inputs_kernel,
        length // TOKENS,
        [(a, block) for a in (acts, acts_other, cot, cot_other)]
        + [(cond, spec(cond.shape))]
        + branch
        + quarters(qkvg_w, own)
        + [(q_bias, spec((1, half), at=(0, own))), (out_w, spec((half, width), at=(own, 0)))],
        [
            ((samples, length, width), BF16, wide),
            ((samples, length, half), F32, narrow),
            ((samples, length, half), F32, narrow),
        ]
        + [((chunks, samples, length, LANES), BF16, nat)] * 4
        + [((samples, half, length), BF16, turned)] * 4
        + [((length, width), F32, spec((length, width)))] * 2,
        [pltpu.VMEM((length, width), F32)],
        deps,
        order,
    )


def transition_kernel(
    halving, place, acts_ref, cot_ref, cond_ref, gain_ref, cond_w_ref, cond_b_ref, zero_w_ref, zero_b_ref,
    swiglu_ref, down_ref,
    partial_ref, acts_grad_ref, cond_gate_ref, cond_norm_ref, packed_out, cond_b_out, zero_b_out, gain_out,
    swiglu_acc, down_acc, zero_gate_ref, factor_ref, shift_ref, zero_low, projected,
):
    step = pl.program_id(0)
    clear(step, swiglu_acc, down_acc, cond_b_out, zero_b_out)
    samples, tokens, width = acts_ref.shape
    rows = samples * tokens
    hidden_width = down_ref.shape[0]

    @pl.when(step == 0)
    def _():
        conditions(
            cond_ref, gain_ref, cond_w_ref, cond_b_ref, zero_w_ref, zero_b_ref, zero_gate_ref, factor_ref, shift_ref
        )

    here = step_rows(step, tokens)
    zero_gate = zero_gate_ref[here, :]
    factor = factor_ref[here, :]
    acts = acts_ref[...].astype(F32)
    normed, _ = layer_norm(acts)
    second = (factor[None] * normed + shift_ref[here, :][None]).astype(BF16).reshape(rows, width)
    grad_out = cot_ref[...].astype(F32)
    grad_tr = (grad_out * zero_gate[None]).astype(BF16).reshape(rows, width)
    transition = grad_input = 0.0
    second_t = second.T
    for at in range(0, hidden_width, HIDDEN):
        gate_at, up_at = slice(at, at + HIDDEN), slice(hidden_width + at, hidden_width + at + HIDDEN)
        gate_part = dot(second, swiglu_ref[:, gate_at])
        up_part = dot(second, swiglu_ref[:, up_at])
        gate_sig = jax.nn.sigmoid(gate_part)
        silu = gate_part * gate_sig
        product = (silu * up_part).astype(BF16)
        transition += dot(product, down_ref[gate_at, :])
        grad_product = dot(grad_tr, down_ref[gate_at, :], 1, 1)
        down_acc[gate_at, :] += dot(product, grad_tr, 0, 0)
        grad_up = (grad_product * silu).astype(BF16)
        grad_gate = (grad_product * up_part * gate_sig * (1.0 + gate_part * (1.0 - gate_sig))).astype(BF16)
        swiglu_acc[:, gate_at] += dot(second_t, grad_gate)
        swiglu_acc[:, up_at] += dot(second_t, grad_up)
        grad_input += dot(grad_gate, swiglu_ref[:, gate_at], 1, 1)
        grad_input += dot(grad_up, swiglu_ref[:, up_at], 1, 1)
    transition = transition.reshape(samples, tokens, width)
    grad_input = grad_input.reshape(samples, tokens, width)
    partial_ref[...] = acts + zero_gate[None] * transition
    grad_zero = jnp.sum(grad_out * transition, axis=0) * slope(zero_gate)
    zero_b_out[...] += column_sum(grad_zero)
    zero_low[here, :] = grad_zero.astype(BF16)
    grad_factor = jnp.sum(grad_input * normed, axis=0) * slope(factor)
    cond_b_out[...] += column_sum(grad_factor)
    projected[here, :width] = grad_factor.astype(BF16)
    projected[here, width:] = jnp.sum(grad_input, axis=0).astype(BF16)
    acts_grad_ref[...] = grad_input * factor[None]

    @pl.when(step == pl.num_programs(0) - 1)
    def _():
        cond_w_grad, zero_w_grad, gain_grad, cond_gate, cond_norm, _, _ = conditions_back(
            cond_ref, gain_ref, cond_w_ref, zero_w_ref, zero_low[...], projected[...]
        )
        gain_out[...] = gain_grad
        cond_gate_ref[...] = cond_gate
        cond_norm_ref[...] = cond_norm
        halving.pack(packed_out, [swiglu_acc, down_acc, cond_w_grad, zero_w_grad])


def transition_call(acts, cot, cond, branch, swiglu, down, halving, deps, order):
    samples, length, width = acts.shape
    cond_width = cond.shape[1]
    hidden = down.shape[0]
    rows = samples * length
    block = spec((samples, TOKENS, width), 1)
    weights = [(width, 2 * hidden), (hidden, width), (cond_width, 2 * width), (cond_width, width)]
    vectors = [(1, width), (1, width), (1, cond_width)]
    results = call(
        "transition",
        functools.partial(transition_kernel, halving),
        length // TOKENS,
        [(acts, block), (cot, block), (cond, spec(cond.shape))]
        + branch
        + [(swiglu, spec(swiglu.shape)), (down, spec(down.shape))],
        [(acts.shape, F32, block)] * 2
        + [(cond.shape, F32, spec(cond.shape))] * 2
        + [(halving.slabs(weights), BF16, spec(halving.slabs(weights)))]
        + [(s, F32, spec(s)) for s in vectors],
        [pltpu.VMEM(s, F32) for s in weights[:2]]
        + [pltpu.VMEM((length, width), F32)] * 3
        + [pltpu.VMEM((length, width), BF16), pltpu.VMEM((length, 2 * width), BF16)],
        deps,
        order,
    )
    return results, weights


def attention_kernel(
    halving, head_dim, place, q_ref, k_ref, v_ref, g_ref, qt_ref, kt_ref, vt_ref, gt_ref, bias_ref,
    mixed_ref, dq_ref, dkt_ref, dvt_ref, sent_ref, kept_ref, kz, vz, plow, dslow, dsum, dlow,
):
    h = pl.program_id(0)
    samples, length, wide = q_ref.shape
    scale = head_dim ** (-0.5)
    off = pl.multiple_of(h * head_dim, 16)
    lane = lax.broadcasted_iota(jnp.int32, (1, wide), 1)
    mask = ((lane >= off) & (lane < off + head_dim)).astype(BF16)

    @pl.when(h == 0)
    def _():
        mixed_ref[...] = jnp.zeros_like(mixed_ref)
        dq_ref[...] = jnp.zeros_like(dq_ref)

    kz[...] = jnp.zeros_like(kz)
    vz[...] = jnp.zeros_like(vz)
    for s in range(samples):
        kz[s, pl.ds(off, head_dim), :] = kt_ref[s]
        vz[s, pl.ds(off, head_dim), :] = vt_ref[s]
    parts, _, share, _ = bias_ref.shape
    if share % 16 == 0:
        bias = bias_ref[:, 0].reshape(length, length).astype(F32) * LOG2E
    else:
        bias = jnp.concatenate([bias_ref[p, 0].astype(F32) for p in range(parts)], axis=0) * LOG2E
    for s in range(samples):
        x = dot(q_ref[s], kz[s]) * (scale * LOG2E) + bias
        x = jnp.exp2(x - jnp.max(x, axis=-1, keepdims=True))
        probs = x * (1.0 / jnp.sum(x, axis=-1, keepdims=True))
        low = probs.astype(BF16)
        plow[s % 2] = low
        mixed = dot(low, v_ref[s] * mask)
        mixed_ref[s] += mixed
        grad = g_ref[s]
        delta = jnp.sum(grad.astype(F32) * mixed, axis=-1, keepdims=True)
        grad_scores = probs * (dot(grad, vz[s]) - delta)
        grad_low = grad_scores.astype(BF16)
        dslow[s % 2] = grad_low
        total = grad_scores if s == 0 else dsum[...] + grad_scores
        if s < samples - 1:
            dsum[...] = total
        else:
            dlow[...] = total.astype(dlow.dtype)
            bit = halving.order[0][1]
            slabs = halving.places()[: sent_ref.shape[0] // 2]
            for ref, value in ((sent_ref, 1 - place[bit]), (kept_ref, place[bit])):
                for p, (dest, _) in enumerate(slabs):
                    for c in range(2):
                        at = (dest + c) * share + value * (share << bit)
                        ref[2 * p + c, 0] = dlow[pl.ds(pl.multiple_of(at, 16 if share % 16 == 0 else 8), share), :].astype(BF16)
        dq_ref[s] += (dot(grad_low, k_ref[s] * mask) * scale).astype(BF16)
        dvt_ref[s] = dot(gt_ref[s], plow[s % 2]).astype(BF16)
        dkt_ref[s] = (dot(qt_ref[s], dslow[s % 2]) * scale).astype(BF16)


def attention_call(chunk, nats, turned, bias, head_dim, halving, deps, order):
    _, samples, length, wide = nats[0].shape
    parts, heads, share, _ = bias.shape
    nat = pl.BlockSpec((None, samples, length, wide), lambda h, core: (chunk, 0, 0, 0))
    turn = pl.BlockSpec((samples, head_dim, length), lambda h, core: (0, chunk * CHUNK_HEADS + h, 0))
    turn_out = pl.BlockSpec((samples, head_dim, length), lambda h, core: (0, h, 0))
    bias_in = pl.BlockSpec(
        (parts, 1, share, length), lambda h, core: (0, core[0] * (heads // 2) + chunk * CHUNK_HEADS + h, 0, 0)
    )
    bias_out = pl.BlockSpec((parts // 2, 1, share, length), lambda h, core: (0, h, 0, 0))
    aligned = share % 16 == 0
    held = pl.BlockSpec((samples, length, wide), lambda h, core: (0, 0, 0))
    return call(
        "attention",
        functools.partial(attention_kernel, halving, head_dim),
        CHUNK_HEADS,
        [(a, nat) for a in nats] + [(a, turn) for a in turned] + [(bias, bias_in)],
        [((samples, length, wide), F32, held), ((samples, length, wide), BF16, held)]
        + [((samples, CHUNK_HEADS * head_dim, length), BF16, turn_out)] * 2
        + [((parts // 2, CHUNK_HEADS, share, length), BF16, bias_out)] * 2,
        [
            pltpu.VMEM((samples, wide, length), BF16),
            pltpu.VMEM((samples, wide, length), BF16),
            pltpu.VMEM((2, length, length), BF16),
            pltpu.VMEM((2, length, length), BF16),
            pltpu.VMEM((length, length), F32),
            pltpu.VMEM((length, length), BF16 if aligned else F32),
        ],
        deps,
        order,
        SHORT,
    )


def mixed_kernel(chunks, place, *refs):
    (gate_ref, gated_grad_ref), refs = refs[:2], refs[2:]
    mixed_refs, refs = refs[:chunks], refs[chunks:]
    dq_refs, refs = refs[:chunks], refs[chunks:]
    dkt_refs, refs = refs[:chunks], refs[chunks:]
    dvt_refs, refs = refs[:chunks], refs[chunks:]
    joined_refs, q_bias_out = refs[:2], refs[2]
    clear(pl.program_id(0), q_bias_out)
    samples, tokens, half = gate_ref.shape
    own_samples = samples // 2

    def join(refs):
        return jnp.concatenate([ref[:, :, : half // chunks] for ref in refs], axis=-1)

    def turn(turned_refs):
        joined = jnp.concatenate([ref[...] for ref in turned_refs], axis=1)
        return jnp.stack([joined[s].T for s in range(samples)], axis=0)

    mixed = join(mixed_refs)
    gate = gate_ref[...]
    gated = (gate * mixed).astype(BF16)
    grad_queries = join(dq_refs)
    q_bias_out[...] += column_sum(grad_queries.astype(F32))
    grad_gate = gated_grad_ref[...] * mixed * slope(gate)
    parts = [gated, grad_queries, turn(dkt_refs), turn(dvt_refs), grad_gate.astype(BF16)]
    for i in range(2):
        here = slice(i * own_samples, (i + 1) * own_samples)
        for j, part in enumerate(parts):
            joined_refs[i][:, :, j * half : (j + 1) * half] = part[here]


def mixed_call(gate, gated_grad, mixeds, dqs, dkts, dvts, deps, order):
    samples, length, half = gate.shape
    chunks = len(mixeds)
    own_samples = samples // 2
    block = spec((samples, TOKENS, half), 1)
    window = spec((samples, TOKENS, LANES), 1)
    turned = spec((samples, half // chunks, TOKENS), 2)
    return call(
        "mixed",
        functools.partial(mixed_kernel, chunks),
        length // TOKENS,
        [(a, block) for a in (gate, gated_grad)]
        + [(a, window) for a in mixeds + dqs]
        + [(a, turned) for a in dkts + dvts],
        [((own_samples, length, 5 * half), BF16, spec((own_samples, TOKENS, 5 * half), 1))] * 2
        + [((1, half), F32, spec((1, half)))],
        [],
        deps,
        order,
    )


def qkvg_kernel(halving, place, first_ref, *refs):
    joined_refs, other_refs, packed_out = refs[:2], refs[2:4], refs[4]
    step = pl.program_id(0)
    samples, length, width = first_ref.shape
    rows = samples * length // 2
    half = joined_refs[0].shape[2]

    def both(pair):
        return jnp.concatenate([ref[...].reshape(rows, half) for ref in pair], axis=1)

    grad = dot(first_ref[: samples // 2].reshape(rows, width), both(joined_refs), 0, 0)
    grad += dot(first_ref[samples // 2 :].reshape(rows, width), both(other_refs), 0, 0)
    share = packed_out.shape[1] * halving.halves() // 4

    for block in range(4):

        @pl.when(step == block // 2)
        def _():
            column = block % 2 * half
            for p, (dest, part) in enumerate(halving.places()):
                piece = block - part * (4 // halving.halves())
                if 0 <= piece < 4 // halving.halves():
                    for c in range(2):
                        at = (dest + c) * share
                        packed_out[2 * p + c, piece * share : (piece + 1) * share] = grad[
                            at : at + share, column : column + half
                        ].astype(BF16)


def qkvg_call(first, joined, joined_other, halving, deps, order):
    samples, length, width = first.shape
    half = joined.shape[2] // 5
    share = width // halving.counts["sample"]
    slabs = (2 * 2 ** len(halving.order), 4 // halving.halves() * share, half)
    blocks = [
        pl.BlockSpec((samples // 2, length, half), lambda t, place, i=i: (0, 0, 1 + 2 * t + i)) for i in range(2)
    ]
    (packed,) = call(
        "qkvg_grad",
        functools.partial(qkvg_kernel, halving),
        2,
        [(first, spec(first.shape))] + [(a, b) for a in (joined, joined_other) for b in blocks],
        [(slabs, BF16, spec(slabs))],
        [],
        deps,
        order,
    )
    return packed


def outputs_kernel(place, acts_ref, cot_ref, partial_ref, acts_part_ref, zero_gate_ref, factor_ref, *refs):
    joined_refs, refs = refs[:2], refs[2:]
    out_w_refs, qkvg_refs, refs = refs[:2], (refs[2:6], refs[6:10]), refs[10:]
    block_ref, acts_grad_ref, projected_ref, zero_low_ref, cond_b_out, zero_b_out, out_out = refs
    clear(pl.program_id(0), cond_b_out, zero_b_out, out_out)
    samples, tokens, width = acts_ref.shape
    rows = samples * tokens
    half = width // 2
    zero_gate = zero_gate_ref[...]
    factor = factor_ref[...]
    normed, inverse = layer_norm(acts_ref[...].astype(F32))
    grad_out = cot_ref[...].astype(F32)
    grad_att = (grad_out * zero_gate[None]).astype(BF16).reshape(rows, width)
    attended = grad_input = 0.0
    for i, half_at in enumerate((place[0], 1 - place[0])):
        gated = joined_refs[i][:, :, :half].reshape(rows, half)
        attended += dot(gated, out_w_refs[i][...])
        out_out[pl.ds(pl.multiple_of(half_at * half, half), half), :] += dot(gated, grad_att, 0, 0)
        for j in range(4):
            grad_input += dot(
                joined_refs[i][:, :, (1 + j) * half : (2 + j) * half].reshape(rows, half), qkvg_refs[i][j][...], 1, 1
            )
    attended = attended.reshape(samples, tokens, width)
    grad_input = grad_input.reshape(samples, tokens, width)
    block_ref[...] = (partial_ref[...] + zero_gate[None] * attended).astype(BF16)
    grad_zero = jnp.sum(grad_out * attended, axis=0) * slope(zero_gate)
    zero_b_out[...] += column_sum(grad_zero)
    zero_low_ref[...] = grad_zero.astype(BF16)
    grad_factor = jnp.sum(grad_input * normed, axis=0) * slope(factor)
    cond_b_out[...] += column_sum(grad_factor)
    projected_ref[:, :width] = grad_factor.astype(BF16)
    projected_ref[:, width:] = jnp.sum(grad_input, axis=0).astype(BF16)
    acts_grad_ref[...] = (
        grad_out + norm_back(grad_input * factor[None] + acts_part_ref[...], normed, inverse)
    ).astype(BF16)


def outputs_call(acts, cot, partial, acts_part, zero_gate, factor, joineds, out_w, qkvg_w, deps, order):
    samples, length, width = acts.shape
    half = width // 2
    block = spec((samples, TOKENS, width), 1)
    tokens = spec((TOKENS, width), 0)
    return call(
        "outputs",
        outputs_kernel,
        length // TOKENS,
        [(a, block) for a in (acts, cot, partial, acts_part)]
        + [(zero_gate, tokens), (factor, tokens)]
        + [(a, spec((samples, TOKENS, 5 * half), 1)) for a in joineds]
        + [(out_w, spec((half, width), at=(whose, 0))) for whose in (own, other)]
        + quarters(qkvg_w, own)
        + quarters(qkvg_w, other),
        [
            (acts.shape, BF16, block),
            (acts.shape, BF16, block),
            ((length, 2 * width), BF16, spec((TOKENS, 2 * width), 0)),
            ((length, width), BF16, tokens),
        ]
        + [(s, F32, spec(s)) for s in ((1, width), (1, width), (width, width))],
        [],
        deps,
        order,
    )


def conditions_kernel(
    rest, vector_parts, place, cond_ref, gain_ref, cond_w_ref, zero_w_ref, zero_low_ref, projected_ref,
    cond_gate_in, cond_norm_in, out_w_grad_ref, *refs
):
    vector_refs, (packed_out,) = refs[:vector_parts], refs[vector_parts:]
    cond_w_grad, zero_w_grad, gain_grad, cond_gate, cond_norm, cond_normed, cond_inverse = conditions_back(
        cond_ref, gain_ref, cond_w_ref, zero_w_ref, zero_low_ref[...], projected_ref[...]
    )
    cond_grad = (
        cond_gate + cond_gate_in[...] + norm_back(cond_norm + cond_norm_in[...], cond_normed, cond_inverse)
    )
    vectors = [gain_grad] + [ref[...] for ref in vector_refs[:-1]]
    q_bias = vector_refs[-1][...]
    vectors += [jnp.where(place[0] == 0, q_bias, 0.0), jnp.where(place[0] == 1, q_bias, 0.0)]
    pieces = [v[:, at : at + PIECE] for v in vectors for at in range(0, v.shape[1], PIECE)]
    rest.pack(packed_out, [out_w_grad_ref[...], cond_w_grad, zero_w_grad, cond_grad], pieces)


def conditions_call(cond, branch, zero_w, zero_low, projected, cond_gate, cond_norm, out_w_grad, vectors, rest, deps, order):
    cond_width = cond.shape[1]
    width = zero_low.shape[1]
    weights = [out_w_grad.shape, (cond_width, 2 * width), (cond_width, width), cond.shape]
    count, rows, columns = rest.slabs(weights)
    rows += (sum(v.shape[1] for v in vectors) + cond_width + width // 2) // PIECE
    rows += -rows % 16
    fixed = (zero_low, projected, cond_gate, cond_norm, out_w_grad, *vectors)
    (packed,) = call(
        "conditions",
        functools.partial(conditions_kernel, rest, len(vectors)),
        1,
        [(cond, spec(cond.shape))] + branch[:2] + [zero_w] + [(a, spec(a.shape)) for a in fixed],
        [((count, rows, columns), BF16, spec((count, rows, columns)))],
        [],
        deps,
        order,
    )
    return packed, weights


def results_kernel(
    early_halving, rest_halving, early_shapes, rest_shapes, halves, place, *refs
):
    early_refs, refs = refs[:halves], refs[halves:]
    qkvg_refs, refs = refs[: 2 * halves], refs[2 * halves :]
    (rest_ref, rest_got_ref, pair_sum_ref, pair_wt_ref, pair_gain_ref), refs = refs[:5], refs[5:]
    (cond_ref, cond_w_ref, zero_w_ref, qkvg_ref, out_w_ref, swiglu_ref, down_ref), refs = refs[:7], refs[7:]
    gains_ref, cond_b_ref, zero_b_ref, q_bias_ref, pair_gain_out, pair_w_out = refs
    bits = place.shape[0] - 1
    device = sum(place[bit] << bit for bit in range(bits))

    def columns(ref, pieces):
        for c, piece in enumerate(pieces):
            ref[:, c * PIECE : (c + 1) * PIECE] = piece.astype(F32)

    early = [early_halving.unpack(ref[...].astype(F32), early_shapes) for ref in early_refs]
    swiglu, down, cond_w_one, zero_w_one = [sum(parts, []) for parts in zip(*early)]
    before = rest_ref[...].astype(F32)
    total = before + rest_got_ref[...].astype(F32)
    out_w, cond_w_zero, zero_w_zero, _ = rest_halving.unpack(total, rest_shapes)
    columns(swiglu_ref, swiglu)
    columns(down_ref, down)
    columns(cond_w_ref, cond_w_zero + cond_w_one)
    columns(zero_w_ref, zero_w_zero + zero_w_one)
    columns(out_w_ref, out_w)
    columns(cond_ref, rest_halving.unpack(before, rest_shapes)[3])
    parts = []
    for i in range(2):
        held = [ref[...].astype(F32) for ref in qkvg_refs[i * halves : (i + 1) * halves]]
        if halves == 2:
            first = place[bits] == 0
            held = [jnp.where(first, held[0], held[1]), jnp.where(first, held[1], held[0])]
        parts.append(jnp.concatenate(held, axis=0))
    first = place[0] == 0
    parts = [jnp.where(first, parts[0], parts[1]), jnp.where(first, parts[1], parts[0])]
    rows = parts[0].shape[0] // 4
    columns(qkvg_ref, [part[j * rows : (j + 1) * rows] for j in range(4) for part in parts])
    at = sum(r * c for r, c in map(rest_halving.pieces, rest_shapes))
    for ref in (gains_ref, cond_b_ref, zero_b_ref, q_bias_ref):
        size = ref.shape[1]
        count = size * rest_halving.counts["sample"] // PIECE
        value = 0.0
        for c in range(count):
            source = lax.broadcasted_iota(jnp.int32, (PIECE, size), 0) + c * PIECE
            target = lax.broadcasted_iota(jnp.int32, (PIECE, size), 1) + device * size
            chosen = (source == target).astype(F32)
            value += lax.dot_general(
                total[at + c : at + c + 1],
                chosen,
                (((1,), (0,)), ((), ())),
                precision=lax.Precision.HIGHEST,
                preferred_element_type=F32,
            )
        ref[...] = value
        at += count
    size, heads = pair_w_out.shape
    channels = pair_sum_ref.shape[1]
    source = lax.broadcasted_iota(jnp.int32, (channels, size), 0)
    target = lax.broadcasted_iota(jnp.int32, (channels, size), 1) + device * size
    chosen = (source == target).astype(F32)

    def choose(array):
        return lax.dot_general(
            chosen,
            array,
            (((0,), (1,)), ((), ())),
            precision=lax.Precision.HIGHEST,
            preferred_element_type=F32,
        )

    grad = choose(pair_sum_ref[...])
    pair_w_out[...] = grad
    weighted = grad * choose(pair_wt_ref[...].astype(F32))

    def across(left, right, right_dim):
        return lax.dot_general(
            left,
            right,
            (((1,), (right_dim,)), ((), ())),
            precision=lax.Precision.HIGHEST,
            preferred_element_type=F32,
        )

    pair_gain_out[...] = across(jnp.ones((1, heads), F32), weighted, 1) / across(pair_gain_ref[...], chosen, 0)


def results_call(
    early, early_halving, early_shapes, qkvg, rest, rest_got, rest_halving, rest_shapes, pair_sum, pair_wt, pair_gain, order
):
    count = rest_halving.counts["sample"]
    heads, channels = pair_wt.shape
    swiglu, down, cond_w, zero_w = early_shapes
    out_w, _, _, cond = rest_shapes
    width = out_w[1]
    arrays = [cond, (cond_w[0], 2 * cond_w[1]), (zero_w[0], 2 * zero_w[1]), (width, 4 * width), out_w, swiglu, down]
    shapes = [(rows // count, columns) for rows, columns in arrays]
    shapes += [(1, size // count) for size in (2 * cond[1], 2 * width, 2 * width, width)]
    shapes += [(1, channels // count), (channels // count, heads)]
    ins = [*early, *qkvg, rest, rest_got, pair_sum, pair_wt, pair_gain]
    return call(
        "results",
        functools.partial(
            results_kernel, early_halving, rest_halving, early_shapes, rest_shapes, early_halving.halves()
        ),
        1,
        [(a, spec(a.shape)) for a in ins],
        [(shape, F32, spec(shape)) for shape in shapes],
        [],
        [],
        order,
    )


def body(
    struct_count, sample_devices,
    acts, cond, pair, lengths, token_mask, cond_gains, cond_w, cond_bias, output_gate_weights, zero_bias,
    qkvg_w, q_bias, out_w, swiglu_w, down_w, pair_gain, pair_w, cotangent,
):
    acts, cond, pair, cotangent = acts[0], cond[0], pair[0], cotangent[0]
    samples, length, width = acts.shape
    cond_width = cond.shape[1]
    heads = pair_w.shape[1]
    head_dim = width // heads
    chunks = heads // 2 // CHUNK_HEADS
    counts = {"struct": struct_count, "sample": sample_devices}
    bits = sample_devices.bit_length() - 1
    pair_wt = pair_w.T
    device = lax.axis_index("sample")
    core = device & 1
    place = [(device >> bit) & 1 for bit in range(bits)] + [lax.axis_index("struct")]
    order = Order(jnp.stack(place).astype(jnp.int32))

    def swap(array):
        return lax.ppermute(array, "sample", [(i, i ^ 1) for i in range(sample_devices)])

    acts_other, cotangent_other = swap(acts), swap(cotangent)

    bias_rows = pair_forward(pair, pair_gain[None], pair_wt, token_mask, lengths, Order(jnp.zeros(bits + 1, jnp.int32)))
    bias = lax.all_gather(bias_rows, "sample", axis=0, tiled=False)

    rows = {}
    at = 0
    packed = [
        ("gain", cond_gains), ("cond_b", cond_bias), ("zero_b", zero_bias), ("q_bias", q_bias), ("pair", pair_gain)
    ]
    vector = jnp.concatenate([v for _, v in packed]).astype(F32)[None]
    for name, v in packed:
        rows[name] = vector[:, at : at + v.shape[0]]
        at += v.shape[0]

    def conditioning(b):
        return [
            (rows["gain"], spec((1, cond_width), at=(0, b))),
            (cond_w, spec((cond_width, 2 * width), at=(0, b))),
            (rows["cond_b"], spec((1, width), at=(0, b))),
        ]

    def zero(b):
        return [
            (output_gate_weights, spec((cond_width, width), at=(0, b))),
            (rows["zero_b"], spec((1, width), at=(0, b))),
        ]

    def path(*order):
        steps = [("struct", 0) if o == "y" else ("sample", o) for o in order]
        steps = [s for s in steps if s[0] == "sample" or struct_count == 2]
        return Halving(steps + [("sample", b) for b in range(4, bits)], counts)

    along_x = path(0, 1, 2, 3)
    along_y = path(0, "y", 2, 3, 1)
    chip_x = path(1, 2, 3)
    chip_y = path("y", 2, 3, 1)
    results, early_shapes = transition_call(
        acts, cotangent, cond, conditioning(1) + zero(1), swiglu_w, down_w, along_y, [], order
    )
    partial, acts_part, cond_gate, cond_norm, early, cond_b_one, zero_b_one, gain_one = results
    early = Running(along_y.run(early))
    first, gate, gated_grad, *rest = inputs_call(
        acts, acts_other, cotangent, cotangent_other, cond, conditioning(0) + zero(0), qkvg_w, rows["q_bias"], out_w,
        heads, [], order,
    )
    nats, turned, (zero_gate, factor) = rest[:4], rest[4:8], rest[8:]

    mixeds, dqs, dkts, dvts, bias_sums = [], [], [], [], []
    deps = advance(order, early)
    for chunk in range(chunks):
        mixed, dq, dkt, dvt, sent, kept = attention_call(chunk, nats, turned, bias, head_dim, chip_x, deps, order)
        mixeds.append(mixed)
        dqs.append(dq)
        dkts.append(dkt)
        dvts.append(dvt)
        deps = advance(order, *bias_sums, *([early] if chunk % 2 else []))
        bias_sums.append(Running(chip_x.run(kept, "swap", sent)))

    joined, joined_sent, q_bias_grad = mixed_call(
        gate, gated_grad, mixeds, dqs, dkts, dvts, deps, order
    )
    joined_got = swap(joined_sent)
    qkvg_sum = Running(
        chip_y.run(qkvg_call(first, joined, joined_sent, chip_y, [], order), "cores")
    )
    deps = advance(order, *bias_sums, qkvg_sum)
    block_out, acts_grad, projected, zero_low, cond_b_zero, zero_b_zero, out_grad = outputs_call(
        acts, cotangent, partial, acts_part, zero_gate, factor, [joined, joined_got],
        out_w, qkvg_w, deps, order,
    )
    deps = advance(order, *bias_sums, qkvg_sum, early)
    rest, rest_shapes = conditions_call(
        cond, conditioning(0), zero(0)[0], zero_low, projected, cond_gate, cond_norm, out_grad,
        [gain_one, cond_b_zero, cond_b_one, zero_b_zero, zero_b_one, q_bias_grad], along_x, deps, order,
    )
    rest = Running(along_x.run(rest, ""))
    while any(b.result is None for b in bias_sums):
        advance(order, *bias_sums)
    share = length // sample_devices
    block = 16 if share % 16 == 0 else share
    turned_wt = jnp.where(core == 0, pair_wt, jnp.roll(pair_wt, heads // 2, axis=0))
    grads = [b.result[0] for b in bias_sums] + [b.result[1] for b in bias_sums]
    grad_pair, part = pair_backward(0, block, None, pair, grads, rows["pair"], turned_wt, [], order)
    pair_parts = [part]
    if share > block:
        deps = advance(order, qkvg_sum, rest, early)
        grad_pair, part = pair_backward(
            block, share - block, grad_pair, pair, grads, rows["pair"], turned_wt, deps, order
        )
        pair_parts.append(part)
    struct_bits = struct_count.bit_length() - 1

    def summed(array, *masks):
        found = [
            lax.ppermute(array, ("struct", "sample"), [(i, i ^ mask) for i in range(struct_count * sample_devices)])
            for mask in masks
        ]
        if len(found) == 1:
            return array + found[0]
        return (array + found[0]) + (found[1] + found[2])

    class Pair:
        asked = [[(p, p.shape[0], lambda place: 0, True) for p in pair_parts]]
        result = None

        def send(self, found):
            self.result = found[0]

    pair_grad = Pair()
    advance(order, pair_grad, qkvg_sum, rest, early)
    left = [bits + struct_bits - 1] + list(range(bits + struct_bits - 1)) if struct_bits else list(range(bits))
    pair_sum = pair_grad.result
    while left:
        one = 1 << left.pop(0)
        two = 1 << left.pop(0) if left else 0
        pair_sum = summed(pair_sum, one, two, one | two) if two else summed(pair_sum, one)
    chains = (qkvg_sum, rest, early)
    advance(order, *chains)
    while any(r.result is None for r in chains):
        advance(order, *chains, near=True)
    mine_qkvg, sent = qkvg_sum.result
    if chip_y.halves() == 2:
        across = [
            (s * sample_devices + i, (1 - s) * sample_devices + (i ^ 1))
            for s in range(2)
            for i in range(sample_devices)
        ]
        from_y = lax.ppermute(mine_qkvg, "struct", [(0, 1), (1, 0)])
        from_both = lax.ppermute(sent, ("struct", "sample"), across)
        qkvg = [mine_qkvg, from_y, swap(sent), from_both]
    else:
        for bit in range(struct_bits):
            mine_qkvg, sent = [summed(part, 1 << (bits + bit)) for part in (mine_qkvg, sent)]
        qkvg = [mine_qkvg, swap(sent)]
    early = list(early.result) if along_y.halves() == 2 else [early.result]
    rest_sum, rest_got = rest.result, jnp.zeros_like(rest.result)
    for bit in range(struct_bits):
        if bit:
            rest_sum = rest_sum + rest_got
        rest_got = lax.ppermute(
            rest_sum, "struct", [(i, i ^ (1 << bit)) for i in range(struct_count)]
        )
    (cond_sum, cond_w_sum, zero_w_sum, qkvg_total, out_sum, swiglu_sum, down_sum,
     gains, cond_b, zero_b, q_b, pair_g, pair_w_sum) = results_call(
        early, along_y, early_shapes, qkvg, rest_sum, rest_got, along_x, rest_shapes, pair_sum, pair_wt, rows["pair"], order
    )
    if struct_bits > 1:
        cond_sum = along_x.unpack(rest.result, rest_shapes)[3][0].astype(F32)
    return (
        block_out[None], acts_grad[None], cond_sum[None], grad_pair[None], gains[0], cond_w_sum, cond_b[0], zero_w_sum,
        zero_b[0], qkvg_total, q_b[0], out_sum, swiglu_sum, down_sum, pair_g[0], pair_w_sum,
    )


def solution(mesh):
    per_struct = P("struct", "sample", None, None)
    in_specs = (
        (per_struct, P("struct", None, None), per_struct, P("struct"), P("struct", None))
        + (P(),) * 12
        + (per_struct,)
    )
    one, two = P("sample"), P("sample", None)
    out_specs = (
        per_struct, per_struct, P("struct", "sample", None), per_struct,
        one, two, one, two, one, two, one, two, two, two, one, two,
    )
    local = functools.partial(body, mesh.shape["struct"], mesh.shape["sample"])
    return jax.shard_map(local, mesh=mesh, in_specs=in_specs, out_specs=out_specs, check_vma=False)
```
